128 devices in a mesh: rep: 2 (over z_lo), shard: 16 (over y, z_hi, core), ctx: 4 (over x).
Axes of the slice: x: 4, y: 4, z: 4 (z_hi: 2, z_lo: 2; z = z_hi * 2 + z_lo), core: 2. Of those that a mesh axis runs over, the one named last changes fastest.
Arguments:
- image_tokens: bfloat16 [32, 384, 1536], P(('rep', 'shard'), 'ctx'), may hold values from -6 to 6
- text_tokens: bfloat16 [32, 160, 1536], P(('rep', 'shard'), 'ctx'), may hold values from -6 to 6
- text_lengths: int32 [32, 4], P(('rep', 'shard'), 'ctx'), may hold values from 1 to 40, 154 in all within a row
- slot_sequence: int32 [32], P(('rep', 'shard')), may hold values from -1 to 26, as said below
- conditioning: bfloat16 [27, 1536], replicated, may hold values from -6 to 6
- mod_weight: bfloat16 [1536, 2, 9216], P(('shard', 'ctx')), may hold values from -0.15625 to 0.15625
- mod_bias: bfloat16 [2, 9216], replicated, may hold values from -3 to 3
- qkv_weight: bfloat16 [1536, 2, 4608], P(('shard', 'ctx')), may hold values from -0.15625 to 0.15625
- qv_bias: bfloat16 [2, 3072], replicated, may hold values from -2 to 2
- out_weight: bfloat16 [1536, 2, 1536], P(('shard', 'ctx')), may hold values from -0.625 to 0.625
- out_bias: bfloat16 [2, 1536], replicated, may hold values from -2 to 2
- up_weight: bfloat16 [1536, 2, 6144], P(('shard', 'ctx')), may hold values from -0.15625 to 0.15625
- up_bias: bfloat16 [2, 6144], replicated, may hold values from -2 to 2
- down_weight: bfloat16 [6144, 2, 1536], P(('shard', 'ctx')), may hold values from -0.078125 to 0.078125
- down_bias: bfloat16 [2, 1536], replicated, may hold values from -2 to 2
- image_cotan: bfloat16 [32, 384, 1536], P(('rep', 'shard'), 'ctx'), may hold values from -6 to 6
- text_cotan: bfloat16 [32, 160, 1536], P(('rep', 'shard'), 'ctx'), may hold values from -6 to 6
Outputs:
- image_out: bfloat16 [32, 384, 1536], P(('rep', 'shard'), 'ctx')
- text_out: bfloat16 [32, 160, 1536], P(('rep', 'shard'), 'ctx')
- image_grad: float32 [32, 384, 1536], P(('rep', 'shard'), 'ctx')
- text_grad: float32 [32, 160, 1536], P(('rep', 'shard'), 'ctx')
- cond_grad: float32 [27, 1536], P(None, ('shard', 'ctx'))
- mod_weight_grad: float32 [1536, 2, 9216], P(('shard', 'ctx'))
- mod_bias_grad: float32 [2, 9216], P(None, ('shard', 'ctx'))
- qkv_weight_grad: float32 [1536, 2, 4608], P(('shard', 'ctx'))
- qv_bias_grad: float32 [2, 3072], P(None, ('shard', 'ctx'))
- out_weight_grad: float32 [1536, 2, 1536], P(('shard', 'ctx'))
- out_bias_grad: float32 [2, 1536], P(None, ('shard', 'ctx'))
- up_weight_grad: float32 [1536, 2, 6144], P(('shard', 'ctx'))
- up_bias_grad: float32 [2, 6144], P(None, ('shard', 'ctx'))
- down_weight_grad: float32 [6144, 2, 1536], P(('shard', 'ctx'))
- down_bias_grad: float32 [2, 1536], P(None, ('shard', 'ctx'))
The draws below stay inside these ranges and needn't reach their ends.
Inputs may be any that keep to these rules, and one draw needn't show every extreme that they name: `slot_sequence`: each of the 27 sequences stands in exactly one slot; the other slots hold -1. `text_lengths`: each slot's row sums to 154.
All inputs are finite; a program needn't handle non-finite values. No bound on the sum of `text_lengths` on one device may be relied on, other than what follows from the above.
Results may differ from the reference program's by a relative error of at most 0.02.
Values may be sent and summed in bfloat16 or wider, within the bound.
No kernel may reach another device: no remote copies, remote signals or barrier semaphores. Data moves between devices by JAX's collectives and lax.ppermute only.
A program may use at most 192 MiB of HBM per device.

```python
import math
import jax
import jax.numpy as jnp
import numpy as np
from jax import lax

HEADS = 24
HEAD_DIM = 64
D = 1536
FF = 6144
TXT = 154
TXT_CAP = 40
IMG = 384
TXT_ROWS = 160
SLOTS = 32
SEQS = 27
N_CTX = 4


def draw_slot_sequence(key, part):
    key = jax.random.fold_in(key, 7)
    order = jax.random.permutation(key, SLOTS)
    return jnp.where(order < SEQS, order, -1).astype(jnp.int32)


def levels(key, extent, pieces, least, high):
    def one(position, parts):
        draws = jax.random.uniform(jax.random.fold_in(jax.random.fold_in(key, 6), position), (parts,), jnp.float32, least / len(pieces), high / len(pieces))
        return jnp.repeat(jnp.exp(draws), extent[position] // parts).reshape((-1,) + (1,) * (len(extent) - position - 1))

    loudness = one(*pieces[0])
    for cut in pieces[1:]:
        loudness = loudness * one(*cut)
    return loudness


def profile(amount, total, bound, lean):
    portions = [(1 << 20) // math.isqrt(standing ** lean) + 1 for standing in range(2, amount + 1)]
    surplus, given = total - bound - (amount - 1), [1] * (amount - 1)
    while surplus > 0:
        movable = [i for i in range(amount - 1) if given[i] < bound]
        whole, budget = sum([portions[i] for i in movable]), surplus
        for i in movable:
            more = min(bound - given[i], max(1, budget * portions[i] // whole), surplus)
            given[i] = given[i] + more
            surplus = surplus - more
    return np.array([bound] + given)


def uneven(rng, count, total, limit, slope):
    if count == 2:
        one = jax.random.randint(rng, (), max(1, total - limit), min(limit, total - 1) + 1)
        return jnp.stack([one, total - one])
    tallies = jnp.asarray(profile(count, total, limit, slope), jnp.int32)
    pairs = (count - 1) // 2
    donor, taker = tallies[1:1 + 2 * pairs:2], tallies[2:2 + 2 * pairs:2]
    room = jnp.minimum(donor - 1, limit - taker)
    passed = jax.random.randint(jax.random.fold_in(rng, 1), (pairs,), 0, 1 << 20) % (room + 1)
    tallies = tallies.at[1:1 + 2 * pairs:2].set(donor - passed).at[2:2 + 2 * pairs:2].set(taker + passed)
    return tallies[jax.random.permutation(jax.random.fold_in(rng, 2), count)]


def gaussian(rng, shape, spread, reach, cuts=(), held_as=jnp.bfloat16):
    drawn = spread * jax.random.normal(rng, shape, jnp.float32)
    if cuts:
        drawn = drawn * levels(rng, shape, cuts, -0.22, 0.18)
    return jnp.clip(drawn, -reach, reach).astype(held_as)


def setup_inputs(seed: int = 0) -> dict:
    key_list = jax.random.split(jax.random.key(seed), 18)
    return {
        "image_tokens": gaussian(key_list[0], (SLOTS, IMG, D), 1.0, 6.0, ((0, 32), (1, 4))),
        "text_tokens": gaussian(key_list[1], (SLOTS, TXT_ROWS, D), 1.0, 6.0, ((0, 32), (1, 4))),
        "text_lengths": jax.vmap(lambda own: uneven(own, N_CTX, TXT, TXT_CAP, 1))(jax.random.split(key_list[2], SLOTS)).reshape((SLOTS, N_CTX)).astype(jnp.int32),
        "slot_sequence": draw_slot_sequence(jax.random.fold_in(key_list[17], 71), 0),
        "conditioning": gaussian(key_list[4], (SEQS, D), 1.0, 6.0),
        "mod_weight": gaussian(key_list[5], (D, 2, 6 * D), D ** -0.5, 0.15625, ((0, 64),)),
        "mod_bias": gaussian(key_list[6], (2, 6 * D), 0.5, 3.0),
        "qkv_weight": gaussian(key_list[7], (D, 2, 3 * D), D ** -0.5, 0.15625, ((0, 64),)),
        "qv_bias": gaussian(key_list[8], (2, 2 * D), 0.3, 2.0),
        "out_weight": gaussian(key_list[9], (D, 2, D), (D // 16) ** -0.5, 0.625, ((0, 64),)),
        "out_bias": gaussian(key_list[10], (2, D), 0.3, 2.0),
        "up_weight": gaussian(key_list[11], (D, 2, FF), D ** -0.5, 0.15625, ((0, 64),)),
        "up_bias": gaussian(key_list[12], (2, FF), 0.3, 2.0),
        "down_weight": gaussian(key_list[13], (FF, 2, D), FF ** -0.5, 0.078125, ((0, 64),)),
        "down_bias": gaussian(key_list[14], (2, D), 0.3, 2.0),
        "image_cotan": gaussian(key_list[15], (SLOTS, IMG, D), 1.0, 6.0, ((0, 32), (1, 4))),
        "text_cotan": gaussian(key_list[16], (SLOTS, TXT_ROWS, D), 1.0, 6.0, ((0, 32), (1, 4))),
    }


@jax.custom_vjp
def low(v):
    return lax.optimization_barrier(v.astype(jnp.bfloat16)).astype(jnp.float32)

@jax.custom_vjp
def low_back(v):
    return v

def low_keep(v):
    return (low(v), None)

def low_pass(kept, grad):
    return (grad,)

def back_keep(v):
    return (v, None)

def back_low(kept, grad):
    return (low(grad),)
low.defvjp(low_keep, low_pass)
low_back.defvjp(back_keep, back_low)

def product(left, right):
    return jnp.matmul(left, right, precision=lax.Precision.HIGHEST)

def layer_norm(values):
    center = values - lax.optimization_barrier(jnp.mean(values, axis=-1, keepdims=True))
    return center * lax.rsqrt(lax.optimization_barrier(jnp.mean(center * center, axis=-1, keepdims=True)) + 1e-06)

def attend(inputs):
    query, key_rows, value_rows, key_bias = inputs
    count = query.shape[0]
    query_heads = query.reshape(count, HEADS, HEAD_DIM)
    key_heads = key_rows.reshape(count, HEADS, HEAD_DIM)
    value_heads = value_rows.reshape(count, HEADS, HEAD_DIM)
    scores = jnp.einsum('qhd,khd->hqk', query_heads, key_heads, precision=lax.Precision.HIGHEST) * 0.125
    scores = low_back(scores) + key_bias[None, None, :]
    top_score = lax.optimization_barrier(jnp.max(scores, axis=-1, keepdims=True))
    exp_scores = jnp.exp(scores - top_score)
    weights = low(exp_scores / lax.optimization_barrier(jnp.sum(exp_scores, axis=-1, keepdims=True)))
    mixed = jnp.einsum('hqk,khd->qhd', weights, value_heads, precision=lax.Precision.HIGHEST)
    return mixed.reshape(count, HEADS * HEAD_DIM)

def forward(params, image, text, seq_hot, image_mask, text_mask, key_bias):
    cond, mod_w, mod_b, qkv_w, qv_b, out_w, out_b, up_w, up_b, down_w, down_b = params
    cond_low = low(jax.nn.silu(cond))
    group = image.shape[0]
    modulation = []
    queries, keys, values = ([], [], [])
    for stream, tokens in enumerate((image, text)):
        table = product(cond_low, mod_w[:, stream]) + mod_b[stream]
        shifts = product(seq_hot, table).reshape(group, 6, 1, D)
        modulated = low(layer_norm(tokens) * (1.0 + shifts[:, 1]) + shifts[:, 0])
        projected = product(modulated, qkv_w[:, stream])
        queries.append(low_back(low(projected[..., :D] + qv_b[stream, :D])))
        keys.append(low_back(low(projected[..., D:2 * D])))
        values.append(low_back(low(projected[..., 2 * D:] + qv_b[stream, D:])))
        modulation.append(shifts)
    mixed = lax.map(jax.checkpoint(attend), (jnp.concatenate(queries, 1), jnp.concatenate(keys, 1), jnp.concatenate(values, 1), key_bias))
    mixed = low_back(low(mixed))
    mixed_parts = (mixed[:, :IMG], mixed[:, IMG:])
    outputs = []
    for stream, (tokens, mask) in enumerate(((image, image_mask), (text, text_mask))):
        shifts = modulation[stream]
        attn_out = low_back(product(mixed_parts[stream], out_w[:, stream]) + out_b[stream])
        middle = tokens + shifts[:, 2] * attn_out
        modulated = low(layer_norm(middle) * (1.0 + shifts[:, 4]) + shifts[:, 3])
        hidden = low_back(product(modulated, up_w[:, stream]) + up_b[stream])
        activated = low(jax.nn.gelu(hidden, approximate=True))
        branch = low_back(product(activated, down_w[:, stream]) + down_b[stream])
        outputs.append((middle + shifts[:, 5] * branch) * mask[..., None])
    return tuple(outputs)

def reference(image_tokens, text_tokens, text_lengths, slot_sequence, conditioning, mod_weight, mod_bias, qkv_weight, qv_bias, out_weight, out_bias, up_weight, up_bias, down_weight, down_bias, image_cotan, text_cotan):
    params = tuple((a.astype(jnp.float32) for a in (conditioning, mod_weight, mod_bias, qkv_weight, qv_bias, out_weight, out_bias, up_weight, up_bias, down_weight, down_bias)))
    seq_hot = (slot_sequence[:, None] == jnp.arange(SEQS, dtype=jnp.int32)[None, :]).astype(jnp.float32)
    live = (slot_sequence >= 0).astype(jnp.float32)
    local_row = jnp.arange(TXT_ROWS, dtype=jnp.int32) % TXT_CAP
    slice_of = jnp.arange(TXT_ROWS, dtype=jnp.int32) // TXT_CAP
    counts = jnp.take(text_lengths, slice_of, axis=1)
    text_valid = (local_row[None, :] < counts).astype(jnp.float32)
    key_bias = jnp.concatenate([jnp.zeros((SLOTS, IMG), jnp.float32), (text_valid - 1.0) * 1000000000.0], 1)
    image_mask = jnp.broadcast_to(live[:, None], (SLOTS, IMG)).astype(jnp.float32)
    text_mask = text_valid * live[:, None]
    group = 4 if SLOTS % 4 == 0 else 1

    def split(values):
        return values.reshape((SLOTS // group, group) + values.shape[1:])

    def step(totals, inputs):
        image, text, hot, image_m, text_m, bias_rows, image_d, text_d = inputs

        def local_forward(weights, image_f, text_f):
            return forward(weights, image_f, text_f, hot, image_m, text_m, bias_rows)
        outs, pull = jax.vjp(local_forward, params, image.astype(jnp.float32), text.astype(jnp.float32))
        grads, image_g, text_g = pull((image_d.astype(jnp.float32), text_d.astype(jnp.float32)))
        totals = jax.tree.map(jnp.add, totals, grads)
        return (totals, (outs[0], outs[1], image_g, text_g))
    zeros = jax.tree.map(jnp.zeros_like, params)
    inputs = tuple((split(a) for a in (image_tokens, text_tokens, seq_hot, image_mask, text_mask, key_bias, image_cotan, text_cotan)))
    totals, stacked = lax.scan(step, zeros, inputs)
    image_out = stacked[0].reshape(SLOTS, IMG, D).astype(jnp.bfloat16)
    text_out = stacked[1].reshape(SLOTS, TXT_ROWS, D).astype(jnp.bfloat16)
    image_grad = stacked[2].reshape(SLOTS, IMG, D)
    text_grad = stacked[3].reshape(SLOTS, TXT_ROWS, D)
    return (image_out, text_out, image_grad, text_grad, totals[0], totals[1], totals[2], totals[3], totals[4], totals[5], totals[6], totals[7], totals[8], totals[9], totals[10])
```

```python
import jax
import jax.numpy as jnp
from jax import lax
from jax.sharding import Mesh, PartitionSpec as P

HEAD_DIM = 64
SHARD = ("y", "zh", "core")
OWNER = ("y", "zh", "core", "ctx")
SLOT = ("rep", "y", "zh", "core")
EVERY = ("rep", "y", "zh", "core", "ctx")
BF = jnp.bfloat16
F32 = jnp.float32


def norm_rows(values):
    center = values - jnp.mean(values, axis=-1, keepdims=True)
    inv_scale = lax.rsqrt(jnp.mean(center * center, axis=-1, keepdims=True) + 1e-06)
    return (center * inv_scale, inv_scale)


def norm_back(grad_out, normed, inv_scale):
    return inv_scale * (
        grad_out
        - jnp.mean(grad_out, axis=-1, keepdims=True)
        - normed * jnp.mean(grad_out * normed, axis=-1, keepdims=True)
    )


def gelu_tanh(values):
    return jax.nn.gelu(values, approximate=True)


def mm(left, right):
    return jnp.dot(left, right, preferred_element_type=F32)


def mm_nt(left, right):
    return lax.dot_general(left, right, (((1,), (1,)), ((), ())), preferred_element_type=F32)


def mm_tn(left, right):
    return lax.dot_general(left, right, (((0,), (0,)), ((), ())), preferred_element_type=F32)


def split_heads(matrix):
    return matrix.reshape(matrix.shape[0], -1, HEAD_DIM)


def joint_scores(query, all_keys, all_bias):
    scores = jnp.einsum(
        "qhd,khd->hqk", split_heads(query), split_heads(all_keys), preferred_element_type=F32
    )
    return scores * 0.125 + all_bias[None, None, :]


def attention_forward(query, all_keys, all_values, all_bias):
    scores = joint_scores(query, all_keys, all_bias)
    top_score = jnp.max(scores, axis=-1, keepdims=True)
    exp_scores = jnp.exp(scores - top_score)
    row_total = jnp.sum(exp_scores, axis=-1, keepdims=True)
    log_total = top_score + jnp.log(row_total)
    weights = (exp_scores / row_total).astype(BF)
    mixed = jnp.einsum("hqk,khd->qhd", weights, split_heads(all_values), preferred_element_type=F32)
    return (mixed.reshape(query.shape).astype(BF), log_total)


def attention_backward(query, all_keys, all_values, all_bias, log_total, grad_mixed):
    grad_heads = split_heads(grad_mixed)
    probs = jnp.exp(joint_scores(query, all_keys, all_bias) - log_total)
    grad_probs = jnp.einsum(
        "qhd,khd->hqk", grad_heads, split_heads(all_values), preferred_element_type=F32
    )
    delta = jnp.sum(probs * grad_probs, axis=-1, keepdims=True)
    grad_scores = (probs * (grad_probs - delta)).astype(BF)
    grad_query = (
        jnp.einsum("hqk,khd->qhd", grad_scores, split_heads(all_keys), preferred_element_type=F32)
        * 0.125
    )
    grad_keys = (
        jnp.einsum("hqk,qhd->khd", grad_scores, split_heads(query), preferred_element_type=F32)
        * 0.125
    )
    grad_values = jnp.einsum(
        "hqk,qhd->khd", probs.astype(BF), grad_heads, preferred_element_type=F32
    )
    return tuple(g.reshape(query.shape).astype(BF) for g in (grad_query, grad_keys, grad_values))


def turn(values, axis, step):
    count = lax.axis_size(axis)
    return lax.ppermute(values, axis, [(i, (i + step) % count) for i in range(count)])


def ring_gather(block):
    half = block.shape[0] // 2 // 8 * 8
    behind = turn(block, "ctx", 1)
    ahead = turn(block, "ctx", -1)
    far_top = turn(behind[:half], "ctx", 1)
    far_bottom = turn(ahead[half:], "ctx", -1)
    return [block, ahead, jnp.concatenate([far_top, far_bottom]), behind]


def ring_scatter(blocks):
    half = blocks[0].shape[0] // 2 // 8 * 8
    from_behind = turn(blocks[2][:half], "ctx", 1)
    from_ahead = turn(blocks[2][half:], "ctx", -1)
    to_ahead = jnp.concatenate([blocks[1][:half] + from_behind, blocks[1][half:]])
    to_behind = jnp.concatenate([blocks[3][:half], blocks[3][half:] + from_ahead])
    got_behind = turn(to_ahead, "ctx", 1)
    got_ahead = turn(to_behind, "ctx", -1)
    return blocks[0].astype(F32) + got_behind.astype(F32) + got_ahead.astype(F32)


def direct_gather(block, axis):
    return [block] + [turn(block, axis, -k) for k in range(1, lax.axis_size(axis))]


def split_streams(blocks, image_rows, rows):
    return (
        jnp.concatenate([b[:image_rows] for b in blocks]),
        jnp.concatenate([b[image_rows:rows] for b in blocks]),
    )


def join_streams(image, text):
    image_rows, text_rows = image.shape[0] // 4, text.shape[0] // 4
    return [
        jnp.concatenate(
            [
                image[k * image_rows : (k + 1) * image_rows],
                text[k * text_rows : (k + 1) * text_rows],
            ]
        )
        for k in range(4)
    ]


def per_device(
    image_tokens,
    text_tokens,
    text_lengths,
    slot_sequence,
    conditioning,
    mod_weight,
    mod_bias,
    qkv_weight,
    qv_bias,
    out_weight,
    out_bias,
    up_weight,
    up_bias,
    down_weight,
    down_bias,
    image_cotan,
    text_cotan,
):
    seq_total, width = conditioning.shape
    image_rows, text_cap = image_tokens.shape[1], text_tokens.shape[1]
    rows = image_rows + text_cap
    own_rows = mod_weight.shape[0]
    span, ff = width // 4, up_weight.shape[2]
    ff_span = ff // 4
    position = lax.axis_index("ctx")
    owner_index = lax.axis_index(OWNER)
    shards = 16

    meta = jnp.broadcast_to(text_lengths[0, 0].astype(BF), (8, width))
    token_blocks = ring_gather(jnp.concatenate([image_tokens[0], text_tokens[0], meta]))
    image_all, text_all = split_streams(token_blocks, image_rows, rows)
    lengths = [b[rows, 0].astype(F32) for b in token_blocks]
    cotan_blocks = ring_gather(jnp.concatenate([image_cotan[0], text_cotan[0]]))
    image_cot_all, text_cot_all = split_streams(cotan_blocks, image_rows, rows)

    col_send = jnp.concatenate(
        [
            qkv_weight.reshape(own_rows, 2, 3, 4, span)
            .transpose(3, 1, 0, 2, 4)
            .reshape(4, 2, own_rows, 3 * span),
            up_weight.reshape(own_rows, 2, 4, ff_span).transpose(2, 1, 0, 3),
        ],
        axis=3,
    )
    col_got = lax.all_to_all(col_send, "ctx", split_axis=0, concat_axis=0, tiled=True)
    col_got = col_got.transpose(1, 0, 2, 3).reshape(2, 4 * own_rows, -1)
    to_slice = [(b, (b % shards) * 4 + b // shards) for b in range(4 * shards)]
    from_slice = [(d, s) for s, d in to_slice]
    row_send = jnp.concatenate([out_weight, down_weight]).transpose(1, 0, 2)
    row_got = lax.ppermute(row_send, OWNER, to_slice)

    def gather_rows(values):
        return lax.all_gather(values, SHARD, axis=0, tiled=True)

    qkv_cols = [gather_rows(col_got[t, :, : 3 * span]) for t in range(2)]
    out_rows = [gather_rows(row_got[t, :own_rows]) for t in range(2)]
    up_cols = [gather_rows(col_got[t, :, 3 * span :]) for t in range(2)]
    down_rows = [gather_rows(row_got[t, own_rows:]) for t in range(2)]

    all_sequences = lax.all_gather(slot_sequence, SLOT, axis=0, tiled=True)
    slot_hot = (
        all_sequences[:, None] == jnp.arange(seq_total, dtype=jnp.int32)[None, :]
    ).astype(F32)
    live = (slot_sequence[0] >= 0).astype(F32)
    cond_float = conditioning.astype(F32)
    cond_cols = lax.dynamic_slice_in_dim(
        jax.nn.silu(cond_float).astype(BF), owner_index * own_rows, own_rows, 1
    )
    slot_cond = mm(slot_hot.astype(BF), cond_cols).astype(BF)
    my_cond = lax.dynamic_slice_in_dim(slot_cond, lax.axis_index("rep") * shards, shards, 0)
    mod_matrix = mod_weight.reshape(own_rows, -1)
    partial_mod = mm(my_cond, mod_matrix).astype(BF)
    got_mod = lax.all_to_all(partial_mod, SHARD, split_axis=0, concat_axis=0, tiled=True)
    slot_mod = jnp.sum(got_mod.astype(F32), axis=0).astype(BF).reshape(8, -1)
    all_mod = direct_gather(slot_mod, "ctx")
    modulation = (
        sum(m.astype(F32) for m in all_mod).reshape(2, 6, width)
        + mod_bias.astype(F32).reshape(2, 6, width)
    ) * live

    own_masks = (
        jnp.full((image_rows, 1), 1.0, F32) * live,
        (jnp.arange(text_cap, dtype=jnp.int32) < text_lengths[0, 0]).astype(F32)[:, None] * live,
    )
    row_mask = jnp.concatenate(own_masks)
    text_valid = jnp.concatenate(
        [(jnp.arange(text_cap, dtype=jnp.int32).astype(F32) < n).astype(F32) for n in lengths]
    )
    key_bias = jnp.concatenate(
        [jnp.zeros((4 * image_rows,), F32), (text_valid - 1.0) * 1000000000.0]
    )
    bias_at = lambda values, start, size: lax.dynamic_slice_in_dim(values, start, size, 1)
    q_bias = bias_at(qv_bias, position * span, span).astype(F32)
    v_bias = bias_at(qv_bias, width + position * span, span).astype(F32)
    up_part = bias_at(up_bias, position * ff_span, ff_span).astype(F32)
    normed_first, modulated_first, queries, keys, values = ([], [], [], [], [])
    for t, tokens in enumerate((image_all, text_all)):
        normed, _ = norm_rows(tokens.astype(F32))
        modulated = (normed * (1.0 + modulation[t, 1]) + modulation[t, 0]).astype(BF)
        projected = mm(modulated, qkv_cols[t])
        queries.append((projected[:, :span] + q_bias[t]).astype(BF))
        keys.append(projected[:, span : 2 * span].astype(BF))
        values.append((projected[:, 2 * span :] + v_bias[t]).astype(BF))
        normed_first.append(normed)
        modulated_first.append(modulated)
    query, all_keys, all_values = (jnp.concatenate(v) for v in (queries, keys, values))
    mixed, log_total = attention_forward(query, all_keys, all_values, key_bias)
    count = 4 * image_rows
    mixed_parts = (mixed[:count], mixed[count:])
    attn = ring_scatter(
        join_streams(*(mm(mixed_parts[t], out_rows[t]).astype(BF) for t in range(2)))
    )

    def both(at, plus=0.0):
        return jnp.concatenate(
            [
                jnp.broadcast_to(plus + modulation[0, at], (image_rows, width)),
                jnp.broadcast_to(plus + modulation[1, at], (text_cap, width)),
            ]
        )

    def spread(vectors):
        return jnp.concatenate(
            [
                jnp.broadcast_to(vectors[0], (image_rows, width)),
                jnp.broadcast_to(vectors[1], (text_cap, width)),
            ]
        )

    def sums(matrix):
        return jnp.stack([jnp.sum(matrix[:image_rows], 0), jnp.sum(matrix[image_rows:], 0)])

    tokens = jnp.concatenate([image_tokens[0], text_tokens[0]]).astype(F32)
    own_cotan = jnp.concatenate([image_cotan[0], text_cotan[0]]).astype(F32) * row_mask
    attn = attn + spread(out_bias.astype(F32))
    middle = tokens + both(2) * attn
    normed_two, inv_two = norm_rows(middle)
    modulated_two = (normed_two * both(4, 1.0) + both(3)).astype(BF)

    seconds = split_streams(ring_gather(modulated_two), image_rows, rows)
    branch_grads = (
        (image_cot_all.astype(F32) * live * modulation[0, 5]).astype(BF),
        (text_cot_all.astype(F32) * (text_valid * live)[:, None] * modulation[1, 5]).astype(BF),
    )
    actives, hidden_grads, down_parts, second_parts = ([], [], [], [])
    for t in range(2):
        hidden = mm(seconds[t], up_cols[t]) + up_part[t]
        activated, pull = jax.vjp(gelu_tanh, hidden)
        actives.append(activated.astype(BF))
        grad_active = mm_nt(branch_grads[t], down_rows[t])
        hidden_grads.append(pull(grad_active)[0].astype(BF))
        second_parts.append(mm_nt(hidden_grads[t], up_cols[t]).astype(BF))
        down_parts.append(mm(actives[t], down_rows[t]).astype(BF))
    grad_two = ring_scatter(join_streams(*second_parts))
    grad_middle = own_cotan + norm_back(grad_two * both(4, 1.0), normed_two, inv_two)
    grad_attn = (grad_middle * both(2)).astype(BF)
    attn_grads = split_streams(ring_gather(grad_attn), image_rows, rows)

    branch = ring_scatter(join_streams(*down_parts)) + spread(down_bias.astype(F32))
    outs = ((middle + both(5) * branch) * row_mask).astype(BF)
    grad_gate_two = sums(own_cotan * branch)

    def scatter_rows(values):
        return lax.psum_scatter(values, SHARD, scatter_dimension=0, tiled=True)

    down_own = [scatter_rows(mm_tn(actives[t], branch_grads[t]).astype(BF)) for t in range(2)]
    up_own = [scatter_rows(mm_tn(seconds[t], hidden_grads[t]).astype(BF)) for t in range(2)]

    grad_mixed = jnp.concatenate([mm_nt(attn_grads[t], out_rows[t]).astype(BF) for t in range(2)])
    out_own = [scatter_rows(mm_tn(mixed_parts[t], attn_grads[t]).astype(BF)) for t in range(2)]
    grad_qkv = attention_backward(query, all_keys, all_values, key_bias, log_total, grad_mixed)
    grad_qkv = jnp.concatenate(grad_qkv, axis=1)
    proj_grads = (grad_qkv[:count], grad_qkv[count:])
    first_parts = [mm_nt(proj_grads[t], qkv_cols[t]) for t in range(2)]
    grad_one = ring_scatter(join_streams(*(f.astype(BF) for f in first_parts)))
    qkv_own = [scatter_rows(mm_tn(modulated_first[t], proj_grads[t]).astype(BF)) for t in range(2)]

    normed_one, inv_one = norm_rows(tokens)
    input_grad = grad_middle + norm_back(grad_one * both(1, 1.0), normed_one, inv_one)

    vectors = jnp.stack(
        [
            jnp.stack([jnp.sum(f, 0) for f in first_parts]),
            jnp.stack([jnp.sum(f * n, 0) for f, n in zip(first_parts, normed_first)]),
            sums(grad_middle * attn),
            sums(grad_two),
            sums(grad_two * normed_two),
            grad_gate_two,
            sums(grad_attn.astype(F32)),
            sums(own_cotan * both(5)),
        ],
        axis=1,
    )
    vectors = vectors.reshape(2, 8, 4, span).transpose(2, 0, 1, 3).reshape(4, 2 * 8 * span)
    vectors = jnp.sum(
        lax.all_to_all(vectors, "ctx", split_axis=0, concat_axis=0, tiled=True), axis=0
    )
    qv_sums = jnp.stack([jnp.sum(g.astype(F32), 0) for g in proj_grads]).reshape(2, 3, span)
    up_sums = jnp.stack([jnp.sum(g.astype(F32), 0) for g in hidden_grads])
    own_vector = jnp.concatenate(
        [vectors, qv_sums[:, 0].reshape(-1), qv_sums[:, 2].reshape(-1), up_sums.reshape(-1)]
    ).astype(BF)
    size = own_vector.shape[0]
    gathered = own_vector.reshape(1, 1, 1, 1, 4, size // 4)
    for axis, name in ((3, "ctx"), (1, "y")):
        here = lax.axis_index(name)
        blocks = jnp.concatenate(direct_gather(gathered, name), axis=axis)
        gathered = jnp.roll(blocks, here, axis=axis)
    for axis, name in ((0, "rep"), (2, "zh")):
        here = lax.axis_index(name)
        other = turn(gathered, name, 1)
        gathered = jnp.where(
            here == 0,
            jnp.concatenate([gathered, other], axis),
            jnp.concatenate([other, gathered], axis),
        )
    other = turn(gathered, "core", 1)
    gathered = jnp.stack([gathered, other], axis=3)
    gathered = jnp.where(lax.axis_index("core") == 0, gathered, gathered[:, :, :, ::-1])
    everything = gathered.reshape(2 * shards, 4, size)
    slots = 2 * shards
    vec_size = 2 * 8 * span
    table = everything[:, :, :vec_size].reshape(slots, 4, 2, 8, span).transpose(0, 2, 3, 1, 4)
    table = table.reshape(slots, 2, 8, width)
    slot_live = (all_sequences >= 0).astype(BF)[:, None, None, None]
    mod_rows = (table[:, :, :6] * slot_live).reshape(slots, -1)
    mod_weight_grad = mm_tn(slot_cond, mod_rows).reshape(mod_weight.shape)

    def owner_slice(values):
        part = values.shape[1] // (4 * shards)
        return lax.dynamic_slice_in_dim(values, owner_index * part, part, 1)

    mod_bias_grad = owner_slice(jnp.sum(mod_rows.astype(F32), 0).reshape(2, -1))
    out_bias_grad = owner_slice(jnp.sum(table[:, :, 6].astype(F32), 0))
    down_bias_grad = owner_slice(jnp.sum(table[:, :, 7].astype(F32), 0))
    rest = jnp.sum(everything[:, :, vec_size:].astype(F32), 0)
    q_total, v_total, up_total = (
        rest[:, a:b].reshape(4, 2, -1).transpose(1, 0, 2).reshape(2, -1)
        for a, b in ((0, 2 * span), (2 * span, 4 * span), (4 * span, 4 * span + 2 * ff_span))
    )
    qv_bias_grad = owner_slice(jnp.concatenate([q_total, v_total], axis=1))
    up_bias_grad = owner_slice(up_total)
    slot_grads = mm_nt(mod_rows, mod_matrix)
    grad_cond_cols = lax.dot_general(
        slot_hot, slot_grads, (((0,), (0,)), ((), ())), precision=lax.Precision.HIGHEST
    )
    cond_part = lax.dynamic_slice_in_dim(cond_float, owner_index * own_rows, own_rows, 1)
    cond_grad = jax.vjp(jax.nn.silu, cond_part)[1](grad_cond_cols)[0]

    col_back = jnp.stack(
        [
            jnp.concatenate([qkv_own[t], up_own[t]], axis=1).reshape(4, own_rows, -1)
            for t in range(2)
        ],
        axis=2,
    )
    col_back = lax.all_to_all(col_back, "ctx", split_axis=0, concat_axis=0, tiled=True)
    row_back = jnp.stack(
        [jnp.concatenate([out_own[t], down_own[t]]) for t in range(2)], axis=1
    )
    row_back = lax.ppermute(row_back, OWNER, from_slice)
    col_back = col_back.astype(F32) + turn(col_back, "rep", 1).astype(F32)
    row_back = row_back.astype(F32) + turn(row_back, "rep", 1).astype(F32)
    qkv_grad = (
        col_back[..., : 3 * span]
        .reshape(4, own_rows, 2, 3, span)
        .transpose(1, 2, 3, 0, 4)
        .reshape(qkv_weight.shape)
    )
    up_grad = col_back[..., 3 * span :].transpose(1, 2, 0, 3).reshape(up_weight.shape)
    out_grad, down_grad = (row_back[:own_rows], row_back[own_rows:])
    return (
        outs[None, :image_rows],
        outs[None, image_rows:],
        input_grad[None, :image_rows],
        input_grad[None, image_rows:],
        cond_grad,
        mod_weight_grad,
        mod_bias_grad,
        qkv_grad,
        qv_bias_grad,
        out_grad,
        out_bias_grad,
        up_grad,
        up_bias_grad,
        down_grad,
        down_bias_grad,
    )


def solution(mesh):
    fine = Mesh(mesh.devices.reshape(2, 4, 2, 2, 4), EVERY)
    rows = P(SLOT, "ctx", None)
    owned = P(OWNER, None, None)
    columns = P(None, OWNER)
    return jax.shard_map(
        per_device,
        mesh=fine,
        in_specs=(
            rows,
            rows,
            P(SLOT, "ctx"),
            P(SLOT),
            P(),
            owned,
            P(),
            owned,
            P(),
            owned,
            P(),
            owned,
            P(),
            owned,
            P(),
            rows,
            rows,
        ),
        out_specs=(
            rows,
            rows,
            rows,
            rows,
            columns,
            owned,
            columns,
            owned,
            columns,
            owned,
            columns,
            owned,
            columns,
            owned,
            columns,
        ),
        check_vma=False,
    )
```

```python
import jax
import jax.numpy as jnp
from jax import lax
from jax.sharding import Mesh, PartitionSpec as P

HEAD_DIM = 64
SHARD = ("y", "zh", "core")
TP = ("core", "ctx")
OWNER = ("y", "zh", "core", "ctx")
SLOT = ("rep", "y", "zh", "core")
EVERY = ("rep", "y", "zh", "core", "ctx")
BF = jnp.bfloat16
F32 = jnp.float32


def norm_rows(values):
    center = values - jnp.mean(values, axis=-1, keepdims=True)
    inv_scale = lax.rsqrt(jnp.mean(center * center, axis=-1, keepdims=True) + 1e-06)
    return (center * inv_scale, inv_scale)


def norm_back(grad_out, normed, inv_scale):
    return inv_scale * (
        grad_out
        - jnp.mean(grad_out, axis=-1, keepdims=True)
        - normed * jnp.mean(grad_out * normed, axis=-1, keepdims=True)
    )


def gelu_tanh(values):
    return jax.nn.gelu(values, approximate=True)


def mm(left, right):
    return jnp.dot(left, right, preferred_element_type=F32)


def mm_nt(left, right):
    return lax.dot_general(left, right, (((1,), (1,)), ((), ())), preferred_element_type=F32)


def mm_tn(left, right):
    return lax.dot_general(left, right, (((0,), (0,)), ((), ())), preferred_element_type=F32)


def split_heads(matrix):
    return matrix.reshape(matrix.shape[0], -1, HEAD_DIM)


def joint_scores(query, all_keys, all_bias):
    scores = jnp.einsum(
        "qhd,khd->hqk", split_heads(query), split_heads(all_keys), preferred_element_type=F32
    )
    return scores * 0.125 + all_bias[None, None, :]


def attention_forward(query, all_keys, all_values, all_bias):
    scores = joint_scores(query, all_keys, all_bias)
    top_score = jnp.max(scores, axis=-1, keepdims=True)
    exp_scores = jnp.exp(scores - top_score)
    row_total = jnp.sum(exp_scores, axis=-1, keepdims=True)
    log_total = top_score + jnp.log(row_total)
    weights = (exp_scores / row_total).astype(BF)
    mixed = jnp.einsum("hqk,khd->qhd", weights, split_heads(all_values), preferred_element_type=F32)
    return (mixed.reshape(query.shape).astype(BF), log_total)


def attention_backward(query, all_keys, all_values, all_bias, log_total, grad_mixed):
    grad_heads = split_heads(grad_mixed)
    probs = jnp.exp(joint_scores(query, all_keys, all_bias) - log_total)
    grad_probs = jnp.einsum(
        "qhd,khd->hqk", grad_heads, split_heads(all_values), preferred_element_type=F32
    )
    delta = jnp.sum(probs * grad_probs, axis=-1, keepdims=True)
    grad_scores = (probs * (grad_probs - delta)).astype(BF)
    grad_query = (
        jnp.einsum("hqk,khd->qhd", grad_scores, split_heads(all_keys), preferred_element_type=F32)
        * 0.125
    )
    grad_keys = (
        jnp.einsum("hqk,qhd->khd", grad_scores, split_heads(query), preferred_element_type=F32)
        * 0.125
    )
    grad_values = jnp.einsum(
        "hqk,qhd->khd", probs.astype(BF), grad_heads, preferred_element_type=F32
    )
    return tuple(g.reshape(query.shape).astype(BF) for g in (grad_query, grad_keys, grad_values))


def turn(values, axis, step):
    count = lax.axis_size(axis)
    return lax.ppermute(values, axis, [(i, (i + step) % count) for i in range(count)])


def cross(values):
    return lax.ppermute(values, ("rep", "zh"), [(0, 3), (3, 0), (1, 2), (2, 1)])


def after(values, *others):
    return lax.optimization_barrier((values, *others))[0]


def cut(values, axis, low, high):
    return lax.slice_in_dim(values, low, high, axis=axis)


def ring_gather(block, name="ctx", axis=0):
    size = block.shape[axis]
    half = size // 2 // 8 * 8
    behind = turn(block, name, 1)
    ahead = turn(block, name, -1)
    far_top = turn(cut(behind, axis, 0, half), name, 1)
    far_bottom = turn(cut(ahead, axis, half, size), name, -1)
    return [block, ahead, jnp.concatenate([far_top, far_bottom], axis), behind]


def ring_scatter(blocks, name="ctx", axis=0):
    size = blocks[0].shape[axis]
    half = size // 2 // 8 * 8
    from_behind = turn(cut(blocks[2], axis, 0, half), name, 1)
    from_ahead = turn(cut(blocks[2], axis, half, size), name, -1)
    to_ahead = jnp.concatenate(
        [cut(blocks[1], axis, 0, half) + from_behind, cut(blocks[1], axis, half, size)], axis
    )
    to_behind = jnp.concatenate(
        [cut(blocks[3], axis, 0, half), cut(blocks[3], axis, half, size) + from_ahead], axis
    )
    got_behind = turn(to_ahead, name, 1)
    got_ahead = turn(to_behind, name, -1)
    return blocks[0].astype(F32) + got_behind.astype(F32) + got_ahead.astype(F32)


def direct_gather(block, axis):
    return [block] + [turn(block, axis, -k) for k in range(1, lax.axis_size(axis))]


def pair(mine, axis):
    other = cross(mine)
    first = lax.axis_index("zh") == 0
    return jnp.where(
        first, jnp.concatenate([mine, other], axis), jnp.concatenate([other, mine], axis)
    )


def pair_sum(both_halves, axis):
    zh = lax.axis_index("zh")
    theirs = lax.dynamic_index_in_dim(both_halves, 1 - zh, axis, keepdims=False)
    mine = lax.dynamic_index_in_dim(both_halves, zh, axis, keepdims=False)
    half_sum = (mine.astype(F32) + cross(theirs).astype(F32)).astype(BF)
    return half_sum, turn(half_sum, "rep", 1)


def to_relative(values):
    size = values.shape[-1]
    return lax.dynamic_slice_in_dim(
        jnp.concatenate([values, values], -1), lax.axis_index("y") * (size // 4), size, values.ndim - 1
    )


def from_relative(values):
    size = values.shape[-1]
    start = (4 - lax.axis_index("y")) % 4 * (size // 4)
    return lax.dynamic_slice_in_dim(
        jnp.concatenate([values, values], -1), start, size, values.ndim - 1
    )


def split_streams(blocks, image_rows, rows):
    return (
        jnp.concatenate([b[:image_rows] for b in blocks]),
        jnp.concatenate([b[image_rows:rows] for b in blocks]),
    )


def join_streams(image, text):
    image_rows, text_rows = image.shape[0] // 4, text.shape[0] // 4
    return [
        jnp.concatenate(
            [
                image[k * image_rows : (k + 1) * image_rows],
                text[k * text_rows : (k + 1) * text_rows],
            ]
        )
        for k in range(4)
    ]


def per_device(
    image_tokens,
    text_tokens,
    text_lengths,
    slot_sequence,
    conditioning,
    mod_weight,
    mod_bias,
    qkv_weight,
    qv_bias,
    out_weight,
    out_bias,
    up_weight,
    up_bias,
    down_weight,
    down_bias,
    image_cotan,
    text_cotan,
):
    seq_total, width = conditioning.shape
    image_rows, text_cap = image_tokens.shape[1], text_tokens.shape[1]
    rows = image_rows + text_cap
    own_rows = mod_weight.shape[0]
    span, ff = width // 4, up_weight.shape[2]
    ff_span = ff // 4
    half_span, half_ff = span // 2, ff_span // 2
    position = lax.axis_index("ctx")
    core = lax.axis_index("core")
    owner_index = lax.axis_index(OWNER)
    shards = 16

    def from_columns(columns):
        got = lax.all_to_all(columns, TP, split_axis=0, concat_axis=0, tiled=True)
        return got.transpose(1, 0, 2, 3).reshape(2, 8 * own_rows, -1)

    qkv_got = from_columns(
        qkv_weight.reshape(own_rows, 2, 3, 4, 2, half_span)
        .transpose(4, 3, 1, 0, 2, 5)
        .reshape(8, 2, own_rows, 3 * half_span)
    )
    qkv_own = jnp.concatenate(ring_gather(pair(qkv_got, 1), "y", 1), 1)
    qkv_cols = (qkv_own, turn(qkv_own, "core", 1))

    all_sequences = lax.all_gather(after(slot_sequence, qkv_got), SLOT, axis=0, tiled=True)
    slot_hot = (
        all_sequences[:, None] == jnp.arange(seq_total, dtype=jnp.int32)[None, :]
    ).astype(F32)
    live = (slot_sequence[0] >= 0).astype(F32)
    cond_float = conditioning.astype(F32)
    cond_cols = lax.dynamic_slice_in_dim(
        jax.nn.silu(cond_float).astype(BF), owner_index * own_rows, own_rows, 1
    )
    slot_cond = mm(slot_hot.astype(BF), cond_cols).astype(BF)
    my_cond = lax.dynamic_slice_in_dim(slot_cond, lax.axis_index("rep") * shards, shards, 0)
    mod_matrix = mod_weight.reshape(own_rows, -1)
    partial_mod = mm(my_cond, mod_matrix).astype(BF)
    got_mod = lax.all_to_all(partial_mod, SHARD, split_axis=0, concat_axis=0, tiled=True)
    slot_mod = jnp.sum(got_mod.astype(F32), axis=0).astype(BF).reshape(8, -1)
    all_mod = direct_gather(slot_mod, "ctx")
    modulation = (
        sum(m.astype(F32) for m in all_mod).reshape(2, 6, width)
        + mod_bias.astype(F32).reshape(2, 6, width)
    ) * live

    meta = jnp.broadcast_to(text_lengths[0, 0].astype(BF), (8, width))
    own_tokens = jnp.concatenate([image_tokens[0], text_tokens[0], meta])
    token_blocks = ring_gather(to_relative(after(own_tokens, qkv_got)))
    image_all, text_all = split_streams(token_blocks, image_rows, rows)
    lengths = [b[rows, 0].astype(F32) for b in token_blocks]
    own_cots = jnp.concatenate([image_cotan[0], text_cotan[0]])
    cotan_blocks = ring_gather(after(own_cots, got_mod))
    image_cot_all, text_cot_all = split_streams(cotan_blocks, image_rows, rows)

    to_slice = []
    for source in range(4 * shards):
        y, zh, k, c = source // 16, source // 8 % 2, source // 4 % 2, source % 4
        to_slice.append((source, ((c * 2 + k) * 2 + zh) * 4 + y))
    from_slice = [(d, s) for s, d in to_slice]
    out_got = lax.ppermute(after(out_weight, got_mod).transpose(1, 0, 2), OWNER, to_slice)
    out_own = pair(lax.all_gather(out_got, "y", axis=1, tiled=True), 1)
    out_rows = jnp.concatenate([out_own, turn(out_own, "core", 1)], 1)
    up_got = from_columns(
        after(up_weight, got_mod)
        .reshape(own_rows, 2, 4, 2, half_ff)
        .transpose(3, 2, 1, 0, 4)
        .reshape(8, 2, own_rows, half_ff)
    )
    up_own = jnp.concatenate(ring_gather(pair(up_got, 1), "y", 1), 1)
    up_cols = (up_own, turn(up_own, "core", 1))
    down_got = lax.ppermute(after(down_weight, got_mod).transpose(1, 0, 2), OWNER, to_slice)
    down_own = pair(lax.all_gather(down_got, "y", axis=1, tiled=True), 1)
    down_rows = (down_own, turn(down_own, "core", 1))

    own_masks = (
        jnp.full((image_rows, 1), 1.0, F32) * live,
        (jnp.arange(text_cap, dtype=jnp.int32) < text_lengths[0, 0]).astype(F32)[:, None] * live,
    )
    row_mask = jnp.concatenate(own_masks)
    text_valid = jnp.concatenate(
        [(jnp.arange(text_cap, dtype=jnp.int32).astype(F32) < n).astype(F32) for n in lengths]
    )
    key_bias = jnp.concatenate(
        [jnp.zeros((4 * image_rows,), F32), (text_valid - 1.0) * 1000000000.0]
    )

    def bias_part(values, start, size):
        return [
            lax.dynamic_slice_in_dim(values, start + k * size, size, 1).astype(F32)
            for k in (core, 1 - core)
        ]

    q_bias = bias_part(qv_bias, position * span, half_span)
    v_bias = bias_part(qv_bias, width + position * span, half_span)
    up_part = bias_part(up_bias, position * ff_span, half_ff)
    first_mod = to_relative(modulation[:, :2])
    normed_first, modulated_first = ([], [])
    parts = [[], [], []]
    for t, tokens in enumerate((image_all, text_all)):
        normed, _ = norm_rows(tokens.astype(F32))
        modulated = (normed * (1.0 + first_mod[t, 1]) + first_mod[t, 0]).astype(BF)
        pieces = [[], [], []]
        for h in range(2):
            projected = mm(modulated, qkv_cols[h][t])
            pieces[0].append((projected[:, :half_span] + q_bias[h][t]).astype(BF))
            pieces[1].append(projected[:, half_span : 2 * half_span].astype(BF))
            pieces[2].append((projected[:, 2 * half_span :] + v_bias[h][t]).astype(BF))
        for part, piece in zip(parts, pieces):
            part.append(jnp.concatenate(piece, 1))
        normed_first.append(normed)
        modulated_first.append(modulated)
    query, all_keys, all_values = (jnp.concatenate(v) for v in parts)
    mixed, log_total = attention_forward(query, all_keys, all_values, key_bias)
    count = 4 * image_rows
    mixed_parts = (mixed[:count], mixed[count:])
    attn = ring_scatter(
        join_streams(*(mm(mixed_parts[t], out_rows[t]).astype(BF) for t in range(2)))
    )

    def both(at, plus=0.0):
        return jnp.concatenate(
            [
                jnp.broadcast_to(plus + modulation[0, at], (image_rows, width)),
                jnp.broadcast_to(plus + modulation[1, at], (text_cap, width)),
            ]
        )

    def spread(vectors):
        return jnp.concatenate(
            [
                jnp.broadcast_to(vectors[0], (image_rows, width)),
                jnp.broadcast_to(vectors[1], (text_cap, width)),
            ]
        )

    def sums(matrix):
        return jnp.stack([jnp.sum(matrix[:image_rows], 0), jnp.sum(matrix[image_rows:], 0)])

    tokens = jnp.concatenate([image_tokens[0], text_tokens[0]]).astype(F32)
    own_cotan = jnp.concatenate([image_cotan[0], text_cotan[0]]).astype(F32) * row_mask
    attn = attn + spread(out_bias.astype(F32))
    middle = tokens + both(2) * attn
    normed_two, inv_two = norm_rows(middle)
    modulated_two = (normed_two * both(4, 1.0) + both(3)).astype(BF)

    seconds = split_streams(ring_gather(to_relative(modulated_two)), image_rows, rows)
    branch_grads = (
        (image_cot_all.astype(F32) * live * modulation[0, 5]).astype(BF),
        (text_cot_all.astype(F32) * (text_valid * live)[:, None] * modulation[1, 5]).astype(BF),
    )
    actives, hidden_grads, down_parts, second_parts = ([], [], [], [])
    for t in range(2):
        active_halves, grad_halves = ([], [])
        for h in range(2):
            hidden = mm(seconds[t], up_cols[h][t]) + up_part[h][t]
            activated, pull = jax.vjp(gelu_tanh, hidden)
            active_halves.append(activated.astype(BF))
            grad_active = mm_nt(branch_grads[t], down_rows[h][t])
            grad_halves.append(pull(grad_active)[0].astype(BF))
        second_parts.append(
            (mm_nt(grad_halves[0], up_cols[0][t]) + mm_nt(grad_halves[1], up_cols[1][t])).astype(BF)
        )
        down_parts.append(
            (mm(active_halves[0], down_rows[0][t]) + mm(active_halves[1], down_rows[1][t])).astype(BF)
        )
        actives.append(active_halves)
        hidden_grads.append(grad_halves)
    grad_two = from_relative(ring_scatter(join_streams(*second_parts)))
    grad_middle = own_cotan + norm_back(grad_two * both(4, 1.0), normed_two, inv_two)
    grad_attn = (grad_middle * both(2)).astype(BF)
    attn_grads = split_streams(ring_gather(grad_attn), image_rows, rows)

    branch = ring_scatter(join_streams(*down_parts)) + spread(down_bias.astype(F32))
    outs = ((middle + both(5) * branch) * row_mask).astype(BF)
    grad_gate_two = sums(own_cotan * branch)

    def core_sum(own, other):
        return (own.astype(F32) + turn(other, "core", 1).astype(F32)).astype(BF)

    def columns_total(lefts, rights):
        own, other = (
            jnp.stack([mm_tn(lefts[t], rights[t][h]).astype(BF) for t in range(2)]) for h in range(2)
        )
        summed = core_sum(own, other)
        quarter = summed.shape[1] // 4
        blocks = [cut(summed, 1, j * quarter, (j + 1) * quarter) for j in range(4)]
        mine = ring_scatter(blocks, "y", 1).astype(BF)
        total, more = pair_sum(mine.reshape(2, 2, quarter // 2, -1), 1)
        total = (total.astype(F32) + more.astype(F32)).astype(BF)
        total = total.reshape(2, 8, own_rows, -1).transpose(1, 0, 2, 3)
        total = lax.all_to_all(total, TP, split_axis=0, concat_axis=0, tiled=True)
        return total.reshape((2, 4) + total.shape[1:]).astype(F32)

    def rows_total(lefts, rights):
        own, other = (
            jnp.stack([mm_tn(lefts[t][h], rights[t]).astype(BF) for t in range(2)]) for h in range(2)
        )
        summed = core_sum(own, other)
        summed = summed.reshape(4, summed.shape[1] // 2, -1)
        mine = lax.psum_scatter(summed, "y", scatter_dimension=1, tiled=True)
        total, more = pair_sum(mine.reshape((2, 2) + mine.shape[1:]), 1)
        total = (total.astype(F32) + more.astype(F32)).astype(BF)
        return lax.ppermute(total, OWNER, from_slice).astype(F32).transpose(1, 0, 2)

    down_grad = rows_total(actives, branch_grads)
    up_total = columns_total(seconds, hidden_grads)
    up_grad = up_total.transpose(3, 2, 1, 0, 4).reshape(up_weight.shape)

    grad_mixed = jnp.concatenate([mm_nt(attn_grads[t], out_rows[t]).astype(BF) for t in range(2)])
    out_grad = rows_total([(m[:, :half_span], m[:, half_span:]) for m in mixed_parts], attn_grads)
    grad_qkv = attention_backward(query, all_keys, all_values, key_bias, log_total, grad_mixed)
    proj_grads = []
    for low, high in ((0, count), (count, 4 * rows)):
        proj_grads.append(
            [
                jnp.concatenate(
                    [g[low:high, h * half_span : (h + 1) * half_span] for g in grad_qkv], axis=1
                )
                for h in range(2)
            ]
        )
    first_parts = [
        mm_nt(proj_grads[t][0], qkv_cols[0][t]) + mm_nt(proj_grads[t][1], qkv_cols[1][t])
        for t in range(2)
    ]
    grad_one = from_relative(ring_scatter(join_streams(*(f.astype(BF) for f in first_parts))))
    qkv_total = columns_total(modulated_first, proj_grads)
    qkv_grad = (
        qkv_total.reshape(2, 4, 2, own_rows, 3, half_span)
        .transpose(3, 2, 4, 1, 0, 5)
        .reshape(qkv_weight.shape)
    )

    normed_one, inv_one = norm_rows(tokens)
    input_grad = grad_middle + norm_back(grad_one * both(1, 1.0), normed_one, inv_one)

    vectors = jnp.stack(
        [
            from_relative(jnp.stack([jnp.sum(f, 0) for f in first_parts])),
            from_relative(
                jnp.stack([jnp.sum(f * n, 0) for f, n in zip(first_parts, normed_first)])
            ),
            sums(grad_middle * attn),
            sums(grad_two),
            sums(grad_two * normed_two),
            grad_gate_two,
            sums(grad_attn.astype(F32)),
            sums(own_cotan * both(5)),
        ],
        axis=1,
    )
    vectors = vectors.reshape(2, 8, 4, span).transpose(2, 0, 1, 3).reshape(4, 2 * 8 * span)
    vectors = jnp.sum(
        lax.all_to_all(vectors, "ctx", split_axis=0, concat_axis=0, tiled=True), axis=0
    )
    def in_order(halves):
        mine, other = (jnp.sum(h.astype(F32), 0) for h in halves)
        return jnp.where(
            core == 0, jnp.concatenate([mine, other], -1), jnp.concatenate([other, mine], -1)
        )

    q_sums, v_sums = (
        jnp.stack(
            [in_order([h[:, a * half_span : (a + 1) * half_span] for h in g]) for g in proj_grads]
        )
        for a in (0, 2)
    )
    up_sums = jnp.stack([in_order(g) for g in hidden_grads])
    own_vector = jnp.concatenate(
        [vectors, q_sums.reshape(-1), v_sums.reshape(-1), up_sums.reshape(-1)]
    ).astype(BF)
    size = own_vector.shape[0]
    gathered = own_vector.reshape(1, 1, 1, 1, 4, size // 4)
    for axis, name in ((3, "ctx"), (1, "y")):
        here = lax.axis_index(name)
        blocks = jnp.concatenate(direct_gather(gathered, name), axis=axis)
        gathered = jnp.roll(blocks, here, axis=axis)
    for axis, name in ((0, "rep"), (2, "zh")):
        here = lax.axis_index(name)
        other = turn(gathered, name, 1)
        gathered = jnp.where(
            here == 0,
            jnp.concatenate([gathered, other], axis),
            jnp.concatenate([other, gathered], axis),
        )
    other = turn(gathered, "core", 1)
    gathered = jnp.stack([gathered, other], axis=3)
    gathered = jnp.where(lax.axis_index("core") == 0, gathered, gathered[:, :, :, ::-1])
    everything = gathered.reshape(2 * shards, 4, size)
    slots = 2 * shards
    vec_size = 2 * 8 * span
    table = everything[:, :, :vec_size].reshape(slots, 4, 2, 8, span).transpose(0, 2, 3, 1, 4)
    table = table.reshape(slots, 2, 8, width)
    slot_live = (all_sequences >= 0).astype(BF)[:, None, None, None]
    mod_rows = (table[:, :, :6] * slot_live).reshape(slots, -1)
    mod_weight_grad = mm_tn(slot_cond, mod_rows).reshape(mod_weight.shape)

    def owner_slice(values):
        part = values.shape[1] // (4 * shards)
        return lax.dynamic_slice_in_dim(values, owner_index * part, part, 1)

    mod_bias_grad = owner_slice(jnp.sum(mod_rows.astype(F32), 0).reshape(2, -1))
    out_bias_grad = owner_slice(jnp.sum(table[:, :, 6].astype(F32), 0))
    down_bias_grad = owner_slice(jnp.sum(table[:, :, 7].astype(F32), 0))
    rest = jnp.sum(everything[:, :, vec_size:].astype(F32), 0)
    q_total, v_total, u_total = (
        rest[:, a:b].reshape(4, 2, -1).transpose(1, 0, 2).reshape(2, -1)
        for a, b in ((0, 2 * span), (2 * span, 4 * span), (4 * span, 4 * span + 2 * ff_span))
    )
    qv_bias_grad = owner_slice(jnp.concatenate([q_total, v_total], axis=1))
    up_bias_grad = owner_slice(u_total)
    slot_grads = mm_nt(mod_rows, mod_matrix)
    grad_cond_cols = lax.dot_general(
        slot_hot, slot_grads, (((0,), (0,)), ((), ())), precision=lax.Precision.HIGHEST
    )
    cond_part = lax.dynamic_slice_in_dim(cond_float, owner_index * own_rows, own_rows, 1)
    cond_grad = jax.vjp(jax.nn.silu, cond_part)[1](grad_cond_cols)[0]

    return (
        outs[None, :image_rows],
        outs[None, image_rows:],
        input_grad[None, :image_rows],
        input_grad[None, image_rows:],
        cond_grad,
        mod_weight_grad,
        mod_bias_grad,
        qkv_grad,
        qv_bias_grad,
        out_grad,
        out_bias_grad,
        up_grad,
        up_bias_grad,
        down_grad,
        down_bias_grad,
    )


def solution(mesh):
    fine = Mesh(mesh.devices.reshape(2, 4, 2, 2, 4), EVERY)
    rows = P(SLOT, "ctx", None)
    owned = P(OWNER, None, None)
    columns = P(None, OWNER)
    return jax.shard_map(
        per_device,
        mesh=fine,
        in_specs=(
            rows,
            rows,
            P(SLOT, "ctx"),
            P(SLOT),
            P(),
            owned,
            P(),
            owned,
            P(),
            owned,
            P(),
            owned,
            P(),
            owned,
            P(),
            rows,
            rows,
        ),
        out_specs=(
            rows,
            rows,
            rows,
            rows,
            columns,
            owned,
            columns,
            owned,
            columns,
            owned,
            columns,
            owned,
            columns,
            owned,
            columns,
        ),
        check_vma=False,
    )
```

```python
import functools

import jax
import jax.numpy as jnp
from jax import lax
from jax.experimental import pallas as pl
from jax.experimental.pallas import tpu as pltpu
from jax.sharding import Mesh, PartitionSpec as P

HEAD_DIM = 64
SHARD = ("y", "zh", "core")
TP = ("core", "ctx")
OWNER = ("y", "zh", "core", "ctx")
SLOT = ("rep", "y", "zh", "core")
EVERY = ("rep", "y", "zh", "core", "ctx")
BF = jnp.bfloat16
F32 = jnp.float32


def norm_rows(values):
    center = values - jnp.mean(values, axis=-1, keepdims=True)
    inv_scale = lax.rsqrt(jnp.mean(center * center, axis=-1, keepdims=True) + 1e-06)
    return (center * inv_scale, inv_scale)


def norm_back(grad_out, normed, inv_scale):
    return inv_scale * (
        grad_out
        - jnp.mean(grad_out, axis=-1, keepdims=True)
        - normed * jnp.mean(grad_out * normed, axis=-1, keepdims=True)
    )


def mm(left, right):
    return jnp.dot(left, right, preferred_element_type=F32)


def mm_nt(left, right):
    return lax.dot_general(left, right, (((1,), (1,)), ((), ())), preferred_element_type=F32)


def mm_tn(left, right):
    return lax.dot_general(left, right, (((0,), (0,)), ((), ())), preferred_element_type=F32)


GELU_A = 0.7978845608028654
GELU_B = 0.044715
PAD = 8


def gelu_both(values):
    square = values * values
    bent = jnp.tanh(values * (GELU_A + GELU_A * GELU_B * square))
    half_up = 0.5 + 0.5 * bent
    slope = GELU_A + 3.0 * GELU_A * GELU_B * square
    return values * half_up, half_up + 0.5 * values * (1.0 - bent * bent) * slope


def mlp_kernel(
    image_rows,
    second_in,
    grad_in,
    up_own,
    up_other,
    down_own,
    down_other,
    bias,
    second_out,
    down_out,
    d_up_own,
    d_up_other,
    d_down_own,
    d_down_other,
    bias_sums,
    turned,
    second_total,
    down_total,
):
    stream, chunk = pl.program_id(0), pl.program_id(1)
    last = pl.num_programs(1) - 1
    blocks, rows, width = second_in.shape

    def work(low, count):
        total = blocks * count
        left = second_in[:, low : low + count, :].reshape(total, width)
        grad = grad_in[:, low : low + count, :].reshape(total, width)

        @pl.when(chunk == 0)
        def _():
            turned[:, :total] = left.T
            second_total[:total, :] = jnp.zeros((total, width), F32)
            down_total[:total, :] = jnp.zeros((total, width), F32)

        halves = ((up_own, down_own, d_up_own, d_down_own), (up_other, down_other, d_up_other, d_down_other))
        for h, (up, down, d_up, d_down) in enumerate(halves):
            hidden = mm(left, up[0]) + bias[h, 0]
            active, slope = gelu_both(hidden)
            active = active.astype(BF)
            grad_hidden = (slope * mm_nt(grad, down[0])).astype(BF)
            second_total[:total, :] += mm_nt(grad_hidden, up[0])
            down_total[:total, :] += mm(active, down[0])
            d_up[0] = mm(turned[:, :total], grad_hidden).astype(BF)
            d_down[0] = mm_tn(active, grad).astype(BF)
            bias_sums[h, 0] = jnp.sum(grad_hidden.astype(F32), axis=0, keepdims=True)

        @pl.when(chunk == last)
        def _():
            second_out[:, low : low + count, :] = (
                second_total[:total, :].astype(BF).reshape(blocks, count, width)
            )
            down_out[:, low : low + count, :] = (
                down_total[:total, :].astype(BF).reshape(blocks, count, width)
            )

    @pl.when(stream == 0)
    def _():
        work(0, image_rows)

    @pl.when(stream == 1)
    def _():
        work(image_rows, rows - image_rows)


def mlp(image_rows, seconds, grads, ups, downs, bias):
    blocks, rows, width = seconds.shape
    hidden = ups[0].shape[2]
    chunk = min(256, hidden)
    whole = pl.BlockSpec((blocks, rows, width), lambda t, c: (0, 0, 0))
    columns = pl.BlockSpec((1, width, chunk), lambda t, c: (t, 0, c))
    lines = pl.BlockSpec((1, chunk, width), lambda t, c: (t, c, 0))
    line = pl.BlockSpec((2, 1, 1, chunk), lambda t, c: (0, t, 0, c))
    image_all = blocks * image_rows
    flops = 12 * blocks * rows * width * 2 * hidden
    moved = 16 * width * 2 * hidden + 8 * blocks * rows * width
    like = jax.ShapeDtypeStruct
    return pl.pallas_call(
        functools.partial(mlp_kernel, image_rows),
        grid=(2, hidden // chunk),
        in_specs=[whole, whole, columns, columns, lines, lines, line],
        out_specs=[whole, whole, columns, columns, lines, lines, line],
        out_shape=[
            like(seconds.shape, BF),
            like(seconds.shape, BF),
            like(ups[0].shape, BF),
            like(ups[0].shape, BF),
            like(downs[0].shape, BF),
            like(downs[0].shape, BF),
            like(bias.shape, F32),
        ],
        scratch_shapes=[
            pltpu.VMEM((width, image_all), BF),
            pltpu.VMEM((image_all, width), F32),
            pltpu.VMEM((image_all, width), F32),
        ],
        compiler_params=pltpu.CompilerParams(
            dimension_semantics=("arbitrary", "arbitrary"), vmem_limit_bytes=50 << 20
        ),
        cost_estimate=pl.CostEstimate(
            flops=flops, bytes_accessed=moved, transcendentals=2 * blocks * rows * hidden
        ),
        name="feed_forward",
    )(seconds, grads, ups[0], ups[1], downs[0], downs[1], bias)


def turn(values, axis, step):
    count = lax.axis_size(axis)
    return lax.ppermute(values, axis, [(i, (i + step) % count) for i in range(count)])


def cross(values):
    return lax.ppermute(values, ("rep", "zh"), [(0, 3), (3, 0), (1, 2), (2, 1)])


def after(values, *others):
    return lax.optimization_barrier((values, *others))[0]


def cut(values, axis, low, high):
    return lax.slice_in_dim(values, low, high, axis=axis)


def ring_scatter(blocks, name="ctx", axis=0):
    size = blocks[0].shape[axis]
    half = size // 2 // 8 * 8
    from_behind = turn(cut(blocks[2], axis, 0, half), name, 1)
    from_ahead = turn(cut(blocks[2], axis, half, size), name, -1)
    to_ahead = jnp.concatenate(
        [cut(blocks[1], axis, 0, half) + from_behind, cut(blocks[1], axis, half, size)], axis
    )
    to_behind = jnp.concatenate(
        [cut(blocks[3], axis, 0, half), cut(blocks[3], axis, half, size) + from_ahead], axis
    )
    got_behind = turn(to_ahead, name, 1)
    got_ahead = turn(to_behind, name, -1)
    return blocks[0].astype(F32) + got_behind.astype(F32) + got_ahead.astype(F32)


def direct_gather(block, axis):
    return [block] + [turn(block, axis, -k) for k in range(1, lax.axis_size(axis))]


def pair_sum(both_halves, axis):
    zh = lax.axis_index("zh")
    theirs = lax.dynamic_index_in_dim(both_halves, 1 - zh, axis, keepdims=False)
    mine = lax.dynamic_index_in_dim(both_halves, zh, axis, keepdims=False)
    half_sum = (mine.astype(F32) + cross(theirs).astype(F32)).astype(BF)
    return half_sum, turn(half_sum, "rep", 1)


def gather_ctx(block):
    gathered = lax.all_gather(block, "ctx", axis=0, tiled=True)
    return gathered.reshape((4,) + block.shape)


def scatter_ctx(blocks):
    flat = blocks.reshape(-1, blocks.shape[-1])
    return lax.psum_scatter(flat, "ctx", scatter_dimension=0, tiled=True).astype(F32)


def spread_mask(width, high):
    lane = lax.broadcasted_iota(jnp.int32, (1, width), 1)
    return ((lane >= HEAD_DIM) if high else (lane < HEAD_DIM)).astype(F32)


def key_bias_row(lengths, blocks, rows, image_rows):
    lane = lax.broadcasted_iota(jnp.int32, (1, blocks * rows), 1)
    bias = jnp.zeros((1, blocks * rows), F32)
    for c in range(blocks):
        first = c * rows + image_rows + lengths[c]
        bias = jnp.where((lane >= first) & (lane < (c + 1) * rows), -1000000000.0, bias)
    return bias


def softmax_rows(query, keys, bias):
    scores = mm_nt(query, keys) * 0.125 + bias
    grown = jnp.exp(scores - jnp.max(scores, axis=-1, keepdims=True))
    return grown / jnp.sum(grown, axis=-1, keepdims=True)


def lane_tile(ref, at, width=128):
    return ref[:, :, at : at + width].reshape(ref.shape[0] * ref.shape[1], width)


def attend_kernel(
    image_rows,
    lengths,
    tokens,
    mods,
    qkv_own,
    qkv_other,
    qkv_bias,
    out_own,
    out_other,
    modulated,
    proj_own,
    proj_other,
    mixed_own,
    mixed_other,
    partial,
):
    blocks, rows, width = tokens.shape
    streams = ((0, image_rows), (image_rows, rows))

    @pl.loop(0, blocks)
    def _(c):
        for t, (low, high) in enumerate(streams):
            normed, _ = norm_rows(tokens[c, low:high, :].astype(F32))
            modulated[c, low:high, :] = (normed * mods[t, 1:2, :] + mods[t, 0:1, :]).astype(BF)

    for t, (low, high) in enumerate(streams):
        left = modulated[:, low:high, :].reshape(-1, width)
        for h, (weight, proj) in enumerate(((qkv_own, proj_own), (qkv_other, proj_other))):
            values = (mm(left, weight[t]) + qkv_bias[h, t]).astype(BF)
            proj[:, low:high, :] = values.reshape(blocks, high - low, -1)
    bias = key_bias_row(lengths, blocks, rows, image_rows)
    low_mask, high_mask = (spread_mask(128, high) for high in (False, True))
    lower = low_mask > 0.5
    for proj, mixed in ((proj_own, mixed_own), (proj_other, mixed_other)):

        @pl.loop(0, blocks)
        def _(c):
            pair_query = proj[c, :, 0:128].astype(F32)
            pair_keys, pair_values = (lane_tile(proj, 256), lane_tile(proj, 384))
            pair_out = [
                mm(softmax_rows((pair_query * m).astype(BF), pair_keys, bias).astype(BF), pair_values)
                for m in (low_mask, high_mask)
            ]
            mixed[c, :, 0:128] = jnp.where(lower, pair_out[0], pair_out[1]).astype(BF)
            last_query = pltpu.roll(proj[c, :, 128:256].astype(F32), HEAD_DIM, 1) * high_mask
            weights = softmax_rows(last_query.astype(BF), lane_tile(proj, 128), bias).astype(BF)
            mixed[c, :, 128:192] = mm(weights, lane_tile(proj, 512, HEAD_DIM)).astype(BF)

    for t, (low, high) in enumerate(streams):
        total = None
        for mixed, weight in ((mixed_own, out_own), (mixed_other, out_other)):
            left = mixed[:, low:high, :].reshape(blocks * (high - low), -1)
            term = mm(left, weight[t])
            total = term if total is None else total + term
        partial[:, low:high, :] = total.astype(BF).reshape(blocks, high - low, width)


def attend(image_rows, lengths, tokens, mods, qkv_cols, qkv_bias, out_rows):
    blocks, rows, width = tokens.shape
    wide, deep = qkv_cols[0].shape[2], out_rows[0].shape[1]
    total = blocks * rows
    like = jax.ShapeDtypeStruct
    whole = pl.BlockSpec(memory_space=pltpu.VMEM)
    return pl.pallas_call(
        functools.partial(attend_kernel, image_rows),
        in_specs=[pl.BlockSpec(memory_space=pltpu.SMEM)] + [whole] * 7,
        out_specs=[whole] * 6,
        out_shape=[
            like(tokens.shape, BF),
            like((blocks, rows, wide), BF),
            like((blocks, rows, wide), BF),
            like((blocks, rows, deep), BF),
            like((blocks, rows, deep), BF),
            like(tokens.shape, BF),
        ],
        compiler_params=pltpu.CompilerParams(vmem_limit_bytes=50 << 20),
        cost_estimate=pl.CostEstimate(
            flops=4 * total * width * (wide + deep) + 32 * total * total * deep,
            bytes_accessed=12 * width * (wide + deep),
            transcendentals=6 * total * total,
        ),
        name="attend",
    )(lengths, tokens, mods, *qkv_cols, qkv_bias, *out_rows)


def attend_back_kernel(
    image_rows,
    lengths,
    grads,
    tokens,
    proj_own,
    proj_other,
    qkv_own,
    qkv_other,
    out_own,
    out_other,
    grad_own,
    grad_other,
    partial,
    row_sums,
    proj_sums,
    grad_mixed,
    pair_key,
    pair_value,
    last_query,
    last_key,
    last_value,
):
    blocks, rows, width = tokens.shape
    total_rows = blocks * rows
    streams = ((0, image_rows), (image_rows, rows))
    bias = key_bias_row(lengths, blocks, rows, image_rows)
    low_mask, high_mask = (spread_mask(128, high) for high in (False, True))
    lower = low_mask > 0.5
    halves = ((proj_own, qkv_own, out_own, grad_own), (proj_other, qkv_other, out_other, grad_other))
    for h, (proj, weight, out, grad) in enumerate(halves):
        for t, (low, high) in enumerate(streams):
            right = grads[:, low:high, :].reshape(-1, width)
            grad_mixed[:, low:high, :] = (
                mm_nt(right, out[t]).astype(BF).reshape(blocks, high - low, -1)
            )
        for total in (pair_key, pair_value, last_key, last_value):
            total[...] = jnp.zeros(total.shape, F32)

        @pl.loop(0, blocks)
        def _(c):
            pair_query = proj[c, :, 0:128].astype(F32)
            pair_grad = grad_mixed[c, :, 0:128].astype(F32)
            pair_keys, pair_values = (lane_tile(proj, 256), lane_tile(proj, 384))
            query_grads = []
            for mask in (low_mask, high_mask):
                query, back = ((v * mask).astype(BF) for v in (pair_query, pair_grad))
                probs = softmax_rows(query, pair_keys, bias)
                grad_probs = mm_nt(back, pair_values)
                delta = jnp.sum(probs * grad_probs, axis=-1, keepdims=True)
                grad_scores = (probs * (grad_probs - delta)).astype(BF)
                query_grads.append(mm(grad_scores, pair_keys))
                pair_key[...] += mm_tn(grad_scores, query)
                pair_value[...] += mm_tn(probs.astype(BF), back)
            grad[c, :, 0:128] = (
                jnp.where(lower, query_grads[0], query_grads[1]) * 0.125
            ).astype(BF)
            keys = lane_tile(proj, 128)
            query = (pltpu.roll(proj[c, :, 128:256].astype(F32), HEAD_DIM, 1) * high_mask).astype(BF)
            back = grad_mixed[c, :, 128:192]
            probs = softmax_rows(query, keys, bias)
            grad_probs = mm_nt(back, lane_tile(proj, 512, HEAD_DIM))
            delta = jnp.sum(probs * grad_probs, axis=-1, keepdims=True)
            grad_scores = (probs * (grad_probs - delta)).astype(BF)
            last_query[c] = pltpu.roll(mm(grad_scores, keys), HEAD_DIM, 1)
            last_key[...] += mm_tn(grad_scores, query)
            last_value[...] += mm_tn(probs.astype(BF), back)

        shape = (blocks, rows, 128)
        grad[:, :, 128:256] = (
            (jnp.where(lower, last_query[...].reshape(total_rows, 128), last_key[...]) * 0.125)
            .astype(BF)
            .reshape(shape)
        )
        grad[:, :, 256:384] = (pair_key[...] * 0.125).astype(BF).reshape(shape)
        grad[:, :, 384:512] = pair_value[...].astype(BF).reshape(shape)
        grad[:, :, 512:576] = last_value[...].astype(BF).reshape(blocks, rows, HEAD_DIM)

    for t, (low, high) in enumerate(streams):
        count = high - low
        rights = [g[:, low:high, :].reshape(blocks * count, -1) for g in (grad_own, grad_other)]
        for h, right in enumerate(rights):
            proj_sums[h, t] = jnp.sum(right.astype(F32), axis=0, keepdims=True)
        total = mm_nt(rights[0], qkv_own[t]) + mm_nt(rights[1], qkv_other[t])
        partial[:, low:high, :] = total.astype(BF).reshape(blocks, count, width)
        row_sums[t, 0:1, :] = jnp.sum(total, axis=0, keepdims=True)
        row_sums[t, 1:2, :] = jnp.zeros((1, width), F32)

    @pl.loop(0, blocks)
    def _(c):
        for t, (low, high) in enumerate(streams):
            normed, _ = norm_rows(tokens[c, low:high, :].astype(F32))
            row_sums[t, 1:2, :] += jnp.sum(
                normed * partial[c, low:high, :].astype(F32), axis=0, keepdims=True
            )


def attend_back(image_rows, lengths, grads, tokens, projs, qkv_cols, out_rows):
    blocks, rows, width = tokens.shape
    wide, deep = qkv_cols[0].shape[2], out_rows[0].shape[1]
    total = blocks * rows
    like = jax.ShapeDtypeStruct
    whole = pl.BlockSpec(memory_space=pltpu.VMEM)
    return pl.pallas_call(
        functools.partial(attend_back_kernel, image_rows),
        in_specs=[pl.BlockSpec(memory_space=pltpu.SMEM)] + [whole] * 8,
        out_specs=[whole] * 5,
        out_shape=[
            like(projs[0].shape, BF),
            like(projs[0].shape, BF),
            like(tokens.shape, BF),
            like((2, 2, width), F32),
            like((2, 2, 1, wide), F32),
        ],
        scratch_shapes=[
            pltpu.VMEM((blocks, rows, deep), BF),
            pltpu.VMEM((total, 128), F32),
            pltpu.VMEM((total, 128), F32),
            pltpu.VMEM((blocks, rows, 128), F32),
            pltpu.VMEM((total, 128), F32),
            pltpu.VMEM((total, HEAD_DIM), F32),
        ],
        compiler_params=pltpu.CompilerParams(vmem_limit_bytes=50 << 20),
        cost_estimate=pl.CostEstimate(
            flops=4 * total * width * (wide + deep) + 80 * total * total * deep,
            bytes_accessed=12 * width * (wide + deep),
            transcendentals=6 * total * total,
        ),
        name="attend_back",
    )(lengths, grads, tokens, *projs, *qkv_cols, *out_rows)


def attend_weights_kernel(
    image_rows,
    modulated,
    grad_own,
    grad_other,
    mixed_own,
    mixed_other,
    grads,
    d_qkv_own,
    d_qkv_other,
    d_out_own,
    d_out_other,
):
    blocks, rows, width = modulated.shape
    for t, (low, high) in enumerate(((0, image_rows), (image_rows, rows))):
        left = modulated[:, low:high, :].reshape(-1, width)
        right = grads[:, low:high, :].reshape(-1, width)
        turned = left.T
        for grad, d_qkv in ((grad_own, d_qkv_own), (grad_other, d_qkv_other)):
            values = grad[:, low:high, :].reshape(blocks * (high - low), -1)
            d_qkv[t] = mm(turned, values).astype(BF)
        for mixed, d_out in ((mixed_own, d_out_own), (mixed_other, d_out_other)):
            values = mixed[:, low:high, :].reshape(blocks * (high - low), -1)
            d_out[t] = mm_tn(values, right).astype(BF)


def attend_weights(image_rows, modulated, proj_grads, mixed, grads):
    blocks, rows, width = modulated.shape
    wide, deep = proj_grads[0].shape[2], mixed[0].shape[2]
    like = jax.ShapeDtypeStruct
    whole = pl.BlockSpec(memory_space=pltpu.VMEM)
    return pl.pallas_call(
        functools.partial(attend_weights_kernel, image_rows),
        in_specs=[whole] * 6,
        out_specs=[whole] * 4,
        out_shape=[
            like((2, width, wide), BF),
            like((2, width, wide), BF),
            like((2, deep, width), BF),
            like((2, deep, width), BF),
        ],
        compiler_params=pltpu.CompilerParams(vmem_limit_bytes=50 << 20),
        cost_estimate=pl.CostEstimate(
            flops=4 * blocks * rows * width * (wide + deep),
            bytes_accessed=8 * width * (wide + deep),
            transcendentals=0,
        ),
        name="attend_weights",
    )(modulated, *proj_grads, *mixed, grads)


def place_kernel(parts, count, index, *refs):
    pieces, out = refs[:-1], refs[-1]
    block = out.shape[1] // parts
    for piece, (shift, offset) in zip(pieces, count):
        start = pl.multiple_of(lax.rem(index[0] + shift, parts) * block + offset, 8)
        out[:, pl.ds(start, piece.shape[1]), :] = piece[...]


def place(pieces, index, parts):
    values = [p for p, _, _ in pieces]
    rows = sum(v.shape[1] for v in values)
    shape = (values[0].shape[0], rows, values[0].shape[2])
    whole = pl.BlockSpec(memory_space=pltpu.VMEM)
    return pl.pallas_call(
        functools.partial(place_kernel, parts, [(s, o) for _, s, o in pieces]),
        in_specs=[pl.BlockSpec(memory_space=pltpu.SMEM)] + [whole] * len(values),
        out_specs=whole,
        out_shape=jax.ShapeDtypeStruct(shape, BF),
        compiler_params=pltpu.CompilerParams(vmem_limit_bytes=20 << 20),
        cost_estimate=pl.CostEstimate(flops=0, bytes_accessed=4 * rows * shape[0] * shape[2], transcendentals=0),
        name="place",
    )(index.reshape(1), *values)


def ring_near(block):
    return block, turn(block, "y", 1), turn(block, "y", -1)


def ring_far(block, behind, ahead):
    size = block.shape[1]
    half = size // 2 // 8 * 8
    far_top = turn(cut(behind, 1, 0, half), "y", 1)
    far_bottom = turn(cut(ahead, 1, half, size), "y", -1)
    pieces = [(block, 0, 0), (ahead, 1, 0), (behind, 3, 0), (far_top, 2, 0), (far_bottom, 2, half)]
    return place(pieces, lax.axis_index("y").astype(jnp.int32), 4)


def pair(mine):
    pieces = [(mine, 0, 0), (cross(mine), 1, 0)]
    return place(pieces, lax.axis_index("zh").astype(jnp.int32), 2)


def per_device(
    image_tokens,
    text_tokens,
    text_lengths,
    slot_sequence,
    conditioning,
    mod_weight,
    mod_bias,
    qkv_weight,
    qv_bias,
    out_weight,
    out_bias,
    up_weight,
    up_bias,
    down_weight,
    down_bias,
    image_cotan,
    text_cotan,
):
    seq_total, width = conditioning.shape
    image_rows, text_cap = image_tokens.shape[1], text_tokens.shape[1]
    rows = image_rows + text_cap + PAD
    own_rows = mod_weight.shape[0]
    span, ff = width // 4, up_weight.shape[2]
    ff_span = ff // 4
    half_span, half_ff = span // 2, ff_span // 2
    position = lax.axis_index("ctx")
    core = lax.axis_index("core")
    rep, y, zh = lax.axis_index("rep"), lax.axis_index("y"), lax.axis_index("zh")
    owner_index = lax.axis_index(OWNER)
    shards = 16

    def from_columns(columns):
        got = lax.all_to_all(columns, TP, split_axis=0, concat_axis=0, tiled=True)
        return got.transpose(1, 0, 2, 3).reshape(2, 8 * own_rows, -1)

    cuts = [0, half_span, 2 * half_span, 3 * half_span]
    turn_at = cuts[2] - HEAD_DIM
    qkv_got = from_columns(
        jnp.concatenate(
            [
                part
                for v in [
                    qkv_weight.reshape(own_rows, 2, 3, 4, 2, half_span)
                    .transpose(4, 3, 1, 0, 2, 5)
                    .reshape(8, 2, own_rows, 3 * half_span)
                ]
                for part in (
                    v[..., : cuts[1]],
                    v[..., turn_at : cuts[2]],
                    v[..., cuts[1] : turn_at],
                    v[..., cuts[2] :],
                )
            ],
            axis=-1,
        )
    )
    qkv_pair = pair(qkv_got)
    qkv_own = ring_far(*ring_near(qkv_pair))
    qkv_cols = (qkv_own, turn(qkv_own, "core", 1))

    all_sequences = lax.all_gather(after(slot_sequence, qkv_got), SLOT, axis=0, tiled=True)
    slot_hot = (
        all_sequences[:, None] == jnp.arange(seq_total, dtype=jnp.int32)[None, :]
    ).astype(F32)
    live = (slot_sequence[0] >= 0).astype(F32)
    cond_float = conditioning.astype(F32)
    cond_cols = lax.dynamic_slice_in_dim(
        jax.nn.silu(cond_float).astype(BF), owner_index * own_rows, own_rows, 1
    )
    slot_cond = mm(slot_hot.astype(BF), cond_cols).astype(BF)
    my_cond = lax.dynamic_slice_in_dim(slot_cond, rep * shards, shards, 0)
    mod_matrix = mod_weight.reshape(own_rows, -1)
    partial_mod = mm(my_cond, mod_matrix).astype(BF)
    got_mod = lax.all_to_all(partial_mod, SHARD, split_axis=0, concat_axis=0, tiled=True)
    slot_mod = jnp.sum(got_mod.astype(F32), axis=0).astype(BF).reshape(8, -1)
    all_mod = direct_gather(slot_mod, "ctx")
    modulation = (
        sum(m.astype(F32) for m in all_mod).reshape(2, 6, width)
        + mod_bias.astype(F32).reshape(2, 6, width)
    ) * live

    meta = jnp.broadcast_to(text_lengths[0, 0].astype(BF), (PAD, width))
    own_tokens = jnp.concatenate([image_tokens[0], text_tokens[0], meta])
    own_cots = jnp.concatenate([image_cotan[0], text_cotan[0], jnp.zeros((PAD, width), BF)])
    gathered = gather_ctx(jnp.concatenate([after(own_tokens, qkv_got), own_cots])).reshape(
        4, 2, rows, width
    )
    tokens_all, cots_all = gathered[:, 0], gathered[:, 1]
    lengths = tokens_all[:, rows - 1, 0].astype(jnp.int32)
    row_at = jnp.arange(rows, dtype=jnp.int32)
    is_image = row_at < image_rows
    valid_all = (
        is_image[None, :] | (row_at[None, :] - image_rows < lengths[:, None])
    ).astype(F32)
    row_mask = (
        is_image | (row_at - image_rows < text_lengths[0, 0])
    ).astype(F32)[:, None] * live

    def by_row(vectors, plus=0.0):
        return jnp.where(is_image[:, None], vectors[0] + plus, vectors[1] + plus)

    to_slice = []
    for source in range(4 * shards):
        y_at, zh_at, i = source // 16, source // 8 % 2, source % 8
        to_slice.append((source, (i * 2 + zh_at) * 4 + y_at))
    from_slice = [(d, s) for s, d in to_slice]
    out_got = pair(
        lax.ppermute(after(out_weight, got_mod).transpose(1, 0, 2), OWNER, to_slice)
    )
    out_own = place(
        [(b, k, 0) for k, b in enumerate(direct_gather(out_got, "y"))], y.astype(jnp.int32), 4
    )
    out_rows = (out_own, turn(out_own, "core", 1))

    unit = own_down = down_weight.shape[0]
    wide_unit = -(-unit // 128) * 128
    lane_in, lane_out = (jnp.arange(8 * u, dtype=jnp.int32) for u in (unit, wide_unit))
    spacing = (
        (lane_in // unit * wide_unit + lane_in % unit)[:, None] == lane_out[None, :]
    ).astype(BF)
    up_wide = mm(
        after(up_weight, got_mod).transpose(1, 0, 2).reshape(16 * own_rows, 8 * unit), spacing
    ).astype(BF)
    up_send = mm_nt(
        up_wide.reshape(2 * own_rows, 8, 8, wide_unit)
        .transpose(2, 0, 1, 3)
        .reshape(16 * own_rows, 8 * wide_unit),
        spacing,
    ).astype(BF)
    up_pair = pair(from_columns(up_send.reshape(8, 2, own_rows, half_ff)))
    up_near = ring_near(after(up_pair, qkv_own))
    up_own = ring_far(*up_near)
    up_cols = (up_own, turn(up_own, "core", 1))
    down_pair = pair(after(down_weight, qkv_pair).transpose(1, 0, 2))
    down_own = ring_far(*ring_near(after(down_pair, up_own)))
    down_rows = (down_own, turn(down_own, "core", 1))

    def bias_part(values, start, size):
        return [
            lax.dynamic_slice_in_dim(values, start + k * size, size, 1).astype(F32)
            for k in (core, 1 - core)
        ]

    q_bias = bias_part(qv_bias, position * span, half_span)
    v_bias = bias_part(qv_bias, width + position * span, half_span)
    qkv_bias = jnp.stack(
        [jnp.concatenate([q, jnp.zeros_like(q), v], 1) for q, v in zip(q_bias, v_bias)]
    )[:, :, None, :]
    up_part = jnp.stack(
        [
            lax.dynamic_index_in_dim(
                up_bias.reshape(2, 8, 8, unit), k * 4 + position, 2, keepdims=False
            ).reshape(2, half_ff)
            for k in (core, 1 - core)
        ]
    ).astype(F32)[:, :, None, :]

    first_mod = modulation[:, :2] + jnp.array([0.0, 1.0], F32)[None, :, None]
    modulated_first, proj_own, proj_other, mixed_own, mixed_other, attn_parts = attend(
        image_rows, lengths, tokens_all, first_mod, qkv_cols, qkv_bias, out_rows
    )
    attn = scatter_ctx(after(attn_parts, *up_near))

    def sums(matrix):
        return jnp.stack([jnp.sum(matrix[:image_rows], 0), jnp.sum(matrix[image_rows:], 0)])

    tokens = own_tokens.astype(F32)
    own_cotan = own_cots.astype(F32) * row_mask
    attn = after(attn, up_own) + by_row(out_bias.astype(F32))
    middle = tokens + by_row(modulation[:, 2]) * attn
    normed_two, inv_two = norm_rows(middle)
    modulated_two = (normed_two * by_row(modulation[:, 4], 1.0) + by_row(modulation[:, 3])).astype(
        BF
    )

    seconds = gather_ctx(modulated_two)
    branch_grads = (
        cots_all.astype(F32) * (valid_all * live)[:, :, None] * by_row(modulation[:, 5])
    ).astype(BF)
    second_parts, down_parts, d_up_own, d_up_other, d_down_own, d_down_other, up_sums = mlp(
        image_rows, seconds, branch_grads, up_cols, down_rows, up_part
    )

    def core_blocks(own, other):
        got = turn(other, "core", 1)
        shape = (2, 4, own.shape[1] // 4, own.shape[2])
        mine, theirs = own.reshape(shape), got.reshape(shape)
        return [
            (
                lax.dynamic_index_in_dim(mine, (y + j) % 4, 1, keepdims=False).astype(F32)
                + lax.dynamic_index_in_dim(theirs, (y + j) % 4, 1, keepdims=False).astype(F32)
            ).astype(BF)
            for j in range(4)
        ]

    def block_total(mine):
        count = mine.shape[1] // 2
        total, more = pair_sum(mine.astype(BF).reshape(2, 2, count, -1), 1)
        return (total.astype(F32) + more.astype(F32)).astype(BF)

    def to_columns(total):
        total = total.reshape(2, 8, own_rows, -1).transpose(1, 0, 2, 3)
        return lax.all_to_all(total, TP, split_axis=0, concat_axis=0, tiled=True)

    up_blocks = core_blocks(d_up_own, d_up_other)
    down_blocks = core_blocks(d_down_own, d_down_other)
    grad_two = after(scatter_ctx(second_parts), *up_blocks, *down_blocks)
    up_mine = ring_scatter(up_blocks, "y", 1)
    down_blocks[2] = after(down_blocks[2], up_mine)
    down_mine = ring_scatter(down_blocks, "y", 1)

    grad_middle = own_cotan + norm_back(grad_two * by_row(modulation[:, 4], 1.0), normed_two, inv_two)
    grad_attn = (grad_middle * by_row(modulation[:, 2])).astype(BF)
    attn_grads = gather_ctx(grad_attn)

    branch = scatter_ctx(after(down_parts, attn_grads)) + by_row(down_bias.astype(F32))
    outs = ((middle + by_row(modulation[:, 5]) * branch) * row_mask).astype(BF)
    grad_gate_two = sums(own_cotan * branch)

    projs, mixed = (proj_own, proj_other), (mixed_own, mixed_other)
    grad_own, grad_other, first_parts, first_sums, proj_sums = attend_back(
        image_rows, lengths, after(attn_grads, up_mine), tokens_all, projs, qkv_cols, out_rows
    )
    first_parts = after(first_parts, down_mine, branch)
    grad_one = scatter_ctx(first_parts)
    d_qkv_own, d_qkv_other, d_out_own, d_out_other = attend_weights(
        image_rows, modulated_first, (grad_own, grad_other), mixed, attn_grads
    )
    qkv_blocks = core_blocks(d_qkv_own, d_qkv_other)
    out_blocks = core_blocks(d_out_own, d_out_other)
    up_total = to_columns(block_total(up_mine))
    down_total = block_total(down_mine)
    qkv_mine = ring_scatter(qkv_blocks, "y", 1)
    qkv_total = to_columns(block_total(qkv_mine))
    out_total = block_total(ring_scatter(out_blocks, "y", 1))

    qkv_total = qkv_total.astype(F32).reshape(2, 4, 2, own_rows, 3 * half_span)
    qkv_grad = (
        jnp.stack(
            [
                qkv_total[..., : cuts[1]],
                jnp.concatenate(
                    [qkv_total[..., cuts[1] + HEAD_DIM : cuts[2]], qkv_total[..., cuts[1] : cuts[1] + HEAD_DIM]],
                    -1,
                ),
                qkv_total[..., cuts[2] :],
            ],
            axis=4,
        )
        .transpose(3, 2, 4, 1, 0, 5)
        .reshape(qkv_weight.shape)
    )
    up_wide = mm(up_total.reshape(16 * own_rows, 8 * unit), spacing).astype(BF)
    up_grad = (
        mm_nt(
            up_wide.reshape(8, 2 * own_rows, 8, wide_unit)
            .transpose(1, 2, 0, 3)
            .reshape(16 * own_rows, 8 * wide_unit),
            spacing,
        )
        .reshape(2, own_rows, ff)
        .transpose(1, 0, 2)
    )
    down_grad = down_total.astype(F32).transpose(1, 0, 2)
    out_grad = lax.ppermute(out_total, OWNER, from_slice).astype(F32).transpose(1, 0, 2)

    normed_one, inv_one = norm_rows(tokens)
    input_grad = grad_middle + norm_back(
        grad_one * by_row(modulation[:, 1], 1.0), normed_one, inv_one
    )

    vectors = jnp.concatenate(
        [
            jnp.concatenate(
                [
                    first_sums,
                    jnp.stack(
                        [
                            sums(grad_middle * attn),
                            sums(grad_two),
                            sums(grad_two * normed_two),
                            grad_gate_two,
                        ],
                        axis=1,
                    ),
                ],
                axis=1,
            ).reshape(-1),
            sums(grad_attn.astype(F32)).reshape(-1),
            sums((own_cotan * by_row(modulation[:, 5])).astype(BF).astype(F32)).reshape(-1),
        ]
    ).reshape(8, -1)
    vectors = sum(direct_gather(vectors, "ctx")).astype(BF).reshape(-1)

    def in_order(mine, other):
        return jnp.where(
            core == 0, jnp.concatenate([mine, other], -1), jnp.concatenate([other, mine], -1)
        )

    q_sums, v_sums = (
        in_order(*(proj_sums[h, :, 0, a * half_span : (a + 1) * half_span] for h in range(2)))
        for a in (0, 2)
    )
    own_vector = jnp.concatenate(
        [vectors]
        + [v.astype(BF).reshape(-1) for v in (q_sums, v_sums, up_sums)]
    )[None]
    everything = jnp.concatenate(direct_gather(own_vector, "y"))
    everything = jnp.concatenate([everything, turn(everything, "rep", 1)])
    everything = jnp.concatenate([everything, cross(everything)])
    other_core = turn(everything, "core", 1)
    up_size = 2 * half_ff
    here_up = jnp.sum(everything[:, -2 * up_size : -up_size].astype(F32), 0) + jnp.sum(
        other_core[:, -up_size:].astype(F32), 0
    )
    everything = jnp.concatenate([everything, other_core])
    slots = 2 * shards
    at = jnp.arange(slots, dtype=jnp.int32)
    core_r, zh_r, rep_r, y_r = at // 16, at // 8 % 2, at // 4 % 2, at % 4
    natural = ((rep + rep_r + zh_r) % 2 * 16 + (y + y_r) % 4 * 4) + (
        (zh + zh_r) % 2 * 2 + (core + core_r) % 2
    )
    order = (natural[:, None] == at[None, :]).astype(F32)
    here_hot = mm(order, slot_hot)
    here_cond = mm(order.astype(BF), slot_cond).astype(BF)
    here_live = jnp.sum(here_hot, 1, keepdims=True)
    mod_size, wide = 12 * width, 2 * width
    mod_rows = everything[:, :mod_size] * here_live.astype(BF)
    mod_weight_grad = mm_tn(here_cond, mod_rows).reshape(mod_weight.shape)

    def owner_slice(values):
        part = values.shape[1] // (4 * shards)
        return lax.dynamic_slice_in_dim(values, owner_index * part, part, 1)

    totals = jnp.sum(everything[:, : -2 * up_size].astype(F32) * here_live, 0)
    mod_bias_grad = owner_slice(totals[:mod_size].reshape(2, -1))
    out_bias_grad = owner_slice(totals[mod_size : mod_size + wide].reshape(2, -1))
    down_bias_grad = owner_slice(totals[mod_size + wide : mod_size + 2 * wide].reshape(2, -1))
    rest = totals[mod_size + 2 * wide :].reshape(1, -1)
    rest = jnp.roll(jnp.concatenate(direct_gather(rest, "ctx")), position, axis=0)
    q_total, v_total = (
        rest[:, a:b].reshape(4, 2, -1).transpose(1, 0, 2).reshape(2, -1)
        for a, b in ((0, 2 * span), (2 * span, 4 * span))
    )
    qv_bias_grad = owner_slice(jnp.concatenate([q_total, v_total], axis=1))
    up_bias_grad = lax.dynamic_index_in_dim(
        here_up.reshape(2, 8, unit), y * 2 + zh, 1, keepdims=False
    )
    slot_grads = mm_nt(mod_rows, mod_matrix)
    grad_cond_cols = lax.dot_general(
        here_hot, slot_grads, (((0,), (0,)), ((), ())), precision=lax.Precision.HIGHEST
    )
    cond_part = lax.dynamic_slice_in_dim(cond_float, owner_index * own_rows, own_rows, 1)
    cond_grad = jax.vjp(jax.nn.silu, cond_part)[1](grad_cond_cols)[0]
    return (
        outs[None, :image_rows],
        outs[None, image_rows : image_rows + text_cap],
        input_grad[None, :image_rows],
        input_grad[None, image_rows : image_rows + text_cap],
        cond_grad,
        mod_weight_grad,
        mod_bias_grad,
        qkv_grad,
        qv_bias_grad,
        out_grad,
        out_bias_grad,
        up_grad,
        up_bias_grad,
        down_grad,
        down_bias_grad,
    )


def solution(mesh):
    fine = Mesh(mesh.devices.reshape(2, 4, 2, 2, 4), EVERY)
    rows = P(SLOT, "ctx", None)
    owned = P(OWNER, None, None)
    columns = P(None, OWNER)
    return jax.shard_map(
        per_device,
        mesh=fine,
        in_specs=(
            rows,
            rows,
            P(SLOT, "ctx"),
            P(SLOT),
            P(),
            owned,
            P(),
            owned,
            P(),
            owned,
            P(),
            owned,
            P(),
            owned,
            P(),
            rows,
            rows,
        ),
        out_specs=(
            rows,
            rows,
            rows,
            rows,
            columns,
            owned,
            columns,
            owned,
            columns,
            owned,
            columns,
            owned,
            columns,
            owned,
            columns,
        ),
        check_vma=False,
    )
```

```python
import functools

import jax
import jax.numpy as jnp
from jax import lax
from jax.experimental import pallas as pl
from jax.experimental.pallas import tpu as pltpu
from jax.sharding import Mesh, PartitionSpec as P

HEAD_DIM = 64
SHARD = ("y", "zh", "core")
TP = ("core", "ctx")
OWNER = ("y", "zh", "core", "ctx")
SLOT = ("rep", "y", "zh", "core")
EVERY = ("rep", "y", "zh", "core", "ctx")
BF = jnp.bfloat16
F32 = jnp.float32


def norm_rows(values):
    center = values - jnp.mean(values, axis=-1, keepdims=True)
    inv_scale = lax.rsqrt(jnp.mean(center * center, axis=-1, keepdims=True) + 1e-06)
    return (center * inv_scale, inv_scale)


def norm_back(grad_out, normed, inv_scale):
    return inv_scale * (
        grad_out
        - jnp.mean(grad_out, axis=-1, keepdims=True)
        - normed * jnp.mean(grad_out * normed, axis=-1, keepdims=True)
    )


def mm(left, right):
    return jnp.dot(left, right, preferred_element_type=F32)


def mm_nt(left, right):
    return lax.dot_general(left, right, (((1,), (1,)), ((), ())), preferred_element_type=F32)


def mm_tn(left, right):
    return lax.dot_general(left, right, (((0,), (0,)), ((), ())), preferred_element_type=F32)


GELU_A = 0.7978845608028654
GELU_B = 0.044715
PAD = 8


def gelu_both(values):
    square = values * values
    bent = jnp.tanh(values * (GELU_A + GELU_A * GELU_B * square))
    half_up = 0.5 + 0.5 * bent
    slope = GELU_A + 3.0 * GELU_A * GELU_B * square
    return values * half_up, half_up + 0.5 * values * (1.0 - bent * bent) * slope


def mlp_kernel(image_rows, second_in, grad_in, *refs):
    weights, bias, outs = refs[:8], refs[8], refs[9:]
    second_out, down_out, weight_grads, bias_sums = outs[0], outs[1], outs[2:10], outs[10]
    turned, second_total, down_total = outs[11:]
    stream, chunk = pl.program_id(0), pl.program_id(1)
    last = pl.num_programs(1) - 1
    blocks, rows, width = second_in.shape

    def work(low, count, t):
        total = blocks * count
        left = second_in[:, low : low + count, :].reshape(total, width)
        grad = grad_in[:, low : low + count, :].reshape(total, width)

        @pl.when(chunk == 0)
        def _():
            turned[:, :total] = left.T
            second_total[:total, :] = jnp.zeros((total, width), F32)
            down_total[:total, :] = jnp.zeros((total, width), F32)

        seconds = forwards = None
        for h in range(2):
            up, down = weights[4 * t + h], weights[4 * t + 2 + h]
            hidden = mm(left, up[...]) + bias[h, 0]
            active, slope = gelu_both(hidden)
            active = active.astype(BF)
            grad_hidden = (slope * mm_nt(grad, down[...])).astype(BF)
            second = mm_nt(grad_hidden, up[...])
            forward = mm(active, down[...])
            if h == 0:
                seconds, forwards = second, forward
            else:
                second_total[:total, :] += seconds + second
                down_total[:total, :] += forwards + forward
            weight_grads[4 * t + h][...] = mm(turned[:, :total], grad_hidden).astype(BF)
            weight_grads[4 * t + 2 + h][...] = mm_tn(active, grad).astype(BF)
            bias_sums[h, 0] = jnp.sum(grad_hidden.astype(F32), axis=0, keepdims=True)

        @pl.when(chunk == last)
        def _():
            second_out[:, low : low + count, :] = (
                second_total[:total, :].astype(BF).reshape(blocks, count, width)
            )
            down_out[:, low : low + count, :] = (
                down_total[:total, :].astype(BF).reshape(blocks, count, width)
            )

    @pl.when(stream == 0)
    def _():
        work(0, image_rows, 0)

    @pl.when(stream == 1)
    def _():
        work(image_rows, rows - image_rows, 1)


def cost(microseconds):
    return pl.CostEstimate(
        flops=int(microseconds * 1e9), bytes_accessed=int(microseconds * 1e6), transcendentals=0
    )


def mlp(image_rows, seconds, grads, ups, downs, bias):
    blocks, rows, width = seconds.shape
    hidden = ups[0][0].shape[1]
    chunk = min(256, hidden)
    last = hidden // chunk - 1
    whole = pl.BlockSpec((blocks, rows, width), lambda t, c: (0, 0, 0))
    at = [lambda t, c: jnp.where(t == 0, c, last), lambda t, c: jnp.where(t == 1, c, 0)]
    columns = [pl.BlockSpec((width, chunk), lambda t, c, f=f: (0, f(t, c))) for f in at]
    lines = [pl.BlockSpec((chunk, width), lambda t, c, f=f: (f(t, c), 0)) for f in at]
    line = pl.BlockSpec((2, 1, 1, chunk), lambda t, c: (0, t, 0, c))
    image_all = blocks * image_rows
    like = jax.ShapeDtypeStruct
    weights = [w for t in range(2) for w in (*ups[t], *downs[t])]
    specs = [v for t in range(2) for v in (columns[t], columns[t], lines[t], lines[t])]
    outs = pl.pallas_call(
        functools.partial(mlp_kernel, image_rows),
        grid=(2, hidden // chunk),
        in_specs=[whole, whole, *specs, line],
        out_specs=[whole, whole, *specs, line],
        out_shape=[
            like(seconds.shape, BF),
            like(seconds.shape, BF),
            *(like(w.shape, BF) for w in weights),
            like(bias.shape, F32),
        ],
        scratch_shapes=[
            pltpu.VMEM((width, image_all), BF),
            pltpu.VMEM((image_all, width), F32),
            pltpu.VMEM((image_all, width), F32),
        ],
        compiler_params=pltpu.CompilerParams(
            dimension_semantics=("arbitrary", "arbitrary"), vmem_limit_bytes=54 << 20
        ),
        cost_estimate=cost(20),
        name="feed_forward",
    )(seconds, grads, *weights, bias)
    return outs[0], outs[1], outs[2:10], outs[10]


def turn(values, axis, step):
    count = lax.axis_size(axis)
    return lax.ppermute(values, axis, [(i, (i + step) % count) for i in range(count)])


def cross(values):
    return lax.ppermute(values, ("rep", "zh"), [(0, 3), (3, 0), (1, 2), (2, 1)])


def after(values, *others):
    return lax.optimization_barrier((values, *others))[0]


def all_after(values, *others):
    return lax.optimization_barrier((tuple(values), *others))[0]


def cut(values, axis, low, high):
    return lax.slice_in_dim(values, low, high, axis=axis)


def scatter_near(top, bottom):
    return turn(top, "y", 1), turn(bottom, "y", -1)


def scatter_add(ahead, behind, got):
    half = got[0].shape[1]
    size = ahead.shape[1]
    to_ahead = jnp.concatenate([cut(ahead, 1, 0, half) + got[0], cut(ahead, 1, half, size)], 1)
    to_behind = jnp.concatenate([cut(behind, 1, 0, half), cut(behind, 1, half, size) + got[1]], 1)
    return to_ahead, to_behind


def scatter_last(mine, sent, others=()):
    got = (turn(sent[0], "y", 1), turn(sent[1], "y", -1))
    got_behind, got_ahead = all_after(got, *others) if others else got
    total = mine.astype(F32) + got_behind.astype(F32) + got_ahead.astype(F32)
    return total.astype(BF)


def direct_gather(block, axis):
    return [block] + [turn(block, axis, -k) for k in range(1, lax.axis_size(axis))]


def pair_sum(both_halves, axis):
    zh = lax.axis_index("zh")
    theirs = lax.dynamic_index_in_dim(both_halves, 1 - zh, axis, keepdims=False)
    mine = lax.dynamic_index_in_dim(both_halves, zh, axis, keepdims=False)
    half_sum = (mine.astype(F32) + cross(theirs).astype(F32)).astype(BF)
    return half_sum, turn(half_sum, "rep", 1)


def gather_ctx(block):
    gathered = lax.all_gather(block, "ctx", axis=0, tiled=True)
    return gathered.reshape((4,) + block.shape)


def scatter_ctx(blocks):
    flat = blocks.reshape(-1, blocks.shape[-1])
    return lax.psum_scatter(flat, "ctx", scatter_dimension=0, tiled=True)


def spread_mask(width, high):
    lane = lax.broadcasted_iota(jnp.int32, (1, width), 1)
    return ((lane >= HEAD_DIM) if high else (lane < HEAD_DIM)).astype(F32)


def key_bias_row(lengths, blocks, rows, image_rows):
    lane = lax.broadcasted_iota(jnp.int32, (1, blocks * rows), 1)
    bias = jnp.zeros((1, blocks * rows), F32)
    for c in range(blocks):
        first = c * rows + image_rows + lengths[c]
        bias = jnp.where((lane >= first) & (lane < (c + 1) * rows), -1000000000.0, bias)
    return bias


def softmax_rows(query, keys, bias):
    scores = mm_nt(query, keys) * 0.125 + bias
    grown = jnp.exp(scores - jnp.max(scores, axis=-1, keepdims=True))
    return grown / jnp.sum(grown, axis=-1, keepdims=True)


def lane_tile(ref, at, width=128):
    return ref[:, :, at : at + width].reshape(ref.shape[0] * ref.shape[1], width)


def attend_kernel(
    image_rows,
    lengths,
    tokens,
    mods,
    own_image,
    own_text,
    other_image,
    other_text,
    qkv_bias,
    modulated,
    proj_own,
    proj_other,
    mixed_own,
    mixed_other,
):
    blocks, rows, width = tokens.shape
    streams = ((0, image_rows), (image_rows, rows))

    @pl.loop(0, blocks)
    def _(c):
        for t, (low, high) in enumerate(streams):
            normed, _ = norm_rows(tokens[c, low:high, :].astype(F32))
            modulated[c, low:high, :] = (
                normed * (1.0 + mods[t, 1:2, :]) + mods[t, 0:1, :]
            ).astype(BF)

    for t, (low, high) in enumerate(streams):
        left = modulated[:, low:high, :].reshape(-1, width)
        sides = (((own_image, own_text), proj_own), ((other_image, other_text), proj_other))
        for h, (weight, proj) in enumerate(sides):
            values = (mm(left, weight[t][...]) + qkv_bias[h, t]).astype(BF)
            proj[:, low:high, :] = values.reshape(blocks, high - low, -1)
    bias = key_bias_row(lengths, blocks, rows, image_rows)
    low_mask, high_mask = (spread_mask(128, high) for high in (False, True))
    lower = low_mask > 0.5
    for proj, mixed in ((proj_own, mixed_own), (proj_other, mixed_other)):

        @pl.loop(0, blocks)
        def _(c):
            pair_query = proj[c, :, 0:128].astype(F32)
            pair_keys, pair_values = (lane_tile(proj, 256), lane_tile(proj, 384))
            pair_out = [
                mm(softmax_rows((pair_query * m).astype(BF), pair_keys, bias).astype(BF), pair_values)
                for m in (low_mask, high_mask)
            ]
            mixed[c, :, 0:128] = jnp.where(lower, pair_out[0], pair_out[1]).astype(BF)
            last_query = pltpu.roll(proj[c, :, 128:256].astype(F32), HEAD_DIM, 1) * high_mask
            weights = softmax_rows(last_query.astype(BF), lane_tile(proj, 128), bias).astype(BF)
            mixed[c, :, 128:192] = mm(weights, lane_tile(proj, 512))[:, :HEAD_DIM].astype(BF)


def attend_out_kernel(
    image_rows, mixed_own, mixed_other, out_own, out_other, partial
):
    blocks, rows, width = partial.shape
    streams = ((0, image_rows), (image_rows, rows))
    for t, (low, high) in enumerate(streams):
        total = None
        for mixed, weight in ((mixed_own, out_own), (mixed_other, out_other)):
            left = mixed[:, low:high, :].reshape(blocks * (high - low), -1)
            term = mm(left, weight[t])
            total = term if total is None else total + term
        partial[:, low:high, :] = total.astype(BF).reshape(blocks, high - low, width)


def attend(image_rows, lengths, tokens, mods, qkv_cols, qkv_bias):
    blocks, rows, width = tokens.shape
    wide, deep = qkv_cols[0][0].shape[1], 3 * HEAD_DIM
    total = blocks * rows
    like = jax.ShapeDtypeStruct
    whole = pl.BlockSpec(memory_space=pltpu.VMEM)
    return pl.pallas_call(
        functools.partial(attend_kernel, image_rows),
        in_specs=[pl.BlockSpec(memory_space=pltpu.SMEM)] + [whole] * 7,
        out_specs=[whole] * 5,
        out_shape=[
            like(tokens.shape, BF),
            like((blocks, rows, wide), BF),
            like((blocks, rows, wide), BF),
            like((blocks, rows, deep), BF),
            like((blocks, rows, deep), BF),
        ],
        compiler_params=pltpu.CompilerParams(vmem_limit_bytes=40 << 20),
        cost_estimate=cost(12),
        name="attend",
    )(lengths, tokens, mods, *qkv_cols[0], *qkv_cols[1], qkv_bias)


def attend_out(image_rows, mixed, out_rows):
    blocks, rows, deep = mixed[0].shape
    width = out_rows[0].shape[2]
    whole = pl.BlockSpec(memory_space=pltpu.VMEM)
    return pl.pallas_call(
        functools.partial(attend_out_kernel, image_rows),
        in_specs=[whole] * 4,
        out_specs=whole,
        out_shape=jax.ShapeDtypeStruct((blocks, rows, width), BF),
        compiler_params=pltpu.CompilerParams(vmem_limit_bytes=20 << 20),
        cost_estimate=cost(3),
        name="attend_out",
    )(*mixed, *out_rows)


def mod_kernel(conds, weights, out):
    for tile in range(out.shape[1]):
        out[:, tile, :] = mm(conds[...], weights[:, tile * 128 : (tile + 1) * 128]).astype(BF)


def mod_parts(conds, weights):
    slots, width = conds.shape[0], weights.shape[1]
    whole = pl.BlockSpec(memory_space=pltpu.VMEM)
    return pl.pallas_call(
        mod_kernel,
        in_specs=[whole] * 2,
        out_specs=whole,
        out_shape=jax.ShapeDtypeStruct((slots, width // 128, 128), BF),
        compiler_params=pltpu.CompilerParams(vmem_limit_bytes=16 << 20),
        cost_estimate=cost(1.5),
        name="mod_parts",
    )(conds, weights)


def attend_back_kernel(
    image_rows,
    lengths,
    grads,
    proj_own,
    proj_other,
    out_own,
    out_other,
    grad_own,
    grad_other,
    grad_mixed,
    pair_key,
    pair_value,
    last_query,
    last_key,
    last_value,
):
    blocks, rows, width = grads.shape
    total_rows = blocks * rows
    streams = ((0, image_rows), (image_rows, rows))
    bias = key_bias_row(lengths, blocks, rows, image_rows)
    low_mask, high_mask = (spread_mask(128, high) for high in (False, True))
    lower = low_mask > 0.5
    halves = ((proj_own, out_own, grad_own), (proj_other, out_other, grad_other))
    grad_mixed[...] = jnp.zeros(grad_mixed.shape, BF)
    for proj, out, grad in halves:
        for t, (low, high) in enumerate(streams):
            right = grads[:, low:high, :].reshape(-1, width)
            grad_mixed[:, low:high, 0:192] = (
                mm_nt(right, out[t]).astype(BF).reshape(blocks, high - low, -1)
            )
        for total in (pair_key, pair_value, last_key, last_value):
            total[...] = jnp.zeros(total.shape, F32)

        @pl.loop(0, blocks)
        def _(c):
            pair_query = proj[c, :, 0:128].astype(F32)
            pair_grad = grad_mixed[c, :, 0:128].astype(F32)
            pair_keys, pair_values = (lane_tile(proj, 256), lane_tile(proj, 384))
            query_grads = []
            for mask in (low_mask, high_mask):
                query, back = ((v * mask).astype(BF) for v in (pair_query, pair_grad))
                probs = softmax_rows(query, pair_keys, bias)
                grad_probs = mm_nt(back, pair_values)
                delta = jnp.sum(probs * grad_probs, axis=-1, keepdims=True)
                grad_scores = (probs * (grad_probs - delta)).astype(BF)
                query_grads.append(mm(grad_scores, pair_keys))
                pair_key[...] += mm_tn(grad_scores, query)
                pair_value[...] += mm_tn(probs.astype(BF), back)
            grad[c, :, 0:128] = (
                jnp.where(lower, query_grads[0], query_grads[1]) * 0.125
            ).astype(BF)
            keys = lane_tile(proj, 128)
            query = (pltpu.roll(proj[c, :, 128:256].astype(F32), HEAD_DIM, 1) * high_mask).astype(BF)
            back = grad_mixed[c, :, 128:256]
            probs = softmax_rows(query, keys, bias)
            grad_probs = mm_nt(back, lane_tile(proj, 512))
            delta = jnp.sum(probs * grad_probs, axis=-1, keepdims=True)
            grad_scores = (probs * (grad_probs - delta)).astype(BF)
            last_query[c] = pltpu.roll(mm(grad_scores, keys), HEAD_DIM, 1)
            last_key[...] += mm_tn(grad_scores, query)
            last_value[...] += mm_tn(probs.astype(BF), back)

        shape = (blocks, rows, 128)
        grad[:, :, 128:256] = (
            (jnp.where(lower, last_query[...].reshape(total_rows, 128), last_key[...]) * 0.125)
            .astype(BF)
            .reshape(shape)
        )
        grad[:, :, 256:384] = (pair_key[...] * 0.125).astype(BF).reshape(shape)
        grad[:, :, 384:512] = pair_value[...].astype(BF).reshape(shape)
        grad[:, :, 512:640] = last_value[...].astype(BF).reshape(shape)


def attend_rows_kernel(
    image_rows,
    tokens,
    grad_own,
    grad_other,
    own_image,
    own_text,
    other_image,
    other_text,
    partial,
    row_sums,
    proj_sums,
):
    blocks, rows, width = tokens.shape
    streams = ((0, image_rows), (image_rows, rows))
    for t, (low, high) in enumerate(streams):
        count = high - low
        rights = [g[:, low:high, :].reshape(blocks * count, -1) for g in (grad_own, grad_other)]
        for h, right in enumerate(rights):
            proj_sums[h, t] = jnp.sum(right.astype(F32), axis=0, keepdims=True)
        own, other = ((own_image, other_image), (own_text, other_text))[t]
        total = mm_nt(rights[0], own[...]) + mm_nt(rights[1], other[...])
        partial[:, low:high, :] = total.astype(BF).reshape(blocks, count, width)
        row_sums[t, 0:1, :] = jnp.sum(total, axis=0, keepdims=True)
        row_sums[t, 1:2, :] = jnp.zeros((1, width), F32)

    @pl.loop(0, blocks)
    def _(c):
        for t, (low, high) in enumerate(streams):
            normed, _ = norm_rows(tokens[c, low:high, :].astype(F32))
            row_sums[t, 1:2, :] += jnp.sum(
                normed * partial[c, low:high, :].astype(F32), axis=0, keepdims=True
            )


def attend_back(image_rows, lengths, grads, projs, out_rows):
    blocks, rows, width = grads.shape
    deep = out_rows[0].shape[1]
    total = blocks * rows
    like = jax.ShapeDtypeStruct
    whole = pl.BlockSpec(memory_space=pltpu.VMEM)
    return pl.pallas_call(
        functools.partial(attend_back_kernel, image_rows),
        in_specs=[pl.BlockSpec(memory_space=pltpu.SMEM)] + [whole] * 5,
        out_specs=[whole] * 2,
        out_shape=[like(projs[0].shape, BF), like(projs[0].shape, BF)],
        scratch_shapes=[
            pltpu.VMEM((blocks, rows, 256), BF),
            pltpu.VMEM((total, 128), F32),
            pltpu.VMEM((total, 128), F32),
            pltpu.VMEM((blocks, rows, 128), F32),
            pltpu.VMEM((total, 128), F32),
            pltpu.VMEM((total, 128), F32),
        ],
        compiler_params=pltpu.CompilerParams(vmem_limit_bytes=40 << 20),
        cost_estimate=cost(13),
        name="attend_back",
    )(lengths, grads, *projs, *out_rows)


def attend_rows(image_rows, tokens, proj_grads, qkv_cols):
    blocks, rows, width = tokens.shape
    wide = qkv_cols[0][0].shape[1]
    like = jax.ShapeDtypeStruct
    whole = pl.BlockSpec(memory_space=pltpu.VMEM)
    return pl.pallas_call(
        functools.partial(attend_rows_kernel, image_rows),
        in_specs=[whole] * 7,
        out_specs=[whole] * 3,
        out_shape=[
            like(tokens.shape, BF),
            like((2, 2, width), F32),
            like((2, 2, 1, wide), F32),
        ],
        compiler_params=pltpu.CompilerParams(vmem_limit_bytes=40 << 20),
        cost_estimate=cost(5),
        name="attend_rows",
    )(tokens, *proj_grads, *qkv_cols[0], *qkv_cols[1])


def attend_weights_kernel(
    image_rows,
    modulated,
    grad_own,
    grad_other,
    mixed_own,
    mixed_other,
    grads,
    own_image,
    own_text,
    other_image,
    other_text,
    d_out_own,
    d_out_other,
):
    blocks, rows, width = modulated.shape
    for t, (low, high) in enumerate(((0, image_rows), (image_rows, rows))):
        left = modulated[:, low:high, :].reshape(-1, width)
        right = grads[:, low:high, :].reshape(-1, width)
        turned = left.T
        sides = ((own_image, other_image), (own_text, other_text))[t]
        for grad, d_qkv in zip((grad_own, grad_other), sides):
            values = grad[:, low:high, :].reshape(blocks * (high - low), -1)
            d_qkv[...] = mm(turned, values).astype(BF)
        for mixed, d_out in ((mixed_own, d_out_own), (mixed_other, d_out_other)):
            values = mixed[:, low:high, :].reshape(blocks * (high - low), -1)
            d_out[t] = mm_tn(values, right).astype(BF)


def attend_weights(image_rows, modulated, proj_grads, mixed, grads):
    blocks, rows, width = modulated.shape
    wide, deep = proj_grads[0].shape[2], mixed[0].shape[2]
    like = jax.ShapeDtypeStruct
    whole = pl.BlockSpec(memory_space=pltpu.VMEM)
    return pl.pallas_call(
        functools.partial(attend_weights_kernel, image_rows),
        in_specs=[whole] * 6,
        out_specs=[whole] * 6,
        out_shape=[
            *(like((width, wide), BF) for _ in range(4)),
            like((2, deep, width), BF),
            like((2, deep, width), BF),
        ],
        compiler_params=pltpu.CompilerParams(vmem_limit_bytes=50 << 20),
        cost_estimate=cost(6),
        name="attend_weights",
    )(modulated, *proj_grads, *mixed, grads)


def rows_one_kernel(image_rows, got, tokens, mods, out_bias, second):
    for t, (low, high) in enumerate(((0, image_rows), (image_rows, got.shape[0]))):
        attn = got[low:high, :].astype(F32) + out_bias[t : t + 1, :]
        normed, _ = norm_rows(tokens[low:high, :].astype(F32) + mods[t, 2:3, :] * attn)
        second[low:high, :] = (normed * (1.0 + mods[t, 4:5, :]) + mods[t, 3:4, :]).astype(BF)


def masked(cots, t, length, live):
    row = lax.broadcasted_iota(jnp.int32, cots.shape, 0)
    keep = live if t == 0 else jnp.where(row < length, live, 0.0)
    return cots.astype(F32) * keep


def rows_two_kernel(
    image_rows, length, live, got, tokens, mods, out_bias, cots, back, grad_attn, grad_middle, sums
):
    for t, (low, high) in enumerate(((0, image_rows), (image_rows, got.shape[0]))):
        attn = got[low:high, :].astype(F32) + out_bias[t : t + 1, :]
        normed, inv = norm_rows(tokens[low:high, :].astype(F32) + mods[t, 2:3, :] * attn)
        grad_two = back[low:high, :].astype(F32)
        middle = masked(cots[low:high, :], t, length[0], live[0]) + norm_back(
            grad_two * (1.0 + mods[t, 4:5, :]), normed, inv
        )
        grad_middle[low:high, :] = middle
        grad = (middle * mods[t, 2:3, :]).astype(BF)
        grad_attn[low:high, :] = grad
        terms = (middle * attn, grad_two, grad_two * normed, grad.astype(F32))
        for k, term in enumerate(terms):
            sums[t, k : k + 1, :] = jnp.sum(term, axis=0, keepdims=True)


def rows_three_kernel(
    image_rows,
    length,
    live,
    got,
    tokens,
    mods,
    out_bias,
    cots,
    branch_got,
    down_bias,
    image_out,
    text_out,
    sums,
):
    for t, (low, high) in enumerate(((0, image_rows), (image_rows, got.shape[0]))):
        attn = got[low:high, :].astype(F32) + out_bias[t : t + 1, :]
        middle = tokens[low:high, :].astype(F32) + mods[t, 2:3, :] * attn
        branch = branch_got[low:high, :].astype(F32) + down_bias[t : t + 1, :]
        grad = masked(cots[low:high, :], t, length[0], live[0])
        keep = masked(jnp.ones(grad.shape, F32), t, length[0], live[0])
        out = ((middle + mods[t, 5:6, :] * branch) * keep).astype(BF)
        target = (image_out, text_out)[t]
        target[0] = out[: target.shape[1], :]
        back = (grad * mods[t, 5:6, :]).astype(BF).astype(F32)
        for k, term in enumerate((grad * branch, back)):
            sums[t, k : k + 1, :] = jnp.sum(term, axis=0, keepdims=True)


def rows_four_kernel(image_rows, tokens, mods, back, grad_middle, image_grad, text_grad):
    for t, (low, high) in enumerate(((0, image_rows), (image_rows, tokens.shape[0]))):
        normed, inv = norm_rows(tokens[low:high, :].astype(F32))
        grad = grad_middle[low:high, :] + norm_back(
            back[low:high, :].astype(F32) * (1.0 + mods[t, 1:2, :]), normed, inv
        )
        target = (image_grad, text_grad)[t]
        target[0] = grad[: target.shape[1], :]


def rows_call(kernel, image_rows, name, outs, scalars, arrays):
    whole = pl.BlockSpec(memory_space=pltpu.VMEM)
    return pl.pallas_call(
        functools.partial(kernel, image_rows),
        in_specs=[pl.BlockSpec(memory_space=pltpu.SMEM)] * len(scalars) + [whole] * len(arrays),
        out_specs=[whole] * len(outs),
        out_shape=[jax.ShapeDtypeStruct(shape, dtype) for shape, dtype in outs],
        compiler_params=pltpu.CompilerParams(vmem_limit_bytes=24 << 20),
        cost_estimate=cost(3),
        name=name,
    )(*scalars, *arrays)


def unpack_kernel(layout, spots, y, zh, *refs):
    pieces, outs = refs[:5], refs[5:]
    for piece, (shift, halves) in zip(pieces, spots):
        for half, base in halves:
            spot = lax.rem(y[0] + shift, 4) * 2 + lax.rem(zh[0] + half, 2)
            for which, rows, low, high, first in layout:
                start = pl.multiple_of(spot * rows, 16)
                outs[which][pl.ds(start, rows), low:high] = piece[
                    0, base + first : base + first + rows, 0 : high - low
                ]


def unpack(layout, shapes, block, near, far):
    size = block.shape[1] // 2
    pair_at = [(0, 0), (1, size)]
    spots = [(0, pair_at), (3, pair_at), (1, pair_at), (2, [(0, 0)]), (2, [(1, 0)])]
    index = [lax.axis_index(n).astype(jnp.int32).reshape(1) for n in ("y", "zh")]
    whole = pl.BlockSpec(memory_space=pltpu.VMEM)
    return pl.pallas_call(
        functools.partial(unpack_kernel, layout, spots),
        in_specs=[pl.BlockSpec(memory_space=pltpu.SMEM)] * 2 + [whole] * 5,
        out_specs=[whole] * len(shapes),
        out_shape=[jax.ShapeDtypeStruct(v, BF) for v in shapes],
        compiler_params=pltpu.CompilerParams(vmem_limit_bytes=30 << 20),
        cost_estimate=cost(4),
        name="unpack",
    )(*index, block, *near, *far)


def sum_kernel(layout, size, count, y, *refs):
    owns, gots, outs = refs[:count], refs[count : 2 * count], refs[2 * count :]
    step = pl.program_id(0)

    def write(out, zone, base):
        for which, rows, low, high, first in layout:
            source = pl.ds(zone * rows, rows)
            value = owns[which][source, low:high].astype(F32) + gots[which][source, low:high].astype(F32)
            out[0, base + first : base + first + rows, 0 : high - low] = value.astype(BF)
            if high - low < out.shape[2]:
                out[0, base + first : base + first + rows, high - low :] = jnp.zeros(
                    (rows, out.shape[2] - high + low), BF
                )

    for j, targets in enumerate(((outs[0],), (outs[1],), (outs[2], outs[3]), (outs[4],))):

        @pl.when(step == j)
        def _(targets=targets):
            for zone in range(2):
                if len(targets) == 2:
                    write(targets[zone], zone, 0)
                else:
                    write(targets[0], zone, zone * size)


def sum_blocks(layout, size, wide, owns, gots, name):
    blocks = [
        pl.BlockSpec((v.shape[0] // 4, v.shape[1]), lambda j, y: (lax.rem(y[0] + j, 4), 0))
        for v in owns
    ]
    fixed = [pl.BlockSpec((1, n * size, wide), lambda j, y: (0, 0, 0)) for n in (2, 2, 1, 1, 2)]
    return pl.pallas_call(
        functools.partial(sum_kernel, layout, size, len(owns)),
        grid_spec=pltpu.PrefetchScalarGridSpec(
            num_scalar_prefetch=1, grid=(4,), in_specs=blocks + blocks, out_specs=fixed
        ),
        out_shape=[jax.ShapeDtypeStruct((1, n * size, wide), BF) for n in (2, 2, 1, 1, 2)],
        compiler_params=pltpu.CompilerParams(
            dimension_semantics=("arbitrary",), vmem_limit_bytes=40 << 20
        ),
        cost_estimate=cost(4),
        name=name,
    )(lax.axis_index("y").astype(jnp.int32).reshape(1), *owns, *gots)


def near_of(block):
    return turn(block, "y", 1), turn(block, "y", -1)


def far_of(near):
    half = near[0].shape[1] // 2
    return turn(cut(near[0], 1, 0, half), "y", 1), turn(cut(near[1], 1, half, 2 * half), "y", -1)


def mod_last_kernel(table, conds, weights, weight_grad, slot_grad, totals):
    total = jnp.zeros(slot_grad.shape, F32)
    for tile in range(weights.shape[1] // 128):
        lanes = slice(tile * 128, (tile + 1) * 128)
        values = table[:, tile, :]
        weight_grad[:, lanes] = mm_tn(conds[...], values)
        total += mm_nt(values, weights[:, lanes])
    slot_grad[...] = total
    for tile in range(0, table.shape[1], 8):
        totals[tile : tile + 8, :] = jnp.sum(table[:, tile : tile + 8, :].astype(F32), axis=0)


def mod_last(table, conds, weights):
    like = jax.ShapeDtypeStruct
    whole = pl.BlockSpec(memory_space=pltpu.VMEM)
    return pl.pallas_call(
        mod_last_kernel,
        in_specs=[whole] * 3,
        out_specs=[whole] * 3,
        out_shape=[
            like(weights.shape, F32),
            like(conds.shape, F32),
            like(table.shape[1:], F32),
        ],
        compiler_params=pltpu.CompilerParams(vmem_limit_bytes=24 << 20),
        cost_estimate=cost(4),
        name="mod_last",
    )(table, conds, weights)


def per_device(
    image_tokens,
    text_tokens,
    text_lengths,
    slot_sequence,
    conditioning,
    mod_weight,
    mod_bias,
    qkv_weight,
    qv_bias,
    out_weight,
    out_bias,
    up_weight,
    up_bias,
    down_weight,
    down_bias,
    image_cotan,
    text_cotan,
):
    seq_total, width = conditioning.shape
    image_rows, text_cap = image_tokens.shape[1], text_tokens.shape[1]
    rows = image_rows + text_cap + PAD
    own_rows = mod_weight.shape[0]
    span, ff = width // 4, up_weight.shape[2]
    ff_span = ff // 4
    half_span, half_ff = span // 2, ff_span // 2
    position = lax.axis_index("ctx")
    core = lax.axis_index("core")
    rep, y, zh = lax.axis_index("rep"), lax.axis_index("y"), lax.axis_index("zh")
    owner_index = lax.axis_index(OWNER)
    shards = 16

    def from_columns(columns):
        got = lax.all_to_all(columns, TP, split_axis=0, concat_axis=0, tiled=True)
        return got.transpose(1, 0, 2, 3).reshape(2, 8 * own_rows, -1)

    cuts = [0, half_span, 2 * half_span, 3 * half_span]
    turn_at = cuts[2] - HEAD_DIM
    qkv_got = from_columns(
        jnp.concatenate(
            [
                part
                for v in [
                    qkv_weight.reshape(own_rows, 2, 3, 4, 2, half_span)
                    .transpose(4, 3, 1, 0, 2, 5)
                    .reshape(8, 2, own_rows, 3 * half_span)
                ]
                for part in (
                    v[..., : cuts[1]],
                    v[..., turn_at : cuts[2]],
                    v[..., cuts[1] : turn_at],
                    v[..., cuts[2] :],
                    jnp.zeros(v.shape[:-1] + (HEAD_DIM,), BF),
                )
            ],
            axis=-1,
        )
    )

    to_slice = []
    for source in range(4 * shards):
        y_at, zh_at, i = source // 16, source // 8 % 2, source % 8
        to_slice.append((source, (i * 2 + zh_at) * 4 + y_at))
    from_slice = [(d, s) for s, d in to_slice]
    out_got = lax.ppermute(out_weight.transpose(1, 0, 2), OWNER, to_slice)

    qkv_wide, third = qkv_got.shape[2], width // 3
    first_layout = [(0, 8 * own_rows, 0, qkv_wide, 0), (1, 8 * own_rows, 0, qkv_wide, 8 * own_rows)]
    first_layout += [
        (2, 2 * own_rows, f * third, (f + 1) * third, (16 + 2 * f) * own_rows) for f in range(3)
    ]
    out_lines = out_got.reshape(2 * own_rows, width)
    first_mine = jnp.concatenate(
        [qkv_got.reshape(16 * own_rows, qkv_wide)]
        + [
            jnp.pad(out_lines[:, f * third : (f + 1) * third], ((0, 0), (0, qkv_wide - third)))
            for f in range(3)
        ]
    )[None]
    first_block = jnp.concatenate([first_mine, cross(first_mine)], 1)
    first_near = near_of(first_block)
    qkv_image, qkv_text, out_raw = unpack(
        first_layout,
        [(width, qkv_wide), (width, qkv_wide), (16 * own_rows, width)],
        first_block,
        first_near,
        far_of(first_near),
    )
    qkv_own = (qkv_image, qkv_text)
    qkv_cols = (qkv_own, tuple(turn(w, "core", 1) for w in qkv_own))
    out_own = out_raw.reshape(8, 2, own_rows, width).transpose(1, 0, 2, 3)
    out_own = out_own.reshape(2, 8 * own_rows, width)
    out_rows = (out_own, turn(out_own, "core", 1))

    def over_slots(values):
        values = jnp.concatenate(direct_gather(values, "y"))
        for name in ("rep", "zh", "core"):
            values = jnp.concatenate([values, turn(values, name, 1)])
        return values

    all_sequences = over_slots(jnp.broadcast_to(slot_sequence, (1, 8, 128)))[:, 0, 0]
    slot_hot = (
        all_sequences[:, None] == jnp.arange(seq_total, dtype=jnp.int32)[None, :]
    ).astype(F32)
    slot_live = jnp.sum(slot_hot, 1)
    live = slot_live[0]
    cond_float = conditioning.astype(F32)
    cond_cols = lax.dynamic_slice_in_dim(
        jax.nn.silu(cond_float).astype(BF), owner_index * own_rows, own_rows, 1
    )
    slot_cond = mm(slot_hot.astype(BF), cond_cols).astype(BF)
    my_cond = slot_cond.reshape(2, 2, 2, 4, own_rows)[:, :, 0].reshape(shards, own_rows)
    mod_matrix = mod_weight.reshape(own_rows, -1)
    sums_mod = mod_parts(my_cond, mod_matrix)
    for name in ("core", "zh"):
        count = sums_mod.shape[0] // 2
        sums_mod = (
            sums_mod[:count].astype(F32) + turn(sums_mod[count:], name, 1).astype(F32)
        ).astype(BF)
    slot_mod = sum(turn(sums_mod[k], "y", k).astype(F32) for k in range(1, 4))
    slot_mod = (slot_mod + sums_mod[0].astype(F32)).astype(BF)
    all_mod = direct_gather(slot_mod, "ctx")
    modulation = (
        sum(m.astype(F32) for m in all_mod).reshape(2, 6, width)
        + mod_bias.astype(F32).reshape(2, 6, width)
    ) * live

    meta = jnp.broadcast_to(text_lengths[0, 0].astype(BF), (PAD, width))
    own_tokens = jnp.concatenate([image_tokens[0], text_tokens[0], meta])
    own_cots = jnp.concatenate([image_cotan[0], text_cotan[0], jnp.zeros((PAD, width), BF)])
    gathered = gather_ctx(jnp.concatenate([after(own_tokens, qkv_got), own_cots])).reshape(
        4, 2, rows, width
    )
    tokens_all, cots_all = gathered[:, 0], gathered[:, 1]
    lengths = tokens_all[:, rows - 1, 0].astype(jnp.int32)
    row_at = jnp.arange(rows, dtype=jnp.int32)
    is_image = row_at < image_rows
    valid_all = (
        is_image[None, :] | (row_at[None, :] - image_rows < lengths[:, None])
    ).astype(F32)
    row_mask = (
        is_image | (row_at - image_rows < text_lengths[0, 0])
    ).astype(F32)[:, None] * live

    def by_row(vectors, plus=0.0):
        return jnp.where(is_image[:, None], vectors[0] + plus, vectors[1] + plus)

    unit = down_weight.shape[0]
    wide_unit = -(-unit // 128) * 128
    lane_in, lane_out = (jnp.arange(8 * u, dtype=jnp.int32) for u in (unit, wide_unit))
    spacing = (
        (lane_in // unit * wide_unit + lane_in % unit)[:, None] == lane_out[None, :]
    ).astype(BF)
    up_wide = mm(
        after(up_weight, first_mine).transpose(1, 0, 2).reshape(16 * own_rows, 8 * unit), spacing
    ).astype(BF)
    up_send = mm_nt(
        up_wide.reshape(2 * own_rows, 8, 8, wide_unit)
        .transpose(2, 0, 1, 3)
        .reshape(16 * own_rows, 8 * wide_unit),
        spacing,
    ).astype(BF)
    up_got = from_columns(up_send.reshape(8, 2, own_rows, half_ff))
    folds = width // half_ff
    both_layout, first = [], 0
    for t in range(2):
        both_layout.append((2 * t, 8 * own_rows, 0, half_ff, first))
        first += 8 * own_rows
        for f in range(folds):
            both_layout.append((2 * t + 1, unit, f * half_ff, (f + 1) * half_ff, first))
            first += unit
    both_size = first
    both_mine = jnp.concatenate(
        [
            part
            for t in range(2)
            for part in (
                up_got[t],
                *(down_weight[:, t, f * half_ff : (f + 1) * half_ff] for f in range(folds)),
            )
        ]
    )[None]
    both_block = jnp.concatenate([both_mine, cross(after(both_mine, *first_near))], 1)
    both_near = near_of(after(both_block, qkv_image))

    def bias_part(values, start, size):
        return [
            lax.dynamic_slice_in_dim(values, start + k * size, size, 1).astype(F32)
            for k in (core, 1 - core)
        ]

    q_bias = bias_part(qv_bias, position * span, half_span)
    v_bias = bias_part(qv_bias, width + position * span, half_span)
    qkv_bias = jnp.stack(
        [
            jnp.concatenate([q, jnp.zeros_like(q), v, jnp.zeros((2, HEAD_DIM), F32)], 1)
            for q, v in zip(q_bias, v_bias)
        ]
    )[:, :, None, :]
    up_part = jnp.stack(
        [
            lax.dynamic_index_in_dim(
                up_bias.reshape(2, 8, 8, unit), k * 4 + position, 2, keepdims=False
            ).reshape(2, half_ff)
            for k in (core, 1 - core)
        ]
    ).astype(F32)[:, :, None, :]

    modulated_first, proj_own, proj_other, mixed_own, mixed_other = attend(
        image_rows, lengths, tokens_all, modulation, qkv_cols, qkv_bias
    )
    projs, mixed = (proj_own, proj_other), (mixed_own, mixed_other)
    attn_got = scatter_ctx(attend_out(image_rows, mixed, out_rows))

    scalars = (text_lengths.reshape(1), live.reshape(1))
    flat, halved = ((rows, width), BF), ((rows, width), F32)
    out_line, down_line = out_bias.astype(F32), down_bias.astype(F32)
    base = (attn_got, own_tokens, modulation, out_line)
    (modulated_two,) = rows_call(rows_one_kernel, image_rows, "rows_one", [flat], (), base)
    both_near = all_after(both_near, modulated_two)
    up_image, down_image, up_text, down_text = unpack(
        both_layout,
        [(width, half_ff), (half_ff, width)] * 2,
        both_block,
        both_near,
        far_of(both_near),
    )
    up_cols = [(w, turn(w, "core", 1)) for w in (up_image, up_text)]
    down_rows = [(w, turn(w, "core", 1)) for w in (down_image, down_text)]

    seconds = gather_ctx(modulated_two)
    branch_grads = (
        cots_all.astype(F32) * (valid_all * live)[:, :, None] * by_row(modulation[:, 5])
    ).astype(BF)
    second_parts, down_parts, both_grads, up_sums = mlp(
        image_rows, seconds, branch_grads, up_cols, down_rows, up_part
    )

    def block_total(mine):
        total, more = pair_sum(mine.reshape(1, 2, mine.shape[1] // 2, -1), 1)
        return (total.astype(F32) + more.astype(F32)).astype(BF)

    def to_columns(total):
        total = total.reshape(2, 8, own_rows, -1).transpose(1, 0, 2, 3)
        return lax.all_to_all(total, TP, split_axis=0, concat_axis=0, tiled=True)

    both_owns = [both_grads[k] for k in (0, 2, 4, 6)]
    both_gots = [turn(both_grads[k], "core", 1) for k in (1, 3, 5, 7)]
    second_got = scatter_ctx(second_parts)
    grad_attn, grad_middle, sums_two = rows_call(
        rows_two_kernel,
        image_rows,
        "rows_two",
        [flat, halved, ((2, 4, width), F32)],
        scalars,
        (*base, own_cots, second_got),
    )
    attn_grads = gather_ctx(grad_attn)
    both_gots[0] = after(both_gots[0], grad_attn)
    both_sums = sum_blocks(both_layout, both_size, half_ff, both_owns, both_gots, "sum_both")
    both_got = scatter_near(both_sums[2], both_sums[3])

    branch_got = scatter_ctx(after(down_parts, attn_grads))
    image_out, text_out, sums_three = rows_call(
        rows_three_kernel,
        image_rows,
        "rows_three",
        [
            (image_tokens.shape, BF),
            (text_tokens.shape, BF),
            ((2, 2, width), F32),
        ],
        scalars,
        (*base, own_cots, branch_got, down_line),
    )

    proj_grads = attend_back(image_rows, lengths, attn_grads, projs, out_rows)
    both_sent = scatter_add(both_sums[1], both_sums[4], all_after(both_got, proj_grads[0]))
    first_parts, first_sums, proj_sums = attend_rows(
        image_rows, tokens_all, all_after(proj_grads, branch_got, *both_sent), qkv_cols
    )
    first_got = scatter_ctx(first_parts)
    *d_qkv, d_out_own, d_out_other = attend_weights(
        image_rows, modulated_first, all_after(proj_grads, first_parts), mixed, attn_grads
    )

    def out_lines_of(values):
        return values.reshape(2, 8, own_rows, width).transpose(1, 0, 2, 3).reshape(-1, width)

    first_gots = [turn(v, "core", 1) for v in (d_qkv[2], d_qkv[3], out_lines_of(d_out_other))]
    first_blocks = sum_blocks(
        first_layout,
        first_mine.shape[1],
        qkv_wide,
        [d_qkv[0], d_qkv[1], out_lines_of(d_out_own)],
        first_gots,
        "sum_first",
    )
    first_sent = scatter_add(
        first_blocks[1], first_blocks[4], scatter_near(first_blocks[2], first_blocks[3])
    )
    both_total = block_total(scatter_last(both_sums[0], both_sent, first_blocks))
    both_total = after(both_total, *first_sent)[0]
    sizes = [8 * own_rows] + [unit] * folds
    marks = [0]
    for n in 2 * sizes:
        marks.append(marks[-1] + n)
    parts = [both_total[a:b] for a, b in zip(marks[:-1], marks[1:])]
    up_total = to_columns(jnp.stack([parts[0], parts[1 + folds]]))
    down_total = jnp.stack(
        [jnp.concatenate(parts[1 + o : 1 + o + folds], axis=1) for o in (0, 1 + folds)], axis=1
    )
    first_total = block_total(scatter_last(first_blocks[0], first_sent))[0]
    qkv_total = to_columns(first_total[: 16 * own_rows].reshape(2, 8 * own_rows, qkv_wide))
    out_total = jnp.concatenate(
        [
            first_total[(16 + 2 * f) * own_rows : (18 + 2 * f) * own_rows, :third]
            for f in range(3)
        ],
        axis=1,
    ).reshape(2, own_rows, width)

    qkv_total = qkv_total.astype(F32).reshape(2, 4, 2, own_rows, -1)
    qkv_grad = (
        jnp.stack(
            [
                qkv_total[..., : cuts[1]],
                jnp.concatenate(
                    [qkv_total[..., cuts[1] + HEAD_DIM : cuts[2]], qkv_total[..., cuts[1] : cuts[1] + HEAD_DIM]],
                    -1,
                ),
                qkv_total[..., cuts[2] : cuts[3]],
            ],
            axis=4,
        )
        .transpose(3, 2, 4, 1, 0, 5)
        .reshape(qkv_weight.shape)
    )
    up_wide = mm(up_total.reshape(16 * own_rows, 8 * unit), spacing).astype(BF)
    up_grad = (
        mm_nt(
            up_wide.reshape(8, 2 * own_rows, 8, wide_unit)
            .transpose(1, 2, 0, 3)
            .reshape(16 * own_rows, 8 * wide_unit),
            spacing,
        )
        .reshape(2, own_rows, ff)
        .transpose(1, 0, 2)
    )
    down_grad = down_total.astype(F32)
    out_grad = lax.ppermute(out_total, OWNER, from_slice).astype(F32).transpose(1, 0, 2)

    image_grad, text_grad = rows_call(
        rows_four_kernel,
        image_rows,
        "rows_four",
        [(image_tokens.shape, F32), (text_tokens.shape, F32)],
        (),
        (own_tokens, modulation, first_got, grad_middle),
    )

    vectors = jnp.concatenate(
        [
            jnp.concatenate([first_sums, sums_two[:, :3], sums_three[:, :1]], axis=1).reshape(-1),
            sums_two[:, 3].reshape(-1),
            sums_three[:, 1].reshape(-1),
        ]
    )

    def in_order(mine, other):
        return jnp.where(
            core == 0, jnp.concatenate([mine, other], -1), jnp.concatenate([other, mine], -1)
        )

    q_sums, v_sums = (
        in_order(*(proj_sums[h, :, 0, a * half_span : (a + 1) * half_span] for h in range(2)))
        for a in (0, 2)
    )
    heads = jnp.stack([q_sums, v_sums], 1).reshape(-1)
    message = jnp.concatenate([vectors, heads]).reshape(-1, 128)
    messages = direct_gather(after(message, *first_blocks), "ctx")
    vectors = sum(m[: vectors.shape[0] // 128] for m in messages).reshape(-1)
    heads = jnp.stack([m[vectors.shape[0] // 128 :] for m in messages])
    heads = jnp.roll(heads.reshape(4, 2, 2, span), position, axis=0).transpose(1, 2, 0, 3)
    own_vector = jnp.concatenate([v.reshape(-1) for v in (vectors, heads, up_sums)])
    own_vector = (own_vector * live).astype(BF).reshape(1, -1, 128)
    everything = lax.optimization_barrier(over_slots(after(own_vector, *first_sent)))
    mod_weight_grad, slot_grads, totals = mod_last(everything, slot_cond, mod_matrix)
    mod_weight_grad = mod_weight_grad.reshape(mod_weight.shape)
    up_lines = 2 * half_ff // 128
    here_up = jnp.sum(everything[:shards, -2 * up_lines : -up_lines].astype(F32), 0) + jnp.sum(
        everything[shards:, -up_lines:].astype(F32), 0
    )
    totals = totals.reshape(-1)
    mod_size, wide = 12 * width, 2 * width

    def owner_slice(values):
        part = values.shape[1] // (4 * shards)
        return lax.dynamic_slice_in_dim(values, owner_index * part, part, 1)

    mod_bias_grad = owner_slice(totals[:mod_size].reshape(2, -1))
    out_bias_grad = owner_slice(totals[mod_size : mod_size + wide].reshape(2, -1))
    down_bias_grad = owner_slice(totals[mod_size + wide : mod_size + 2 * wide].reshape(2, -1))
    qv_bias_grad = owner_slice(totals[mod_size + 2 * wide : mod_size + 4 * wide].reshape(2, -1))
    up_bias_grad = lax.dynamic_index_in_dim(
        here_up.reshape(2, 8, unit), y * 2 + zh, 1, keepdims=False
    )
    grad_cond_cols = lax.dot_general(
        slot_hot, slot_grads, (((0,), (0,)), ((), ())), precision=lax.Precision.HIGHEST
    )
    cond_part = lax.dynamic_slice_in_dim(cond_float, owner_index * own_rows, own_rows, 1)
    cond_grad = jax.vjp(jax.nn.silu, cond_part)[1](grad_cond_cols)[0]
    return (
        image_out,
        text_out,
        image_grad,
        text_grad,
        cond_grad,
        mod_weight_grad,
        mod_bias_grad,
        qkv_grad,
        qv_bias_grad,
        out_grad,
        out_bias_grad,
        up_grad,
        up_bias_grad,
        down_grad,
        down_bias_grad,
    )


def solution(mesh):
    fine = Mesh(mesh.devices.reshape(2, 4, 2, 2, 4), EVERY)
    rows = P(SLOT, "ctx", None)
    owned = P(OWNER, None, None)
    columns = P(None, OWNER)
    return jax.shard_map(
        per_device,
        mesh=fine,
        in_specs=(
            rows,
            rows,
            P(SLOT, "ctx"),
            P(SLOT),
            P(),
            owned,
            P(),
            owned,
            P(),
            owned,
            P(),
            owned,
            P(),
            owned,
            P(),
            rows,
            rows,
        ),
        out_specs=(
            rows,
            rows,
            rows,
            rows,
            columns,
            owned,
            columns,
            owned,
            columns,
            owned,
            columns,
            owned,
            columns,
            owned,
            columns,
        ),
        check_vma=False,
    )
```

```python
import functools

import jax
import jax.numpy as jnp
from jax import lax
from jax.experimental import pallas as pl
from jax.experimental.pallas import tpu as pltpu
from jax.sharding import Mesh, PartitionSpec as P

HEAD_DIM = 64
SHARD = ("y", "zh", "core")
TP = ("core", "ctx")
OWNER = ("y", "zh", "core", "ctx")
SLOT = ("rep", "y", "zh", "core")
EVERY = ("rep", "y", "zh", "core", "ctx")
BF = jnp.bfloat16
F32 = jnp.float32


def norm_rows(values):
    center = values - jnp.mean(values, axis=-1, keepdims=True)
    inv_scale = lax.rsqrt(jnp.mean(center * center, axis=-1, keepdims=True) + 1e-06)
    return (center * inv_scale, inv_scale)


def norm_back(grad_out, normed, inv_scale):
    return inv_scale * (
        grad_out
        - jnp.mean(grad_out, axis=-1, keepdims=True)
        - normed * jnp.mean(grad_out * normed, axis=-1, keepdims=True)
    )


def mm(left, right):
    return jnp.dot(left, right, preferred_element_type=F32)


def mm_nt(left, right):
    return lax.dot_general(left, right, (((1,), (1,)), ((), ())), preferred_element_type=F32)


def mm_tn(left, right):
    return lax.dot_general(left, right, (((0,), (0,)), ((), ())), preferred_element_type=F32)


GELU_A = 0.7978845608028654
GELU_B = 0.044715
PAD = 8


def gelu_both(values):
    square = values * values
    bent = jnp.tanh(values * (GELU_A + GELU_A * GELU_B * square))
    half_up = 0.5 + 0.5 * bent
    slope = GELU_A + 3.0 * GELU_A * GELU_B * square
    return values * half_up, half_up + 0.5 * values * (1.0 - bent * bent) * slope


def mlp_kernel(image_rows, second_in, grad_in, *refs):
    weights, bias, outs = refs[:8], refs[8], refs[9:]
    second_out, down_out, weight_grads, bias_sums = outs[0], outs[1], outs[2:10], outs[10]
    turned, second_total, down_total = outs[11:]
    stream, chunk = pl.program_id(0), pl.program_id(1)
    last = pl.num_programs(1) - 1
    blocks, rows, width = second_in.shape

    def work(low, count, t):
        total = blocks * count
        left = second_in[:, low : low + count, :].reshape(total, width)
        grad = grad_in[:, low : low + count, :].reshape(total, width)

        @pl.when(chunk == 0)
        def _():
            turned[:, :total] = left.T
            second_total[:total, :] = jnp.zeros((total, width), F32)
            down_total[:total, :] = jnp.zeros((total, width), F32)

        seconds = forwards = None
        for h in range(2):
            up, down = weights[4 * t + h], weights[4 * t + 2 + h]
            hidden = mm(left, up[...]) + bias[h, 0]
            active, slope = gelu_both(hidden)
            active = active.astype(BF)
            grad_hidden = (slope * mm_nt(grad, down[...])).astype(BF)
            second = mm_nt(grad_hidden, up[...])
            forward = mm(active, down[...])
            if h == 0:
                seconds, forwards = second, forward
            else:
                second_total[:total, :] += seconds + second
                down_total[:total, :] += forwards + forward
            weight_grads[4 * t + h][...] = mm(turned[:, :total], grad_hidden).astype(BF)
            weight_grads[4 * t + 2 + h][...] = mm_tn(active, grad).astype(BF)
            bias_sums[h, 0] = jnp.sum(grad_hidden.astype(F32), axis=0, keepdims=True)

        @pl.when(chunk == last)
        def _():
            second_out[:, low : low + count, :] = (
                second_total[:total, :].astype(BF).reshape(blocks, count, width)
            )
            down_out[:, low : low + count, :] = (
                down_total[:total, :].astype(BF).reshape(blocks, count, width)
            )

    @pl.when(stream == 0)
    def _():
        work(0, image_rows, 0)

    @pl.when(stream == 1)
    def _():
        work(image_rows, rows - image_rows, 1)


def cost(microseconds):
    return pl.CostEstimate(
        flops=int(microseconds * 1e9), bytes_accessed=int(microseconds * 1e6), transcendentals=0
    )


def mlp(image_rows, seconds, grads, ups, downs, bias):
    blocks, rows, width = seconds.shape
    hidden = ups[0][0].shape[1]
    chunk = min(256, hidden)
    last = hidden // chunk - 1
    whole = pl.BlockSpec((blocks, rows, width), lambda t, c: (0, 0, 0))
    at = [lambda t, c: jnp.where(t == 0, c, last), lambda t, c: jnp.where(t == 1, c, 0)]
    columns = [pl.BlockSpec((width, chunk), lambda t, c, f=f: (0, f(t, c))) for f in at]
    lines = [pl.BlockSpec((chunk, width), lambda t, c, f=f: (f(t, c), 0)) for f in at]
    line = pl.BlockSpec((2, 1, 1, chunk), lambda t, c: (0, t, 0, c))
    image_all = blocks * image_rows
    like = jax.ShapeDtypeStruct
    weights = [w for t in range(2) for w in (*ups[t], *downs[t])]
    specs = [v for t in range(2) for v in (columns[t], columns[t], lines[t], lines[t])]
    outs = pl.pallas_call(
        functools.partial(mlp_kernel, image_rows),
        grid=(2, hidden // chunk),
        in_specs=[whole, whole, *specs, line],
        out_specs=[whole, whole, *specs, line],
        out_shape=[
            like(seconds.shape, BF),
            like(seconds.shape, BF),
            *(like(w.shape, BF) for w in weights),
            like(bias.shape, F32),
        ],
        scratch_shapes=[
            pltpu.VMEM((width, image_all), BF),
            pltpu.VMEM((image_all, width), F32),
            pltpu.VMEM((image_all, width), F32),
        ],
        compiler_params=pltpu.CompilerParams(
            dimension_semantics=("arbitrary", "arbitrary"), vmem_limit_bytes=48 << 20
        ),
        cost_estimate=cost(33),
        name="feed_forward",
    )(seconds, grads, *weights, bias)
    return outs[0], outs[1], outs[2:10], outs[10]


def turn(values, axis, step):
    count = lax.axis_size(axis)
    return lax.ppermute(values, axis, [(i, (i + step) % count) for i in range(count)])


def cross(values):
    return lax.ppermute(values, ("rep", "zh"), [(0, 3), (3, 0), (1, 2), (2, 1)])


def after(values, *others):
    return lax.optimization_barrier((values, *others))[0]


def sync(*values):
    return lax.optimization_barrier(values)


def all_after(values, *others):
    return lax.optimization_barrier((tuple(values), *others))[0]


def cut(values, axis, low, high):
    return lax.slice_in_dim(values, low, high, axis=axis)


def scatter_near(top, bottom):
    return turn(top, "y", 1), turn(bottom, "y", -1)


def scatter_add(ahead, behind, got):
    half = got[0].shape[1]
    size = ahead.shape[1]
    to_ahead = jnp.concatenate([cut(ahead, 1, 0, half) + got[0], cut(ahead, 1, half, size)], 1)
    to_behind = jnp.concatenate([cut(behind, 1, 0, half), cut(behind, 1, half, size) + got[1]], 1)
    return to_ahead, to_behind


def scatter_far(sent):
    return turn(sent[0], "y", 1), turn(sent[1], "y", -1)


def add_three(mine, got):
    return (mine.astype(F32) + got[0].astype(F32) + got[1].astype(F32)).astype(BF)


def add_two(left, right):
    return (left.astype(F32) + right.astype(F32)).astype(BF)


def direct_gather(block, axis):
    return [block] + [turn(block, axis, -k) for k in range(1, lax.axis_size(axis))]


def zones(both):
    both = both.reshape(2, both.shape[1] // 2, both.shape[2])
    zh = lax.axis_index("zh")
    return tuple(lax.dynamic_index_in_dim(both, k, 0, keepdims=False) for k in (zh, 1 - zh))


def gather_ctx(block):
    gathered = lax.all_gather(block, "ctx", axis=0, tiled=True)
    return gathered.reshape((4,) + block.shape)


def scatter_ctx(blocks):
    flat = blocks.reshape(-1, blocks.shape[-1])
    return lax.psum_scatter(flat, "ctx", scatter_dimension=0, tiled=True)


def spread_mask(width, high):
    lane = lax.broadcasted_iota(jnp.int32, (1, width), 1)
    return ((lane >= HEAD_DIM) if high else (lane < HEAD_DIM)).astype(F32)


def key_bias_row(lengths, blocks, rows, image_rows):
    lane = lax.broadcasted_iota(jnp.int32, (1, blocks * rows), 1)
    bias = jnp.zeros((1, blocks * rows), F32)
    for c in range(blocks):
        first = c * rows + image_rows + lengths[c]
        bias = jnp.where((lane >= first) & (lane < (c + 1) * rows), -1000000000.0, bias)
    return bias


def softmax_rows(query, keys, bias):
    scores = mm_nt(query, keys) + bias
    grown = jnp.exp(scores - jnp.max(scores, axis=-1, keepdims=True))
    return grown * (1.0 / jnp.sum(grown, axis=-1, keepdims=True))


def lane_tile(ref, at, width=128):
    return ref[:, :, at : at + width].reshape(ref.shape[0] * ref.shape[1], width)


def attend_heads(image_rows, lengths, modulated, weights, bias_row, proj, mixed):
    blocks, rows, width = modulated.shape
    for t, (low, high) in enumerate(((0, image_rows), (image_rows, rows))):
        left = modulated[:, low:high, :].reshape(-1, width)
        values = (mm(left, weights[t][...]) + bias_row[t]).astype(BF)
        proj[:, low:high, :] = values.reshape(blocks, high - low, -1)
    bias = key_bias_row(lengths, blocks, rows, image_rows)
    low_mask, high_mask = (spread_mask(128, high) for high in (False, True))
    lower = low_mask > 0.5
    masks = (low_mask * 0.125, high_mask * 0.125)

    @pl.loop(0, blocks)
    def _(c):
        pair_query = proj[c, :, 0:128].astype(F32)
        pair_keys, pair_values = (lane_tile(proj, 256), lane_tile(proj, 384))
        pair_out = [
            mm(softmax_rows((pair_query * m).astype(BF), pair_keys, bias).astype(BF), pair_values)
            for m in masks
        ]
        mixed[c, :, 0:128] = jnp.where(lower, pair_out[0], pair_out[1]).astype(BF)
        last_query = pltpu.roll(proj[c, :, 128:256].astype(F32), HEAD_DIM, 1) * masks[1]
        weights = softmax_rows(last_query.astype(BF), lane_tile(proj, 128), bias).astype(BF)
        mixed[c, :, 128:192] = mm(weights, lane_tile(proj, 512))[:, :HEAD_DIM].astype(BF)


def attend_kernel(image_rows, lengths, tokens, mods, image, text, bias, modulated, proj, mixed):
    blocks, rows = modulated.shape[:2]

    @pl.loop(0, blocks)
    def _(c):
        for t, (low, high) in enumerate(((0, image_rows), (image_rows, rows))):
            normed, _ = norm_rows(tokens[c, 0, low:high, :].astype(F32))
            modulated[c, low:high, :] = (
                normed * (1.0 + mods[t, 1:2, :]) + mods[t, 0:1, :]
            ).astype(BF)

    attend_heads(image_rows, lengths, modulated, (image, text), bias, proj, mixed)


def attend_other_kernel(image_rows, lengths, modulated, image, text, bias, proj, mixed):
    attend_heads(image_rows, lengths, modulated, (image, text), bias, proj, mixed)


def attend_out_kernel(
    image_rows, mixed_own, mixed_other, out_own, out_other, partial
):
    blocks, rows, width = partial.shape
    streams = ((0, image_rows), (image_rows, rows))
    for t, (low, high) in enumerate(streams):
        total = None
        for mixed, weight in ((mixed_own, out_own), (mixed_other, out_other)):
            left = mixed[:, low:high, :].reshape(blocks * (high - low), -1)
            term = mm(left, weight[t])
            total = term if total is None else total + term
        partial[:, low:high, :] = total.astype(BF).reshape(blocks, high - low, width)


def attend(image_rows, lengths, tokens, mods, weights, bias):
    blocks, _, rows, width = tokens.shape
    wide, deep = weights[0].shape[1], 3 * HEAD_DIM
    like = jax.ShapeDtypeStruct
    whole = pl.BlockSpec(memory_space=pltpu.VMEM)
    return pl.pallas_call(
        functools.partial(attend_kernel, image_rows),
        in_specs=[pl.BlockSpec(memory_space=pltpu.SMEM)] + [whole] * 5,
        out_specs=[whole] * 3,
        out_shape=[
            like((blocks, rows, width), BF),
            like((blocks, rows, wide), BF),
            like((blocks, rows, deep), BF),
        ],
        compiler_params=pltpu.CompilerParams(vmem_limit_bytes=24 << 20),
        cost_estimate=cost(10),
        name="attend",
    )(lengths, tokens, mods, *weights, bias)


def attend_other(image_rows, lengths, modulated, weights, bias):
    blocks, rows, _ = modulated.shape
    wide, deep = weights[0].shape[1], 3 * HEAD_DIM
    like = jax.ShapeDtypeStruct
    whole = pl.BlockSpec(memory_space=pltpu.VMEM)
    return pl.pallas_call(
        functools.partial(attend_other_kernel, image_rows),
        in_specs=[pl.BlockSpec(memory_space=pltpu.SMEM)] + [whole] * 4,
        out_specs=[whole] * 2,
        out_shape=[like((blocks, rows, wide), BF), like((blocks, rows, deep), BF)],
        compiler_params=pltpu.CompilerParams(vmem_limit_bytes=20 << 20),
        cost_estimate=cost(8),
        name="attend_other",
    )(lengths, modulated, *weights, bias)


def attend_out(image_rows, mixed, out_rows):
    blocks, rows, deep = mixed[0].shape
    width = out_rows[0].shape[2]
    whole = pl.BlockSpec(memory_space=pltpu.VMEM)
    return pl.pallas_call(
        functools.partial(attend_out_kernel, image_rows),
        in_specs=[whole] * 4,
        out_specs=whole,
        out_shape=jax.ShapeDtypeStruct((blocks, rows, width), BF),
        compiler_params=pltpu.CompilerParams(vmem_limit_bytes=12 << 20),
        cost_estimate=cost(4),
        name="attend_out",
    )(*mixed, *out_rows)


def mod_kernel(conds, weights, out):
    for tile in range(out.shape[1]):
        out[:, tile, :] = mm(conds[...], weights[:, tile * 128 : (tile + 1) * 128]).astype(BF)


def mod_parts(conds, weights):
    slots, width = conds.shape[0], weights.shape[1]
    whole = pl.BlockSpec(memory_space=pltpu.VMEM)
    return pl.pallas_call(
        mod_kernel,
        in_specs=[whole] * 2,
        out_specs=whole,
        out_shape=jax.ShapeDtypeStruct((slots, width // 128, 128), BF),
        compiler_params=pltpu.CompilerParams(vmem_limit_bytes=8 << 20),
        cost_estimate=cost(1.5),
        name="mod_parts",
    )(conds, weights)


def attend_back_kernel(
    image_rows,
    lengths,
    grads,
    proj_own,
    proj_other,
    out_own,
    out_other,
    grad_own,
    grad_other,
    grad_mixed,
    pair_key,
    pair_value,
    last_query,
    last_key,
    last_value,
):
    blocks, rows, width = grads.shape
    total_rows = blocks * rows
    streams = ((0, image_rows), (image_rows, rows))
    bias = key_bias_row(lengths, blocks, rows, image_rows)
    low_mask, high_mask = (spread_mask(128, high) for high in (False, True))
    lower = low_mask > 0.5
    masks = (low_mask * 0.125, high_mask * 0.125)
    halves = ((proj_own, out_own, grad_own), (proj_other, out_other, grad_other))
    grad_mixed[...] = jnp.zeros(grad_mixed.shape, BF)
    for proj, out, grad in halves:
        for t, (low, high) in enumerate(streams):
            right = grads[:, low:high, :].reshape(-1, width)
            grad_mixed[:, low:high, 0:192] = (
                mm_nt(right, out[t]).astype(BF).reshape(blocks, high - low, -1)
            )
        for total in (pair_key, pair_value, last_key, last_value):
            total[...] = jnp.zeros(total.shape, F32)

        @pl.loop(0, blocks)
        def _(c):
            pair_query = proj[c, :, 0:128].astype(F32)
            pair_grad = grad_mixed[c, :, 0:128].astype(F32)
            pair_keys, pair_values = (lane_tile(proj, 256), lane_tile(proj, 384))
            query_grads = []
            for mask, scaled in zip((low_mask, high_mask), masks):
                query, back = (pair_query * scaled).astype(BF), (pair_grad * mask).astype(BF)
                probs = softmax_rows(query, pair_keys, bias)
                grad_probs = mm_nt(back, pair_values)
                delta = jnp.sum(probs * grad_probs, axis=-1, keepdims=True)
                grad_scores = (probs * (grad_probs - delta)).astype(BF)
                query_grads.append(mm(grad_scores, pair_keys))
                pair_key[...] += mm_tn(grad_scores, query)
                pair_value[...] += mm_tn(probs.astype(BF), back)
            grad[c, :, 0:128] = (
                jnp.where(lower, query_grads[0], query_grads[1]) * 0.125
            ).astype(BF)
            keys = lane_tile(proj, 128)
            query = (pltpu.roll(proj[c, :, 128:256].astype(F32), HEAD_DIM, 1) * masks[1]).astype(BF)
            back = grad_mixed[c, :, 128:256]
            probs = softmax_rows(query, keys, bias)
            grad_probs = mm_nt(back, lane_tile(proj, 512))
            delta = jnp.sum(probs * grad_probs, axis=-1, keepdims=True)
            grad_scores = (probs * (grad_probs - delta)).astype(BF)
            last_query[c] = pltpu.roll(mm(grad_scores, keys), HEAD_DIM, 1) * 0.125
            last_key[...] += mm_tn(grad_scores, query)
            last_value[...] += mm_tn(probs.astype(BF), back)

        shape = (blocks, rows, 128)
        grad[:, :, 128:256] = (
            jnp.where(lower, last_query[...].reshape(total_rows, 128), last_key[...])
            .astype(BF)
            .reshape(shape)
        )
        grad[:, :, 256:384] = pair_key[...].astype(BF).reshape(shape)
        grad[:, :, 384:512] = pair_value[...].astype(BF).reshape(shape)
        grad[:, :, 512:640] = last_value[...].astype(BF).reshape(shape)


def attend_rows_kernel(
    image_rows,
    tokens,
    grad_own,
    grad_other,
    own_image,
    own_text,
    other_image,
    other_text,
    partial,
    row_sums,
    proj_sums,
):
    blocks, rows, width = partial.shape
    streams = ((0, image_rows), (image_rows, rows))
    for t, (low, high) in enumerate(streams):
        count = high - low
        rights = [g[:, low:high, :].reshape(blocks * count, -1) for g in (grad_own, grad_other)]
        for h, right in enumerate(rights):
            proj_sums[h, t] = jnp.sum(right.astype(F32), axis=0, keepdims=True)
        own, other = ((own_image, other_image), (own_text, other_text))[t]
        total = mm_nt(rights[0], own[...]) + mm_nt(rights[1], other[...])
        partial[:, low:high, :] = total.astype(BF).reshape(blocks, count, width)
        row_sums[t, 0:1, :] = jnp.sum(total, axis=0, keepdims=True)
        row_sums[t, 1:2, :] = jnp.zeros((1, width), F32)

    @pl.loop(0, blocks)
    def _(c):
        for t, (low, high) in enumerate(streams):
            normed, _ = norm_rows(tokens[c, 0, low:high, :].astype(F32))
            row_sums[t, 1:2, :] += jnp.sum(
                normed * partial[c, low:high, :].astype(F32), axis=0, keepdims=True
            )


def attend_back(image_rows, lengths, grads, projs, out_rows):
    blocks, rows, width = grads.shape
    deep = out_rows[0].shape[1]
    total = blocks * rows
    like = jax.ShapeDtypeStruct
    whole = pl.BlockSpec(memory_space=pltpu.VMEM)
    return pl.pallas_call(
        functools.partial(attend_back_kernel, image_rows),
        in_specs=[pl.BlockSpec(memory_space=pltpu.SMEM)] + [whole] * 5,
        out_specs=[whole] * 2,
        out_shape=[like(projs[0].shape, BF), like(projs[0].shape, BF)],
        scratch_shapes=[
            pltpu.VMEM((blocks, rows, 256), BF),
            pltpu.VMEM((total, 128), F32),
            pltpu.VMEM((total, 128), F32),
            pltpu.VMEM((blocks, rows, 128), F32),
            pltpu.VMEM((total, 128), F32),
            pltpu.VMEM((total, 128), F32),
        ],
        compiler_params=pltpu.CompilerParams(vmem_limit_bytes=22 << 20),
        cost_estimate=cost(20),
        name="attend_back",
    )(lengths, grads, *projs, *out_rows)


def attend_rows(image_rows, tokens, proj_grads, qkv_cols):
    blocks, _, rows, width = tokens.shape
    wide = qkv_cols[0][0].shape[1]
    like = jax.ShapeDtypeStruct
    whole = pl.BlockSpec(memory_space=pltpu.VMEM)
    return pl.pallas_call(
        functools.partial(attend_rows_kernel, image_rows),
        in_specs=[whole] * 7,
        out_specs=[whole] * 3,
        out_shape=[
            like((blocks, rows, width), BF),
            like((2, 2, width), F32),
            like((2, 2, 1, wide), F32),
        ],
        compiler_params=pltpu.CompilerParams(vmem_limit_bytes=22 << 20),
        cost_estimate=cost(8),
        name="attend_rows",
    )(tokens, *proj_grads, *qkv_cols[0], *qkv_cols[1])


def attend_weights_kernel(
    image_rows,
    modulated,
    grad_own,
    grad_other,
    mixed_own,
    mixed_other,
    grads,
    own_image,
    own_text,
    other_image,
    other_text,
    d_out_own,
    d_out_other,
):
    blocks, rows, width = modulated.shape
    kept = []
    for t, (low, high) in enumerate(((0, image_rows), (image_rows, rows))):
        left = modulated[:, low:high, :].reshape(-1, width)
        right = grads[:, low:high, :].reshape(-1, width)
        turned = left.T
        sides = ((own_image, other_image), (own_text, other_text))[t]
        for grad, d_qkv in zip((grad_own, grad_other), sides):
            values = grad[:, low:high, :].reshape(blocks * (high - low), -1)
            d_qkv[...] = mm(turned, values).astype(BF)
        for mixed, d_out in ((mixed_own, d_out_own), (mixed_other, d_out_other)):
            values = mixed[:, low:high, :].reshape(blocks * (high - low), -1)
            value = mm_tn(values, right).reshape(8, -1, width)
            if t == 0:
                kept.append(value)
            else:
                both = jnp.concatenate([kept.pop(0), value], axis=1)
                d_out[...] = both.reshape(d_out.shape).astype(BF)


def attend_weights(image_rows, modulated, proj_grads, mixed, grads):
    blocks, rows, width = modulated.shape
    wide, deep = proj_grads[0].shape[2], mixed[0].shape[2]
    like = jax.ShapeDtypeStruct
    whole = pl.BlockSpec(memory_space=pltpu.VMEM)
    return pl.pallas_call(
        functools.partial(attend_weights_kernel, image_rows),
        in_specs=[whole] * 6,
        out_specs=[whole] * 6,
        out_shape=[
            *(like((width, wide), BF) for _ in range(4)),
            like((2 * deep, width), BF),
            like((2 * deep, width), BF),
        ],
        compiler_params=pltpu.CompilerParams(vmem_limit_bytes=28 << 20),
        cost_estimate=cost(9),
        name="attend_weights",
    )(modulated, *proj_grads, *mixed, grads)


def rows_one_kernel(image_rows, got, tokens, mods, out_bias, second):
    for t, (low, high) in enumerate(((0, image_rows), (image_rows, got.shape[0]))):
        attn = got[low:high, :].astype(F32) + out_bias[t : t + 1, :]
        normed, _ = norm_rows(tokens[low:high, :].astype(F32) + mods[t, 2:3, :] * attn)
        second[low:high, :] = (normed * (1.0 + mods[t, 4:5, :]) + mods[t, 3:4, :]).astype(BF)


def masked(cots, t, length, live):
    row = lax.broadcasted_iota(jnp.int32, cots.shape, 0)
    keep = live if t == 0 else jnp.where(row < length, live, 0.0)
    return cots.astype(F32) * keep


def rows_two_kernel(
    image_rows, length, live, got, tokens, mods, out_bias, cots, back, grad_attn, grad_middle, sums
):
    for t, (low, high) in enumerate(((0, image_rows), (image_rows, got.shape[0]))):
        attn = got[low:high, :].astype(F32) + out_bias[t : t + 1, :]
        normed, inv = norm_rows(tokens[low:high, :].astype(F32) + mods[t, 2:3, :] * attn)
        grad_two = back[low:high, :].astype(F32)
        middle = masked(cots[low:high, :], t, length[0], live[0]) + norm_back(
            grad_two * (1.0 + mods[t, 4:5, :]), normed, inv
        )
        grad_middle[low:high, :] = middle
        grad = (middle * mods[t, 2:3, :]).astype(BF)
        grad_attn[low:high, :] = grad
        terms = (middle * attn, grad_two, grad_two * normed, grad.astype(F32))
        for k, term in enumerate(terms):
            sums[t, k : k + 1, :] = jnp.sum(term, axis=0, keepdims=True)


def rows_three_kernel(
    image_rows,
    length,
    live,
    got,
    tokens,
    mods,
    out_bias,
    cots,
    branch_got,
    down_bias,
    image_out,
    text_out,
    sums,
):
    for t, (low, high) in enumerate(((0, image_rows), (image_rows, got.shape[0]))):
        attn = got[low:high, :].astype(F32) + out_bias[t : t + 1, :]
        middle = tokens[low:high, :].astype(F32) + mods[t, 2:3, :] * attn
        branch = branch_got[low:high, :].astype(F32) + down_bias[t : t + 1, :]
        grad = masked(cots[low:high, :], t, length[0], live[0])
        keep = masked(jnp.ones(grad.shape, F32), t, length[0], live[0])
        out = ((middle + mods[t, 5:6, :] * branch) * keep).astype(BF)
        target = (image_out, text_out)[t]
        target[0] = out[: target.shape[1], :]
        back = (grad * mods[t, 5:6, :]).astype(BF).astype(F32)
        for k, term in enumerate((grad * branch, back)):
            sums[t, k : k + 1, :] = jnp.sum(term, axis=0, keepdims=True)


def rows_four_kernel(image_rows, tokens, mods, back, grad_middle, image_grad, text_grad):
    for t, (low, high) in enumerate(((0, image_rows), (image_rows, tokens.shape[0]))):
        normed, inv = norm_rows(tokens[low:high, :].astype(F32))
        grad = grad_middle[low:high, :] + norm_back(
            back[low:high, :].astype(F32) * (1.0 + mods[t, 1:2, :]), normed, inv
        )
        target = (image_grad, text_grad)[t]
        target[0] = grad[: target.shape[1], :]


def rows_call(kernel, image_rows, name, outs, scalars, arrays):
    whole = pl.BlockSpec(memory_space=pltpu.VMEM)
    return pl.pallas_call(
        functools.partial(kernel, image_rows),
        in_specs=[pl.BlockSpec(memory_space=pltpu.SMEM)] * len(scalars) + [whole] * len(arrays),
        out_specs=[whole] * len(outs),
        out_shape=[jax.ShapeDtypeStruct(shape, dtype) for shape, dtype in outs],
        compiler_params=pltpu.CompilerParams(vmem_limit_bytes=16 << 20),
        cost_estimate=cost(2),
        name=name,
    )(*scalars, *arrays)


def unpack_kernel(layout, spots, y, zh, *refs):
    pieces, outs = refs[:5], refs[5:]
    for piece, (shift, halves) in zip(pieces, spots):
        for half, base in halves:
            spot = lax.rem(y[0] + shift, 4) * 2 + lax.rem(zh[0] + half, 2)
            for which, rows, low, high, first in layout:
                start = pl.multiple_of(spot * rows, 16)
                outs[which][pl.ds(start, rows), low:high] = piece[
                    0, base + first : base + first + rows, 0 : high - low
                ]


def unpack(layout, shapes, block, near, far):
    size = block.shape[1] // 2
    pair_at = [(0, 0), (1, size)]
    spots = [(0, pair_at), (3, pair_at), (1, pair_at), (2, [(0, 0)]), (2, [(1, 0)])]
    index = [lax.axis_index(n).astype(jnp.int32).reshape(1) for n in ("y", "zh")]
    whole = pl.BlockSpec(memory_space=pltpu.VMEM)
    return pl.pallas_call(
        functools.partial(unpack_kernel, layout, spots),
        in_specs=[pl.BlockSpec(memory_space=pltpu.SMEM)] * 2 + [whole] * 5,
        out_specs=[whole] * len(shapes),
        out_shape=[jax.ShapeDtypeStruct(v, BF) for v in shapes],
        compiler_params=pltpu.CompilerParams(vmem_limit_bytes=16 << 20),
        cost_estimate=cost(4),
        name="unpack",
    )(*index, block, *near, *far)


def sum_kernel(layout, size, count, y, *refs):
    owns, gots, outs = refs[:count], refs[count : 2 * count], refs[2 * count :]
    step = pl.program_id(0)

    def write(out, zone, base):
        for which, rows, low, high, first in layout:
            source = pl.ds(zone * rows, rows)
            value = owns[which][source, low:high].astype(F32) + gots[which][source, low:high].astype(F32)
            out[0, base + first : base + first + rows, 0 : high - low] = value.astype(BF)
            if high - low < out.shape[2]:
                out[0, base + first : base + first + rows, high - low :] = jnp.zeros(
                    (rows, out.shape[2] - high + low), BF
                )

    for j, targets in enumerate(((outs[0],), (outs[1],), (outs[2], outs[3]), (outs[4],))):

        @pl.when(step == j)
        def _(targets=targets):
            for zone in range(2):
                if len(targets) == 2:
                    write(targets[zone], zone, 0)
                else:
                    write(targets[0], zone, zone * size)


def sum_blocks(layout, size, wide, owns, gots, name):
    blocks = [
        pl.BlockSpec((v.shape[0] // 4, v.shape[1]), lambda j, y: (lax.rem(y[0] + j, 4), 0))
        for v in owns
    ]
    fixed = [pl.BlockSpec((1, n * size, wide), lambda j, y: (0, 0, 0)) for n in (2, 2, 1, 1, 2)]
    return pl.pallas_call(
        functools.partial(sum_kernel, layout, size, len(owns)),
        grid_spec=pltpu.PrefetchScalarGridSpec(
            num_scalar_prefetch=1, grid=(4,), in_specs=blocks + blocks, out_specs=fixed
        ),
        out_shape=[jax.ShapeDtypeStruct((1, n * size, wide), BF) for n in (2, 2, 1, 1, 2)],
        compiler_params=pltpu.CompilerParams(
            dimension_semantics=("arbitrary",), vmem_limit_bytes=20 << 20
        ),
        cost_estimate=cost(4),
        name=name,
    )(lax.axis_index("y").astype(jnp.int32).reshape(1), *owns, *gots)


def lines_kernel(y, own, behind, ahead, far_image, far_text, line_image, line_text):
    rows = line_image.shape[0] // 4
    for t, line in enumerate((line_image, line_text)):
        far = (far_image, far_text)[t]
        for piece, shift, low in ((own, 0, t * rows), (ahead, 1, t * rows), (behind, 3, t * rows), (far, 2, 0)):
            start = pl.multiple_of(lax.rem(y[0] + shift, 4) * rows, 16)
            line[pl.ds(start, rows), :] = piece[0, low : low + rows, :]


def lines_of(block, near, far):
    rows, width = 2 * block.shape[1], block.shape[2]
    whole = pl.BlockSpec(memory_space=pltpu.VMEM)
    return pl.pallas_call(
        lines_kernel,
        in_specs=[pl.BlockSpec(memory_space=pltpu.SMEM)] + [whole] * 5,
        out_specs=[whole] * 2,
        out_shape=[jax.ShapeDtypeStruct((rows, width), BF)] * 2,
        compiler_params=pltpu.CompilerParams(vmem_limit_bytes=12 << 20),
        cost_estimate=cost(2),
        name="lines",
    )(lax.axis_index("y").astype(jnp.int32).reshape(1), block, *near, *far)


def merge_kernel(zh, *refs):
    for line, other, out in zip(refs[:2], refs[2:4], refs[4:]):
        rows = out.shape[0] // 8
        for piece, shift in ((line, 0), (other, 1)):
            zone = lax.rem(zh[0] + shift, 2)
            for y in range(4):
                start = pl.multiple_of((2 * y + zone) * rows, 16)
                out[pl.ds(start, rows), :] = piece[y * rows : (y + 1) * rows, :]


def merge_lines(lines, others):
    rows, width = lines[0].shape
    whole = pl.BlockSpec(memory_space=pltpu.VMEM)
    return pl.pallas_call(
        merge_kernel,
        in_specs=[pl.BlockSpec(memory_space=pltpu.SMEM)] + [whole] * 4,
        out_specs=[whole] * 2,
        out_shape=[jax.ShapeDtypeStruct((2 * rows, width), BF)] * 2,
        compiler_params=pltpu.CompilerParams(vmem_limit_bytes=12 << 20),
        cost_estimate=cost(3),
        name="merge_lines",
    )(lax.axis_index("zh").astype(jnp.int32).reshape(1), *lines, *others)


def near_of(block):
    return turn(block, "y", 1), turn(block, "y", -1)


def far_of(near):
    half = near[0].shape[1] // 2
    return turn(cut(near[0], 1, 0, half), "y", 1), turn(cut(near[1], 1, half, 2 * half), "y", -1)


def mod_last_kernel(table, conds, weights, weight_grad, slot_grad, totals):
    total = jnp.zeros(slot_grad.shape, F32)
    for tile in range(weights.shape[1] // 128):
        lanes = slice(tile * 128, (tile + 1) * 128)
        values = table[:, tile, :]
        weight_grad[:, lanes] = mm_tn(conds[...], values)
        total += mm_nt(values, weights[:, lanes])
    slot_grad[...] = total
    for tile in range(0, table.shape[1], 8):
        totals[tile : tile + 8, :] = jnp.sum(table[:, tile : tile + 8, :].astype(F32), axis=0)


def mod_last(table, conds, weights):
    like = jax.ShapeDtypeStruct
    whole = pl.BlockSpec(memory_space=pltpu.VMEM)
    return pl.pallas_call(
        mod_last_kernel,
        in_specs=[whole] * 3,
        out_specs=[whole] * 3,
        out_shape=[
            like(weights.shape, F32),
            like(conds.shape, F32),
            like(table.shape[1:], F32),
        ],
        compiler_params=pltpu.CompilerParams(vmem_limit_bytes=16 << 20),
        cost_estimate=cost(4),
        name="mod_last",
    )(table, conds, weights)


def per_device(
    image_tokens,
    text_tokens,
    text_lengths,
    slot_sequence,
    conditioning,
    mod_weight,
    mod_bias,
    qkv_weight,
    qv_bias,
    out_weight,
    out_bias,
    up_weight,
    up_bias,
    down_weight,
    down_bias,
    image_cotan,
    text_cotan,
):
    seq_total, width = conditioning.shape
    image_rows, text_cap = image_tokens.shape[1], text_tokens.shape[1]
    rows = image_rows + text_cap + PAD
    own_rows = mod_weight.shape[0]
    span, ff = width // 4, up_weight.shape[2]
    ff_span = ff // 4
    half_span, half_ff = span // 2, ff_span // 2
    position = lax.axis_index("ctx")
    core = lax.axis_index("core")
    rep, y, zh = lax.axis_index("rep"), lax.axis_index("y"), lax.axis_index("zh")
    owner_index = lax.axis_index(OWNER)
    shards = 16

    def from_columns(columns):
        got = lax.all_to_all(columns, TP, split_axis=0, concat_axis=0, tiled=True)
        return got.transpose(1, 0, 2, 3).reshape(16 * own_rows, -1)

    def hot(values):
        values = values[:, 0, 0][:, None]
        return (values == jnp.arange(seq_total, dtype=jnp.int32)[None, :]).astype(F32)

    sequences = jnp.concatenate(
        direct_gather(jnp.broadcast_to(slot_sequence, (1, 8, 128)), "y")
    )
    cuts = [0, half_span, 2 * half_span, 3 * half_span]
    turn_at = cuts[2] - HEAD_DIM
    columns = (
        qkv_weight.reshape(own_rows, 2, 3, 4, 2, half_span)
        .transpose(4, 3, 1, 0, 2, 5)
        .reshape(8, 2, own_rows, 3 * half_span)
    )
    qkv_got = from_columns(
        jnp.concatenate(
            [
                columns[..., : cuts[1]],
                columns[..., turn_at : cuts[2]],
                columns[..., cuts[1] : turn_at],
                columns[..., cuts[2] :],
                jnp.zeros(columns.shape[:-1] + (HEAD_DIM,), BF),
            ],
            axis=-1,
        )
    )

    to_slice = []
    for source in range(4 * shards):
        y_at, zh_at, i = source // 16, source // 8 % 2, source % 8
        to_slice.append((source, (i * 2 + zh_at) * 4 + y_at))
    from_slice = [(d, s) for s, d in to_slice]
    out_got = lax.ppermute(out_weight.transpose(1, 0, 2), OWNER, to_slice)

    unit = down_weight.shape[0]
    wide_unit = -(-unit // 128) * 128
    lane_in, lane_out = (jnp.arange(8 * u, dtype=jnp.int32) for u in (unit, wide_unit))
    spacing = (
        (lane_in // unit * wide_unit + lane_in % unit)[:, None] == lane_out[None, :]
    ).astype(BF)
    down_mine = down_weight.transpose(1, 0, 2).reshape(1, 2 * unit, width)
    down_near = near_of(down_mine)
    for name in ("zh", "core"):
        sequences = jnp.concatenate([sequences, turn(sequences, name, 1)])
    up_wide = mm(
        up_weight.transpose(1, 0, 2).reshape(16 * own_rows, 8 * unit), spacing
    ).astype(BF)
    up_send = mm_nt(
        up_wide.reshape(2 * own_rows, 8, 8, wide_unit)
        .transpose(2, 0, 1, 3)
        .reshape(16 * own_rows, 8 * wide_unit),
        spacing,
    ).astype(BF)
    sequences, qkv_got, out_got, down_near, up_send = sync(
        sequences, qkv_got, out_got, down_near, up_send
    )

    near_hot = hot(sequences)
    live = jnp.sum(near_hot[0])
    cond_float = conditioning.astype(F32)
    cond_cols = lax.dynamic_slice_in_dim(
        jax.nn.silu(cond_float).astype(BF), owner_index * own_rows, own_rows, 1
    )
    mod_matrix = mod_weight.reshape(own_rows, -1)
    mod_hot = near_hot.reshape(2, 2, 4, seq_total).transpose(0, 2, 1, 3).reshape(16, seq_total)
    sums_mod = mod_parts(mm(mod_hot.astype(BF), cond_cols).astype(BF), mod_matrix)
    sums_mod = add_two(sums_mod[:8], turn(sums_mod[8:], "core", 1))
    sums_mod = [sums_mod[:2]] + [turn(sums_mod[2 * k : 2 * k + 2], "y", k) for k in range(1, 4)]
    sums_mod = sum(v.astype(F32) for v in sums_mod).astype(BF)

    qkv_wide, third = qkv_got.shape[1], width // 3
    first_layout = [(0, 8 * own_rows, 0, qkv_wide, 0), (1, 8 * own_rows, 0, qkv_wide, 8 * own_rows)]
    first_layout += [
        (2, 2 * own_rows, f * third, (f + 1) * third, (16 + 2 * f) * own_rows) for f in range(3)
    ]
    out_lines = out_got.reshape(2 * own_rows, width)
    first_mine = jnp.concatenate(
        [qkv_got]
        + [
            jnp.pad(out_lines[:, f * third : (f + 1) * third], ((0, 0), (0, qkv_wide - third)))
            for f in range(3)
        ]
    )[None]
    first_other = cross(first_mine)
    down_far = far_of(down_near)
    up_mine = from_columns(up_send.reshape(8, 2, own_rows, half_ff))[None]
    sums_mod, first_other, down_far, up_mine, own_tokens, own_cots = sync(
        sums_mod,
        first_other,
        down_far,
        up_mine,
        jnp.concatenate(
            [
                image_tokens[0],
                text_tokens[0],
                jnp.broadcast_to(text_lengths[0, 0].astype(BF), (PAD, width)),
            ]
        ),
        jnp.concatenate([image_cotan[0], text_cotan[0], jnp.zeros((PAD, width), BF)]),
    )

    gathered = gather_ctx(jnp.concatenate([own_tokens, own_cots])).reshape(4, 2, rows, width)
    slot_mod = add_two(sums_mod[0], turn(sums_mod[1], "zh", 1))
    modulation = (
        sum(m.astype(F32) for m in direct_gather(slot_mod, "ctx")).reshape(2, 6, width)
        + mod_bias.astype(F32).reshape(2, 6, width)
    ) * live
    down_lines = tuple(lines_of(down_mine, down_near, down_far))
    first_block = jnp.concatenate([first_mine, first_other], 1)
    first_near = near_of(first_block)
    image_line = cross(down_lines[0])
    modulation, first_near, image_line, up_mine = sync(
        modulation, first_near, image_line, up_mine
    )

    first_far = far_of(first_near)
    up_other = cross(up_mine)
    first_far, up_other = sync(first_far, up_other)

    qkv_image, qkv_text, out_raw = unpack(
        first_layout,
        [(width, qkv_wide), (width, qkv_wide), (16 * own_rows, width)],
        first_block,
        first_near,
        first_far,
    )
    qkv_own = (qkv_image, qkv_text)
    qkv_other = tuple(turn(w, "core", 1) for w in qkv_own)
    out_own = out_raw.reshape(8, 2, own_rows, width).transpose(1, 0, 2, 3)
    out_own = out_own.reshape(2, 8 * own_rows, width)
    out_rows = (out_own, turn(out_own, "core", 1))
    up_block = jnp.concatenate([up_mine, up_other], 1)
    qkv_own, up_block, gathered, text_line = sync(qkv_own, up_block, gathered, down_lines[1])

    cots_all = gathered[:, 1]
    lengths = gathered[:, 0, rows - 1, 0].astype(jnp.int32)
    row_at = jnp.arange(rows, dtype=jnp.int32)
    is_image = row_at < image_rows
    valid_all = (
        is_image[None, :] | (row_at[None, :] - image_rows < lengths[:, None])
    ).astype(F32)

    def by_row(vectors, plus=0.0):
        return jnp.where(is_image[:, None], vectors[0] + plus, vectors[1] + plus)

    def bias_part(values, start, size):
        return [
            lax.dynamic_slice_in_dim(values, start + k * size, size, 1).astype(F32)
            for k in (core, 1 - core)
        ]

    q_bias = bias_part(qv_bias, position * span, half_span)
    v_bias = bias_part(qv_bias, width + position * span, half_span)
    qkv_bias = jnp.stack(
        [
            jnp.concatenate([q, jnp.zeros_like(q), v, jnp.zeros((2, HEAD_DIM), F32)], 1)
            for q, v in zip(q_bias, v_bias)
        ]
    )[:, :, None, :]
    up_part = jnp.stack(
        [
            lax.dynamic_index_in_dim(
                up_bias.reshape(2, 8, 8, unit), k * 4 + position, 2, keepdims=False
            ).reshape(2, half_ff)
            for k in (core, 1 - core)
        ]
    ).astype(F32)[:, :, None, :]
    up_near = near_of(up_block)
    other_text_line = cross(text_line)
    modulated_first, proj_own, mixed_own = attend(
        image_rows, lengths, gathered, modulation, qkv_own, qkv_bias[0]
    )
    modulated_first, qkv_other = sync(modulated_first, qkv_other)
    proj_other, mixed_other = attend_other(
        image_rows, lengths, modulated_first, qkv_other, qkv_bias[1]
    )
    projs, mixed = (proj_own, proj_other), (mixed_own, mixed_other)
    qkv_cols = (qkv_own, qkv_other)
    attn_parts = attend_out(image_rows, mixed, out_rows)
    attn_parts, up_near, other_text_line = sync(attn_parts, up_near, other_text_line)

    attn_got = scatter_ctx(attn_parts)
    up_far = far_of(up_near)
    down_own = merge_lines((down_lines[0], text_line), (image_line, other_text_line))
    down_other = [turn(w, "core", 1) for w in down_own]
    attn_got, up_far, down_own, down_other = sync(attn_got, up_far, down_own, down_other)

    scalars = (text_lengths.reshape(1), live.reshape(1))
    flat, halved = ((rows, width), BF), ((rows, width), F32)
    out_line, down_line = out_bias.astype(F32), down_bias.astype(F32)
    base = (attn_got, own_tokens, modulation, out_line)
    (modulated_two,) = rows_call(rows_one_kernel, image_rows, "rows_one", [flat], (), base)
    modulated_two, up_far = sync(modulated_two, up_far)

    up_layout = [(t, 8 * own_rows, 0, half_ff, t * 8 * own_rows) for t in range(2)]
    down_layout = [(t, unit, 0, width, t * unit) for t in range(2)]
    up_own = unpack(up_layout, [(width, half_ff)] * 2, up_block, up_near, up_far)
    up_cols = [(w, turn(w, "core", 1)) for w in up_own]
    down_rows = list(zip(down_own, down_other))
    branch_grads = (
        cots_all.astype(F32) * (valid_all * live)[:, :, None] * by_row(modulation[:, 5])
    ).astype(BF)
    seconds = gather_ctx(modulated_two)
    seconds, up_cols, branch_grads = sync(seconds, up_cols, branch_grads)

    second_parts, down_parts, both_grads, up_sums = mlp(
        image_rows, seconds, branch_grads, up_cols, down_rows, up_part
    )
    second_parts, both_grads = sync(second_parts, both_grads)

    up_sum = sum_blocks(
        up_layout,
        16 * own_rows,
        half_ff,
        [both_grads[0], both_grads[4]],
        [turn(both_grads[k], "core", 1) for k in (1, 5)],
        "sum_up",
    )
    down_sum = sum_blocks(
        down_layout,
        2 * unit,
        width,
        [both_grads[2], both_grads[6]],
        [turn(both_grads[k], "core", 1) for k in (3, 7)],
        "sum_down",
    )
    second_got = scatter_ctx(second_parts)
    second_got, up_sum, down_sum = sync(second_got, up_sum, down_sum)

    grad_attn, grad_middle, sums_two = rows_call(
        rows_two_kernel,
        image_rows,
        "rows_two",
        [flat, halved, ((2, 4, width), F32)],
        scalars,
        (*base, own_cots, second_got),
    )
    grad_attn, up_sum, down_sum = sync(grad_attn, up_sum, down_sum)

    attn_grads = gather_ctx(grad_attn)
    up_got = scatter_near(up_sum[2], up_sum[3])
    down_got = scatter_near(down_sum[2], down_sum[3])
    up_sent = scatter_add(up_sum[1], up_sum[4], up_got)
    attn_grads, up_sent, down_got, down_parts = sync(attn_grads, up_sent, down_got, down_parts)

    branch_got = scatter_ctx(down_parts)
    up_got = scatter_far(up_sent)
    proj_grads = attend_back(image_rows, lengths, attn_grads, projs, out_rows)
    up_got, proj_grads, down_got = sync(up_got, proj_grads, down_got)

    down_sent = scatter_add(down_sum[1], down_sum[4], down_got)
    down_sent, proj_grads = sync(down_sent, proj_grads)
    down_got = scatter_far(down_sent)
    *d_qkv, d_out_own, d_out_other = attend_weights(
        image_rows, modulated_first, proj_grads, mixed, attn_grads
    )
    d_first = [d_qkv[0], d_qkv[1], d_out_own]
    d_first, d_first_other, proj_grads, branch_got, up_got = sync(
        d_first, [d_qkv[2], d_qkv[3], d_out_other], proj_grads, branch_got, up_got
    )
    first_gots = [turn(v, "core", 1) for v in d_first_other]
    first_parts, first_sums, proj_sums = attend_rows(
        image_rows, gathered, proj_grads, qkv_cols
    )
    up_keep, up_give = zones(add_three(up_sum[0], up_got))
    up_got = cross(up_give)
    first_parts, first_gots = sync(first_parts, first_gots)

    first_sum = sum_blocks(
        first_layout, first_mine.shape[1], qkv_wide, d_first, first_gots, "sum_first"
    )
    first_sum, first_parts, branch_got = sync(first_sum, first_parts, branch_got)
    first_got = scatter_ctx(first_parts)
    first_near = scatter_near(first_sum[2], first_sum[3])
    image_out, text_out, sums_three = rows_call(
        rows_three_kernel,
        image_rows,
        "rows_three",
        [(image_tokens.shape, BF), (text_tokens.shape, BF), ((2, 2, width), F32)],
        scalars,
        (*base, own_cots, branch_got, down_line),
    )

    vectors = jnp.concatenate(
        [
            jnp.concatenate([first_sums, sums_two[:, :3], sums_three[:, :1]], axis=1).reshape(-1),
            sums_two[:, 3].reshape(-1),
            sums_three[:, 1].reshape(-1),
        ]
    )

    def in_order(mine, other):
        return jnp.where(
            core == 0, jnp.concatenate([mine, other], -1), jnp.concatenate([other, mine], -1)
        )

    q_sums, v_sums = (
        in_order(*(proj_sums[h, :, 0, a * half_span : (a + 1) * half_span] for h in range(2)))
        for a in (0, 2)
    )
    heads = jnp.stack([q_sums, v_sums], 1).reshape(-1)
    message = jnp.concatenate([vectors, heads]).reshape(-1, 128)
    messages = direct_gather(message, "ctx")
    messages, first_near, down_got, up_got = sync(messages, first_near, down_got, up_got)

    first_sent = scatter_add(first_sum[1], first_sum[4], first_near)
    vectors = sum(m[: vectors.shape[0] // 128] for m in messages).reshape(-1)
    heads = jnp.stack([m[vectors.shape[0] // 128 :] for m in messages])
    heads = jnp.roll(heads.reshape(4, 2, 2, span), position, axis=0).transpose(1, 2, 0, 3)
    own_vector = jnp.concatenate([v.reshape(-1) for v in (vectors, heads, up_sums)])
    own_vector = (own_vector * live).astype(BF).reshape(1, -1, 128)
    everything = jnp.concatenate(direct_gather(own_vector, "y"))
    first_sent, everything, sequences, up_got, down_got = sync(
        first_sent, everything, sequences, up_got, down_got
    )
    first_back = scatter_far(first_sent)
    down_keep, down_give = zones(add_three(down_sum[0], down_got))
    down_got = cross(down_give)
    up_part_sum = add_two(up_keep, up_got)
    up_more = turn(up_part_sum, "rep", 1)
    for name in ("rep", "zh"):
        everything = jnp.concatenate([everything, turn(everything, name, 1)])
    far_hot = hot(turn(sequences, "rep", 1))
    image_grad, text_grad = rows_call(
        rows_four_kernel,
        image_rows,
        "rows_four",
        [(image_tokens.shape, F32), (text_tokens.shape, F32)],
        (),
        (own_tokens, modulation, first_got, grad_middle),
    )
    first_back, everything, up_more, down_got, far_hot, image_grad = sync(
        first_back, everything, up_more, down_got, far_hot, image_grad
    )

    first_keep, first_give = zones(add_three(first_sum[0], first_back))
    first_give, up_more, down_got = sync(first_give, up_more, down_got)
    first_back = cross(first_give)
    down_part_sum = add_two(down_keep, down_got)
    down_more = turn(down_part_sum, "rep", 1)
    everything = jnp.concatenate([everything, turn(everything, "core", 1)])
    first_back, everything, up_more, down_more = sync(first_back, everything, up_more, down_more)

    first_part_sum = add_two(first_keep, first_back)
    first_part_sum, up_more, down_more, everything = sync(
        first_part_sum, up_more, down_more, everything
    )
    first_more = turn(first_part_sum, "rep", 1)
    up_total = add_two(up_part_sum, up_more).reshape(2, 8, own_rows, half_ff)
    up_total = lax.all_to_all(
        up_total.transpose(1, 0, 2, 3), TP, split_axis=0, concat_axis=0, tiled=True
    )
    slot_hot = jnp.stack(
        [near_hot.reshape(4, 4, seq_total), far_hot.reshape(4, 4, seq_total)], axis=1
    ).reshape(2 * shards, seq_total)
    slot_cond = mm(slot_hot.astype(BF), cond_cols).astype(BF)
    mod_weight_grad, slot_grads, totals = mod_last(everything, slot_cond, mod_matrix)
    first_more, mod_weight_grad, slot_grads, totals, up_total, down_more = sync(
        first_more, mod_weight_grad, slot_grads, totals, up_total, down_more
    )

    first_total = add_two(first_part_sum, first_more)
    qkv_total = first_total[: 16 * own_rows].reshape(2, 8, own_rows, qkv_wide)
    qkv_total = lax.all_to_all(
        qkv_total.transpose(1, 0, 2, 3), TP, split_axis=0, concat_axis=0, tiled=True
    )
    out_total = jnp.concatenate(
        [
            first_total[(16 + 2 * f) * own_rows : (18 + 2 * f) * own_rows, :third]
            for f in range(3)
        ],
        axis=1,
    ).reshape(2, own_rows, width)
    out_grad = lax.ppermute(out_total, OWNER, from_slice).astype(F32).transpose(1, 0, 2)
    up_wide = mm(up_total.reshape(16 * own_rows, 8 * unit), spacing).astype(BF)
    up_grad = (
        mm_nt(
            up_wide.reshape(8, 2 * own_rows, 8, wide_unit)
            .transpose(1, 2, 0, 3)
            .reshape(16 * own_rows, 8 * wide_unit),
            spacing,
        )
        .reshape(2, own_rows, ff)
        .transpose(1, 0, 2)
    )
    down_grad = (
        (down_part_sum.astype(F32) + down_more.astype(F32))
        .reshape(2, unit, width)
        .transpose(1, 0, 2)
    )
    qkv_total = qkv_total.astype(F32).reshape(2, 4, 2, own_rows, -1)
    qkv_grad = (
        jnp.stack(
            [
                qkv_total[..., : cuts[1]],
                jnp.concatenate(
                    [
                        qkv_total[..., cuts[1] + HEAD_DIM : cuts[2]],
                        qkv_total[..., cuts[1] : cuts[1] + HEAD_DIM],
                    ],
                    -1,
                ),
                qkv_total[..., cuts[2] : cuts[3]],
            ],
            axis=4,
        )
        .transpose(3, 2, 4, 1, 0, 5)
        .reshape(qkv_weight.shape)
    )
    mod_weight_grad = mod_weight_grad.reshape(mod_weight.shape)
    up_lines = 2 * half_ff // 128
    here_up = jnp.sum(everything[:shards, -2 * up_lines : -up_lines].astype(F32), 0) + jnp.sum(
        everything[shards:, -up_lines:].astype(F32), 0
    )
    totals = totals.reshape(-1)
    mod_size, wide = 12 * width, 2 * width

    def owner_slice(values):
        part = values.shape[1] // (4 * shards)
        return lax.dynamic_slice_in_dim(values, owner_index * part, part, 1)

    mod_bias_grad = owner_slice(totals[:mod_size].reshape(2, -1))
    out_bias_grad = owner_slice(totals[mod_size : mod_size + wide].reshape(2, -1))
    down_bias_grad = owner_slice(totals[mod_size + wide : mod_size + 2 * wide].reshape(2, -1))
    qv_bias_grad = owner_slice(totals[mod_size + 2 * wide : mod_size + 4 * wide].reshape(2, -1))
    up_bias_grad = lax.dynamic_index_in_dim(
        here_up.reshape(2, 8, unit), y * 2 + zh, 1, keepdims=False
    )
    grad_cond_cols = lax.dot_general(
        slot_hot, slot_grads, (((0,), (0,)), ((), ())), precision=lax.Precision.HIGHEST
    )
    cond_part = lax.dynamic_slice_in_dim(cond_float, owner_index * own_rows, own_rows, 1)
    cond_grad = jax.vjp(jax.nn.silu, cond_part)[1](grad_cond_cols)[0]
    return (
        image_out,
        text_out,
        image_grad,
        text_grad,
        cond_grad,
        mod_weight_grad,
        mod_bias_grad,
        qkv_grad,
        qv_bias_grad,
        out_grad,
        out_bias_grad,
        up_grad,
        up_bias_grad,
        down_grad,
        down_bias_grad,
    )


def solution(mesh):
    fine = Mesh(mesh.devices.reshape(2, 4, 2, 2, 4), EVERY)
    rows = P(SLOT, "ctx", None)
    owned = P(OWNER, None, None)
    columns = P(None, OWNER)
    return jax.shard_map(
        per_device,
        mesh=fine,
        in_specs=(
            rows,
            rows,
            P(SLOT, "ctx"),
            P(SLOT),
            P(),
            owned,
            P(),
            owned,
            P(),
            owned,
            P(),
            owned,
            P(),
            owned,
            P(),
            rows,
            rows,
        ),
        out_specs=(
            rows,
            rows,
            rows,
            rows,
            columns,
            owned,
            columns,
            owned,
            columns,
            owned,
            columns,
            owned,
            columns,
            owned,
            columns,
        ),
        check_vma=False,
    )
```

```python
import functools

import jax
import jax.numpy as jnp
from jax import lax
from jax.experimental import pallas as pl
from jax.experimental.pallas import tpu as pltpu
from jax.sharding import Mesh, PartitionSpec as P

HEAD_DIM = 64
SHARD = ("y", "zh", "core")
TP = ("core", "ctx")
OWNER = ("y", "zh", "core", "ctx")
SLOT = ("rep", "y", "zh", "core")
EVERY = ("rep", "y", "zh", "core", "ctx")
BF = jnp.bfloat16
F32 = jnp.float32


def norm_rows(values):
    center = values - jnp.mean(values, axis=-1, keepdims=True)
    inv_scale = lax.rsqrt(jnp.mean(center * center, axis=-1, keepdims=True) + 1e-06)
    return (center * inv_scale, inv_scale)


def norm_back(grad_out, normed, inv_scale):
    return inv_scale * (
        grad_out
        - jnp.mean(grad_out, axis=-1, keepdims=True)
        - normed * jnp.mean(grad_out * normed, axis=-1, keepdims=True)
    )


def mm(left, right):
    return jnp.dot(left, right, preferred_element_type=F32)


def mm_nt(left, right):
    return lax.dot_general(left, right, (((1,), (1,)), ((), ())), preferred_element_type=F32)


def mm_tn(left, right):
    return lax.dot_general(left, right, (((0,), (0,)), ((), ())), preferred_element_type=F32)


GELU_A = 0.7978845608028654
GELU_B = 0.044715
PAD = 8


def gelu_both(values):
    square = values * values
    bent = jnp.tanh(values * (GELU_A + GELU_A * GELU_B * square))
    half_up = 0.5 + 0.5 * bent
    slope = GELU_A + 3.0 * GELU_A * GELU_B * square
    return values * half_up, half_up + 0.5 * values * (1.0 - bent * bent) * slope


def mlp_kernel(image_rows, second_in, grad_in, *refs):
    weights, bias, outs = refs[:8], refs[8], refs[9:]
    second_out, down_out, weight_grads, bias_sums = outs[0], outs[1], outs[2:10], outs[10]
    turned, second_total, down_total = outs[11:]
    stream, chunk = pl.program_id(0), pl.program_id(1)
    last = pl.num_programs(1) - 1
    blocks, rows, width = second_in.shape

    def work(low, count, t):
        total = blocks * count
        left = second_in[:, low : low + count, :].reshape(total, width)
        grad = grad_in[:, low : low + count, :].reshape(total, width)

        @pl.when(chunk == 0)
        def _():
            turned[:, :total] = left.T
            second_total[:total, :] = jnp.zeros((total, width), F32)
            down_total[:total, :] = jnp.zeros((total, width), F32)

        seconds = forwards = None
        for h in range(2):
            up, down = weights[4 * t + h], weights[4 * t + 2 + h]
            hidden = mm(left, up[...]) + bias[h, 0]
            active, slope = gelu_both(hidden)
            active = active.astype(BF)
            grad_hidden = (slope * mm_nt(grad, down[...])).astype(BF)
            second = mm_nt(grad_hidden, up[...])
            forward = mm(active, down[...])
            if h == 0:
                seconds, forwards = second, forward
            else:
                second_total[:total, :] += seconds + second
                down_total[:total, :] += forwards + forward
            weight_grads[4 * t + h][...] = mm(turned[:, :total], grad_hidden).astype(BF)
            weight_grads[4 * t + 2 + h][...] = mm_tn(active, grad).astype(BF)
            bias_sums[h, 0] = jnp.sum(grad_hidden.astype(F32), axis=0, keepdims=True)

        @pl.when(chunk == last)
        def _():
            second_out[:, low : low + count, :] = (
                second_total[:total, :].astype(BF).reshape(blocks, count, width)
            )
            down_out[:, low : low + count, :] = (
                down_total[:total, :].astype(BF).reshape(blocks, count, width)
            )

    @pl.when(stream == 0)
    def _():
        work(0, image_rows, 0)

    @pl.when(stream == 1)
    def _():
        work(image_rows, rows - image_rows, 1)


def cost(microseconds):
    return pl.CostEstimate(
        flops=int(microseconds * 1e9), bytes_accessed=int(microseconds * 1e6), transcendentals=0
    )


def mlp(image_rows, seconds, grads, ups, downs, bias):
    blocks, rows, width = seconds.shape
    hidden = ups[0][0].shape[1]
    chunk = min(256, hidden)
    last = hidden // chunk - 1
    whole = pl.BlockSpec((blocks, rows, width), lambda t, c: (0, 0, 0))
    at = [lambda t, c: jnp.where(t == 0, c, last), lambda t, c: jnp.where(t == 1, c, 0)]
    columns = [pl.BlockSpec((width, chunk), lambda t, c, f=f: (0, f(t, c))) for f in at]
    lines = [pl.BlockSpec((chunk, width), lambda t, c, f=f: (f(t, c), 0)) for f in at]
    line = pl.BlockSpec((2, 1, 1, chunk), lambda t, c: (0, t, 0, c))
    image_all = blocks * image_rows
    like = jax.ShapeDtypeStruct
    weights = [w for t in range(2) for w in (*ups[t], *downs[t])]
    specs = [v for t in range(2) for v in (columns[t], columns[t], lines[t], lines[t])]
    outs = pl.pallas_call(
        functools.partial(mlp_kernel, image_rows),
        grid=(2, hidden // chunk),
        in_specs=[whole, whole, *specs, line],
        out_specs=[whole, whole, *specs, line],
        out_shape=[
            like(seconds.shape, BF),
            like(seconds.shape, BF),
            *(like(w.shape, BF) for w in weights),
            like(bias.shape, F32),
        ],
        scratch_shapes=[
            pltpu.VMEM((width, image_all), BF),
            pltpu.VMEM((image_all, width), F32),
            pltpu.VMEM((image_all, width), F32),
        ],
        compiler_params=pltpu.CompilerParams(
            dimension_semantics=("arbitrary", "arbitrary"), vmem_limit_bytes=48 << 20
        ),
        cost_estimate=cost(33),
        name="feed_forward",
    )(seconds, grads, *weights, bias)
    return outs[0], outs[1], outs[2:10], outs[10]


def turn(values, axis, step):
    count = lax.axis_size(axis)
    return lax.ppermute(values, axis, [(i, (i + step) % count) for i in range(count)])


def cross(values):
    return lax.ppermute(values, ("rep", "zh"), [(0, 3), (3, 0), (1, 2), (2, 1)])


def after(values, *others):
    return lax.optimization_barrier((values, *others))[0]


def sync(*values):
    return lax.optimization_barrier(values)


def all_after(values, *others):
    return lax.optimization_barrier((tuple(values), *others))[0]


def cut(values, axis, low, high):
    return lax.slice_in_dim(values, low, high, axis=axis)


def scatter_near(top, bottom):
    return turn(top, "y", 1), turn(bottom, "y", -1)


def scatter_add(ahead, behind, got):
    half = got[0].shape[1]
    size = ahead.shape[1]
    to_ahead = jnp.concatenate([cut(ahead, 1, 0, half) + got[0], cut(ahead, 1, half, size)], 1)
    to_behind = jnp.concatenate([cut(behind, 1, 0, half), cut(behind, 1, half, size) + got[1]], 1)
    return to_ahead, to_behind


def scatter_far(sent):
    return turn(sent[0], "y", 1), turn(sent[1], "y", -1)


def add_three(mine, got):
    return (mine.astype(F32) + got[0].astype(F32) + got[1].astype(F32)).astype(BF)


def add_two(left, right):
    return (left.astype(F32) + right.astype(F32)).astype(BF)


def direct_gather(block, axis):
    return [block] + [turn(block, axis, -k) for k in range(1, lax.axis_size(axis))]


def zones(both):
    both = both.reshape(2, both.shape[1] // 2, both.shape[2])
    zh = lax.axis_index("zh")
    return tuple(lax.dynamic_index_in_dim(both, k, 0, keepdims=False) for k in (zh, 1 - zh))


def gather_ctx(block):
    gathered = lax.all_gather(block, "ctx", axis=0, tiled=True)
    return gathered.reshape((4,) + block.shape)


def scatter_ctx(blocks):
    flat = blocks.reshape(-1, blocks.shape[-1])
    return lax.psum_scatter(flat, "ctx", scatter_dimension=0, tiled=True)


def spread_mask(width, high):
    lane = lax.broadcasted_iota(jnp.int32, (1, width), 1)
    return ((lane >= HEAD_DIM) if high else (lane < HEAD_DIM)).astype(F32)


def key_bias_row(lengths, blocks, rows, image_rows):
    lane = lax.broadcasted_iota(jnp.int32, (1, blocks * rows), 1)
    bias = jnp.zeros((1, blocks * rows), F32)
    for c in range(blocks):
        first = c * rows + image_rows + lengths[c]
        bias = jnp.where((lane >= first) & (lane < (c + 1) * rows), -1000000000.0, bias)
    return bias


def softmax_rows(query, keys, bias):
    scores = mm_nt(query, keys) + bias
    grown = jnp.exp(scores - jnp.max(scores, axis=-1, keepdims=True))
    return grown * (1.0 / jnp.sum(grown, axis=-1, keepdims=True))


def lane_tile(ref, at, width=128):
    return ref[:, :, at : at + width].reshape(ref.shape[0] * ref.shape[1], width)


def attend_heads(image_rows, lengths, modulated, weights, bias_row, proj, mixed):
    blocks, rows, width = modulated.shape
    for t, (low, high) in enumerate(((0, image_rows), (image_rows, rows))):
        left = modulated[:, low:high, :].reshape(-1, width)
        values = (mm(left, weights[t][...]) + bias_row[t]).astype(BF)
        proj[:, low:high, :] = values.reshape(blocks, high - low, -1)
    bias = key_bias_row(lengths, blocks, rows, image_rows)
    low_mask, high_mask = (spread_mask(128, high) for high in (False, True))
    lower = low_mask > 0.5
    masks = (low_mask * 0.125, high_mask * 0.125)

    @pl.loop(0, 1, unroll=True)
    def _(_):
        at = slice(0, blocks)
        pair_query = proj[at, :, 0:128].reshape(-1, 128).astype(F32)
        pair_keys, pair_values = (lane_tile(proj, 256), lane_tile(proj, 384))
        pair_out = [
            mm(softmax_rows((pair_query * m).astype(BF), pair_keys, bias).astype(BF), pair_values)
            for m in masks
        ]
        pair_out = jnp.where(lower, pair_out[0], pair_out[1]).astype(BF)
        mixed[at, :, 0:128] = pair_out.reshape(-1, rows, 128)
        last_query = pltpu.roll(proj[at, :, 128:256].reshape(-1, 128).astype(F32), HEAD_DIM, 1) * masks[1]
        weights = softmax_rows(last_query.astype(BF), lane_tile(proj, 128), bias).astype(BF)
        last_out = mm(weights, lane_tile(proj, 512))[:, :HEAD_DIM].astype(BF)
        mixed[at, :, 128:192] = last_out.reshape(-1, rows, HEAD_DIM)


def attend_kernel(image_rows, lengths, tokens, mods, image, text, bias, modulated, proj, mixed):
    blocks, rows = modulated.shape[:2]

    @pl.loop(0, blocks, unroll=4)
    def _(c):
        for t, (low, high) in enumerate(((0, image_rows), (image_rows, rows))):
            normed, _ = norm_rows(tokens[c, 0, low:high, :].astype(F32))
            modulated[c, low:high, :] = (
                normed * (1.0 + mods[t, 1:2, :]) + mods[t, 0:1, :]
            ).astype(BF)

    attend_heads(image_rows, lengths, modulated, (image, text), bias, proj, mixed)


def attend_other_kernel(image_rows, lengths, modulated, image, text, bias, proj, mixed):
    attend_heads(image_rows, lengths, modulated, (image, text), bias, proj, mixed)


def attend_out_kernel(
    image_rows, mixed_own, mixed_other, out_own, out_other, partial
):
    blocks, rows, width = partial.shape
    streams = ((0, image_rows), (image_rows, rows))
    for t, (low, high) in enumerate(streams):
        total = None
        for mixed, weight in ((mixed_own, out_own), (mixed_other, out_other)):
            left = mixed[:, low:high, :].reshape(blocks * (high - low), -1)
            term = mm(left, weight[t])
            total = term if total is None else total + term
        partial[:, low:high, :] = total.astype(BF).reshape(blocks, high - low, width)


def attend(image_rows, lengths, tokens, mods, weights, bias):
    blocks, _, rows, width = tokens.shape
    wide, deep = weights[0].shape[1], 3 * HEAD_DIM
    like = jax.ShapeDtypeStruct
    whole = pl.BlockSpec(memory_space=pltpu.VMEM)
    return pl.pallas_call(
        functools.partial(attend_kernel, image_rows),
        in_specs=[pl.BlockSpec(memory_space=pltpu.SMEM)] + [whole] * 5,
        out_specs=[whole] * 3,
        out_shape=[
            like((blocks, rows, width), BF),
            like((blocks, rows, wide), BF),
            like((blocks, rows, deep), BF),
        ],
        compiler_params=pltpu.CompilerParams(vmem_limit_bytes=24 << 20),
        cost_estimate=cost(7),
        name="attend",
    )(lengths, tokens, mods, *weights, bias)


def attend_other(image_rows, lengths, modulated, weights, bias):
    blocks, rows, _ = modulated.shape
    wide, deep = weights[0].shape[1], 3 * HEAD_DIM
    like = jax.ShapeDtypeStruct
    whole = pl.BlockSpec(memory_space=pltpu.VMEM)
    return pl.pallas_call(
        functools.partial(attend_other_kernel, image_rows),
        in_specs=[pl.BlockSpec(memory_space=pltpu.SMEM)] + [whole] * 4,
        out_specs=[whole] * 2,
        out_shape=[like((blocks, rows, wide), BF), like((blocks, rows, deep), BF)],
        compiler_params=pltpu.CompilerParams(vmem_limit_bytes=20 << 20),
        cost_estimate=cost(4),
        name="attend_other",
    )(lengths, modulated, *weights, bias)


def attend_out(image_rows, mixed, out_rows):
    blocks, rows, deep = mixed[0].shape
    width = out_rows[0].shape[2]
    whole = pl.BlockSpec(memory_space=pltpu.VMEM)
    return pl.pallas_call(
        functools.partial(attend_out_kernel, image_rows),
        in_specs=[whole] * 4,
        out_specs=whole,
        out_shape=jax.ShapeDtypeStruct((blocks, rows, width), BF),
        compiler_params=pltpu.CompilerParams(vmem_limit_bytes=12 << 20),
        cost_estimate=cost(1),
        name="attend_out",
    )(*mixed, *out_rows)


def mod_kernel(conds, weights, out):
    for tile in range(out.shape[1]):
        out[:, tile, :] = mm(conds[...], weights[:, tile * 128 : (tile + 1) * 128]).astype(BF)


def mod_parts(conds, weights):
    slots, width = conds.shape[0], weights.shape[1]
    whole = pl.BlockSpec(memory_space=pltpu.VMEM)
    return pl.pallas_call(
        mod_kernel,
        in_specs=[whole] * 2,
        out_specs=whole,
        out_shape=jax.ShapeDtypeStruct((slots, width // 128, 128), BF),
        compiler_params=pltpu.CompilerParams(vmem_limit_bytes=8 << 20),
        cost_estimate=cost(1.5),
        name="mod_parts",
    )(conds, weights)


def attend_back_kernel(
    image_rows,
    lengths,
    grads,
    proj_own,
    proj_other,
    out_own,
    out_other,
    grad_own,
    grad_other,
    grad_mixed,
    pair_key,
    pair_value,
    last_query,
    last_key,
    last_value,
):
    blocks, rows, width = grads.shape
    total_rows = blocks * rows
    streams = ((0, image_rows), (image_rows, rows))
    bias = key_bias_row(lengths, blocks, rows, image_rows)
    low_mask, high_mask = (spread_mask(128, high) for high in (False, True))
    lower = low_mask > 0.5
    masks = (low_mask * 0.125, high_mask * 0.125)
    halves = ((proj_own, out_own, grad_own), (proj_other, out_other, grad_other))
    grad_mixed[...] = jnp.zeros(grad_mixed.shape, BF)
    for proj, out, grad in halves:
        for t, (low, high) in enumerate(streams):
            right = grads[:, low:high, :].reshape(-1, width)
            grad_mixed[:, low:high, 0:192] = (
                mm_nt(right, out[t]).astype(BF).reshape(blocks, high - low, -1)
            )
        for total in (pair_key, pair_value, last_key, last_value):
            total[...] = jnp.zeros(total.shape, F32)

        @pl.loop(0, 1, unroll=True)
        def _(_):
            at = slice(0, blocks)
            pair_query = proj[at, :, 0:128].reshape(-1, 128).astype(F32)
            pair_grad = grad_mixed[at, :, 0:128].reshape(-1, 128).astype(F32)
            pair_keys, pair_values = (lane_tile(proj, 256), lane_tile(proj, 384))
            query_grads = []
            for mask, scaled in zip((low_mask, high_mask), masks):
                query, back = (pair_query * scaled).astype(BF), (pair_grad * mask).astype(BF)
                probs = softmax_rows(query, pair_keys, bias)
                grad_probs = mm_nt(back, pair_values)
                delta = jnp.sum(probs * grad_probs, axis=-1, keepdims=True)
                grad_scores = (probs * (grad_probs - delta)).astype(BF)
                query_grads.append(mm(grad_scores, pair_keys))
                pair_key[...] += mm_tn(grad_scores, query)
                pair_value[...] += mm_tn(probs.astype(BF), back)
            grad[at, :, 0:128] = (
                (jnp.where(lower, query_grads[0], query_grads[1]) * 0.125)
                .astype(BF)
                .reshape(-1, rows, 128)
            )
            keys = lane_tile(proj, 128)
            query = (pltpu.roll(proj[at, :, 128:256].reshape(-1, 128).astype(F32), HEAD_DIM, 1) * masks[1]).astype(BF)
            back = grad_mixed[at, :, 128:256].reshape(-1, 128)
            probs = softmax_rows(query, keys, bias)
            grad_probs = mm_nt(back, lane_tile(proj, 512))
            delta = jnp.sum(probs * grad_probs, axis=-1, keepdims=True)
            grad_scores = (probs * (grad_probs - delta)).astype(BF)
            last_query[at] = (pltpu.roll(mm(grad_scores, keys), HEAD_DIM, 1) * 0.125).reshape(
                -1, rows, 128
            )
            last_key[...] += mm_tn(grad_scores, query)
            last_value[...] += mm_tn(probs.astype(BF), back)

        shape = (blocks, rows, 128)
        grad[:, :, 128:256] = (
            jnp.where(lower, last_query[...].reshape(total_rows, 128), last_key[...])
            .astype(BF)
            .reshape(shape)
        )
        grad[:, :, 256:384] = pair_key[...].astype(BF).reshape(shape)
        grad[:, :, 384:512] = pair_value[...].astype(BF).reshape(shape)
        grad[:, :, 512:640] = last_value[...].astype(BF).reshape(shape)


def attend_rows_kernel(
    image_rows,
    tokens,
    grad_own,
    grad_other,
    own_image,
    own_text,
    other_image,
    other_text,
    partial,
    row_sums,
    proj_sums,
):
    blocks, rows, width = partial.shape
    streams = ((0, image_rows), (image_rows, rows))
    for t, (low, high) in enumerate(streams):
        count = high - low
        rights = [g[:, low:high, :].reshape(blocks * count, -1) for g in (grad_own, grad_other)]
        for h, right in enumerate(rights):
            proj_sums[h, t] = jnp.sum(right.astype(F32), axis=0, keepdims=True)
        own, other = ((own_image, other_image), (own_text, other_text))[t]
        total = mm_nt(rights[0], own[...]) + mm_nt(rights[1], other[...])
        partial[:, low:high, :] = total.astype(BF).reshape(blocks, count, width)
        row_sums[t, 0:1, :] = jnp.sum(total, axis=0, keepdims=True)
        row_sums[t, 1:2, :] = jnp.zeros((1, width), F32)

    @pl.loop(0, blocks, unroll=4)
    def _(c):
        for t, (low, high) in enumerate(streams):
            normed, _ = norm_rows(tokens[c, 0, low:high, :].astype(F32))
            row_sums[t, 1:2, :] += jnp.sum(
                normed * partial[c, low:high, :].astype(F32), axis=0, keepdims=True
            )


def attend_back(image_rows, lengths, grads, projs, out_rows):
    blocks, rows, width = grads.shape
    deep = out_rows[0].shape[1]
    total = blocks * rows
    like = jax.ShapeDtypeStruct
    whole = pl.BlockSpec(memory_space=pltpu.VMEM)
    return pl.pallas_call(
        functools.partial(attend_back_kernel, image_rows),
        in_specs=[pl.BlockSpec(memory_space=pltpu.SMEM)] + [whole] * 5,
        out_specs=[whole] * 2,
        out_shape=[like(projs[0].shape, BF), like(projs[0].shape, BF)],
        scratch_shapes=[
            pltpu.VMEM((blocks, rows, 256), BF),
            pltpu.VMEM((total, 128), F32),
            pltpu.VMEM((total, 128), F32),
            pltpu.VMEM((blocks, rows, 128), F32),
            pltpu.VMEM((total, 128), F32),
            pltpu.VMEM((total, 128), F32),
        ],
        compiler_params=pltpu.CompilerParams(vmem_limit_bytes=22 << 20),
        cost_estimate=cost(5),
        name="attend_back",
    )(lengths, grads, *projs, *out_rows)


def attend_rows(image_rows, tokens, proj_grads, qkv_cols):
    blocks, _, rows, width = tokens.shape
    wide = qkv_cols[0][0].shape[1]
    like = jax.ShapeDtypeStruct
    whole = pl.BlockSpec(memory_space=pltpu.VMEM)
    return pl.pallas_call(
        functools.partial(attend_rows_kernel, image_rows),
        in_specs=[whole] * 7,
        out_specs=[whole] * 3,
        out_shape=[
            like((blocks, rows, width), BF),
            like((2, 2, width), F32),
            like((2, 2, 1, wide), F32),
        ],
        compiler_params=pltpu.CompilerParams(vmem_limit_bytes=22 << 20),
        cost_estimate=cost(8),
        name="attend_rows",
    )(tokens, *proj_grads, *qkv_cols[0], *qkv_cols[1])


def attend_weights_kernel(
    image_rows,
    modulated,
    grad_own,
    grad_other,
    mixed_own,
    mixed_other,
    grads,
    own_image,
    own_text,
    other_image,
    other_text,
    d_out_own,
    d_out_other,
):
    blocks, rows, width = modulated.shape
    kept = []
    for t, (low, high) in enumerate(((0, image_rows), (image_rows, rows))):
        left = modulated[:, low:high, :].reshape(-1, width)
        right = grads[:, low:high, :].reshape(-1, width)
        turned = left.T
        sides = ((own_image, other_image), (own_text, other_text))[t]
        for grad, d_qkv in zip((grad_own, grad_other), sides):
            values = grad[:, low:high, :].reshape(blocks * (high - low), -1)
            d_qkv[...] = mm(turned, values).astype(BF)
        for mixed, d_out in ((mixed_own, d_out_own), (mixed_other, d_out_other)):
            values = mixed[:, low:high, :].reshape(blocks * (high - low), -1)
            value = mm_tn(values, right).reshape(8, -1, width)
            if t == 0:
                kept.append(value)
            else:
                both = jnp.concatenate([kept.pop(0), value], axis=1)
                d_out[...] = both.reshape(d_out.shape).astype(BF)


def attend_weights(image_rows, modulated, proj_grads, mixed, grads):
    blocks, rows, width = modulated.shape
    wide, deep = proj_grads[0].shape[2], mixed[0].shape[2]
    like = jax.ShapeDtypeStruct
    whole = pl.BlockSpec(memory_space=pltpu.VMEM)
    return pl.pallas_call(
        functools.partial(attend_weights_kernel, image_rows),
        in_specs=[whole] * 6,
        out_specs=[whole] * 6,
        out_shape=[
            *(like((width, wide), BF) for _ in range(4)),
            like((2 * deep, width), BF),
            like((2 * deep, width), BF),
        ],
        compiler_params=pltpu.CompilerParams(vmem_limit_bytes=28 << 20),
        cost_estimate=cost(1),
        name="attend_weights",
    )(modulated, *proj_grads, *mixed, grads)


def rows_one_kernel(image_rows, got, tokens, mods, out_bias, second):
    for t, (low, high) in enumerate(((0, image_rows), (image_rows, got.shape[0]))):
        attn = got[low:high, :].astype(F32) + out_bias[t : t + 1, :]
        normed, _ = norm_rows(tokens[low:high, :].astype(F32) + mods[t, 2:3, :] * attn)
        second[low:high, :] = (normed * (1.0 + mods[t, 4:5, :]) + mods[t, 3:4, :]).astype(BF)


def masked(cots, t, length, live):
    row = lax.broadcasted_iota(jnp.int32, cots.shape, 0)
    keep = live if t == 0 else jnp.where(row < length, live, 0.0)
    return cots.astype(F32) * keep


def rows_two_kernel(
    image_rows, length, live, got, tokens, mods, out_bias, cots, back, grad_attn, grad_middle, sums
):
    for t, (low, high) in enumerate(((0, image_rows), (image_rows, got.shape[0]))):
        attn = got[low:high, :].astype(F32) + out_bias[t : t + 1, :]
        normed, inv = norm_rows(tokens[low:high, :].astype(F32) + mods[t, 2:3, :] * attn)
        grad_two = back[low:high, :].astype(F32)
        middle = masked(cots[low:high, :], t, length[0], live[0]) + norm_back(
            grad_two * (1.0 + mods[t, 4:5, :]), normed, inv
        )
        grad_middle[low:high, :] = middle
        grad = (middle * mods[t, 2:3, :]).astype(BF)
        grad_attn[low:high, :] = grad
        terms = (middle * attn, grad_two, grad_two * normed, grad.astype(F32))
        for k, term in enumerate(terms):
            sums[t, k : k + 1, :] = jnp.sum(term, axis=0, keepdims=True)


def rows_three_kernel(
    image_rows,
    length,
    live,
    got,
    tokens,
    mods,
    out_bias,
    cots,
    branch_got,
    down_bias,
    image_out,
    text_out,
    sums,
):
    for t, (low, high) in enumerate(((0, image_rows), (image_rows, got.shape[0]))):
        attn = got[low:high, :].astype(F32) + out_bias[t : t + 1, :]
        middle = tokens[low:high, :].astype(F32) + mods[t, 2:3, :] * attn
        branch = branch_got[low:high, :].astype(F32) + down_bias[t : t + 1, :]
        grad = masked(cots[low:high, :], t, length[0], live[0])
        keep = masked(jnp.ones(grad.shape, F32), t, length[0], live[0])
        out = ((middle + mods[t, 5:6, :] * branch) * keep).astype(BF)
        target = (image_out, text_out)[t]
        target[0] = out[: target.shape[1], :]
        back = (grad * mods[t, 5:6, :]).astype(BF).astype(F32)
        for k, term in enumerate((grad * branch, back)):
            sums[t, k : k + 1, :] = jnp.sum(term, axis=0, keepdims=True)


def rows_four_kernel(image_rows, tokens, mods, back, grad_middle, image_grad, text_grad):
    for t, (low, high) in enumerate(((0, image_rows), (image_rows, tokens.shape[0]))):
        normed, inv = norm_rows(tokens[low:high, :].astype(F32))
        grad = grad_middle[low:high, :] + norm_back(
            back[low:high, :].astype(F32) * (1.0 + mods[t, 1:2, :]), normed, inv
        )
        target = (image_grad, text_grad)[t]
        target[0] = grad[: target.shape[1], :]


def rows_call(kernel, image_rows, name, outs, scalars, arrays):
    whole = pl.BlockSpec(memory_space=pltpu.VMEM)
    return pl.pallas_call(
        functools.partial(kernel, image_rows),
        in_specs=[pl.BlockSpec(memory_space=pltpu.SMEM)] * len(scalars) + [whole] * len(arrays),
        out_specs=[whole] * len(outs),
        out_shape=[jax.ShapeDtypeStruct(shape, dtype) for shape, dtype in outs],
        compiler_params=pltpu.CompilerParams(vmem_limit_bytes=16 << 20),
        cost_estimate=cost(2),
        name=name,
    )(*scalars, *arrays)


def unpack_kernel(layout, spots, y, zh, *refs):
    pieces, outs = refs[:5], refs[5:]
    for piece, (shift, halves) in zip(pieces, spots):
        for half, base in halves:
            spot = lax.rem(y[0] + shift, 4) * 2 + lax.rem(zh[0] + half, 2)
            for which, rows, low, high, first in layout:
                start = pl.multiple_of(spot * rows, 16)
                outs[which][pl.ds(start, rows), low:high] = piece[
                    0, base + first : base + first + rows, 0 : high - low
                ]


def unpack(layout, shapes, block, near, far):
    size = block.shape[1] // 2
    pair_at = [(0, 0), (1, size)]
    spots = [(0, pair_at), (3, pair_at), (1, pair_at), (2, [(0, 0)]), (2, [(1, 0)])]
    index = [lax.axis_index(n).astype(jnp.int32).reshape(1) for n in ("y", "zh")]
    whole = pl.BlockSpec(memory_space=pltpu.VMEM)
    return pl.pallas_call(
        functools.partial(unpack_kernel, layout, spots),
        in_specs=[pl.BlockSpec(memory_space=pltpu.SMEM)] * 2 + [whole] * 5,
        out_specs=[whole] * len(shapes),
        out_shape=[jax.ShapeDtypeStruct(v, BF) for v in shapes],
        compiler_params=pltpu.CompilerParams(vmem_limit_bytes=16 << 20),
        cost_estimate=cost(4),
        name="unpack",
    )(*index, block, *near, *far)


def sum_kernel(layout, size, count, y, *refs):
    owns, gots, outs = refs[:count], refs[count : 2 * count], refs[2 * count :]
    step = pl.program_id(0)

    def write(out, zone, base):
        for which, rows, low, high, first in layout:
            source = pl.ds(zone * rows, rows)
            value = owns[which][source, low:high].astype(F32) + gots[which][source, low:high].astype(F32)
            out[0, base + first : base + first + rows, 0 : high - low] = value.astype(BF)
            if high - low < out.shape[2]:
                out[0, base + first : base + first + rows, high - low :] = jnp.zeros(
                    (rows, out.shape[2] - high + low), BF
                )

    for j, targets in enumerate(((outs[0],), (outs[1],), (outs[2], outs[3]), (outs[4],))):

        @pl.when(step == j)
        def _(targets=targets):
            for zone in range(2):
                if len(targets) == 2:
                    write(targets[zone], zone, 0)
                else:
                    write(targets[0], zone, zone * size)


def sum_blocks(layout, size, wide, owns, gots, name):
    blocks = [
        pl.BlockSpec((v.shape[0] // 4, v.shape[1]), lambda j, y: (lax.rem(y[0] + j, 4), 0))
        for v in owns
    ]
    fixed = [pl.BlockSpec((1, n * size, wide), lambda j, y: (0, 0, 0)) for n in (2, 2, 1, 1, 2)]
    return pl.pallas_call(
        functools.partial(sum_kernel, layout, size, len(owns)),
        grid_spec=pltpu.PrefetchScalarGridSpec(
            num_scalar_prefetch=1, grid=(4,), in_specs=blocks + blocks, out_specs=fixed
        ),
        out_shape=[jax.ShapeDtypeStruct((1, n * size, wide), BF) for n in (2, 2, 1, 1, 2)],
        compiler_params=pltpu.CompilerParams(
            dimension_semantics=("arbitrary",), vmem_limit_bytes=20 << 20
        ),
        cost_estimate=cost(4),
        name=name,
    )(lax.axis_index("y").astype(jnp.int32).reshape(1), *owns, *gots)


def lines_kernel(y, own, behind, ahead, far_image, far_text, line_image, line_text):
    rows = line_image.shape[0] // 4
    for t, line in enumerate((line_image, line_text)):
        far = (far_image, far_text)[t]
        for piece, shift, low in ((own, 0, t * rows), (ahead, 1, t * rows), (behind, 3, t * rows), (far, 2, 0)):
            start = pl.multiple_of(lax.rem(y[0] + shift, 4) * rows, 16)
            line[pl.ds(start, rows), :] = piece[0, low : low + rows, :]


def lines_of(block, near, far):
    rows, width = 2 * block.shape[1], block.shape[2]
    whole = pl.BlockSpec(memory_space=pltpu.VMEM)
    return pl.pallas_call(
        lines_kernel,
        in_specs=[pl.BlockSpec(memory_space=pltpu.SMEM)] + [whole] * 5,
        out_specs=[whole] * 2,
        out_shape=[jax.ShapeDtypeStruct((rows, width), BF)] * 2,
        compiler_params=pltpu.CompilerParams(vmem_limit_bytes=12 << 20),
        cost_estimate=cost(2),
        name="lines",
    )(lax.axis_index("y").astype(jnp.int32).reshape(1), block, *near, *far)


def merge_kernel(zh, *refs):
    for line, other, out in zip(refs[:2], refs[2:4], refs[4:]):
        rows = out.shape[0] // 8
        for piece, shift in ((line, 0), (other, 1)):
            zone = lax.rem(zh[0] + shift, 2)
            for y in range(4):
                start = pl.multiple_of((2 * y + zone) * rows, 16)
                out[pl.ds(start, rows), :] = piece[y * rows : (y + 1) * rows, :]


def merge_lines(lines, others):
    rows, width = lines[0].shape
    whole = pl.BlockSpec(memory_space=pltpu.VMEM)
    return pl.pallas_call(
        merge_kernel,
        in_specs=[pl.BlockSpec(memory_space=pltpu.SMEM)] + [whole] * 4,
        out_specs=[whole] * 2,
        out_shape=[jax.ShapeDtypeStruct((2 * rows, width), BF)] * 2,
        compiler_params=pltpu.CompilerParams(vmem_limit_bytes=12 << 20),
        cost_estimate=cost(3),
        name="merge_lines",
    )(lax.axis_index("zh").astype(jnp.int32).reshape(1), *lines, *others)


def near_of(block):
    return turn(block, "y", 1), turn(block, "y", -1)


def far_of(near):
    half = near[0].shape[1] // 2
    return turn(cut(near[0], 1, 0, half), "y", 1), turn(cut(near[1], 1, half, 2 * half), "y", -1)


def mod_last_kernel(table, conds, weights, weight_grad, slot_grad, totals):
    total = jnp.zeros(slot_grad.shape, F32)
    for tile in range(weights.shape[1] // 128):
        lanes = slice(tile * 128, (tile + 1) * 128)
        values = table[:, tile, :]
        weight_grad[:, lanes] = mm_tn(conds[...], values)
        total += mm_nt(values, weights[:, lanes])
    slot_grad[...] = total
    for tile in range(0, table.shape[1], 8):
        totals[tile : tile + 8, :] = jnp.sum(table[:, tile : tile + 8, :].astype(F32), axis=0)


def mod_last(table, conds, weights):
    like = jax.ShapeDtypeStruct
    whole = pl.BlockSpec(memory_space=pltpu.VMEM)
    return pl.pallas_call(
        mod_last_kernel,
        in_specs=[whole] * 3,
        out_specs=[whole] * 3,
        out_shape=[
            like(weights.shape, F32),
            like(conds.shape, F32),
            like(table.shape[1:], F32),
        ],
        compiler_params=pltpu.CompilerParams(vmem_limit_bytes=16 << 20),
        cost_estimate=cost(4),
        name="mod_last",
    )(table, conds, weights)


def per_device(
    image_tokens,
    text_tokens,
    text_lengths,
    slot_sequence,
    conditioning,
    mod_weight,
    mod_bias,
    qkv_weight,
    qv_bias,
    out_weight,
    out_bias,
    up_weight,
    up_bias,
    down_weight,
    down_bias,
    image_cotan,
    text_cotan,
):
    seq_total, width = conditioning.shape
    image_rows, text_cap = image_tokens.shape[1], text_tokens.shape[1]
    rows = image_rows + text_cap + PAD
    own_rows = mod_weight.shape[0]
    span, ff = width // 4, up_weight.shape[2]
    ff_span = ff // 4
    half_span, half_ff = span // 2, ff_span // 2
    position = lax.axis_index("ctx")
    core = lax.axis_index("core")
    rep, y, zh = lax.axis_index("rep"), lax.axis_index("y"), lax.axis_index("zh")
    owner_index = lax.axis_index(OWNER)
    shards = 16

    def from_columns(columns):
        got = lax.all_to_all(columns, TP, split_axis=0, concat_axis=0, tiled=True)
        return got.transpose(1, 0, 2, 3).reshape(16 * own_rows, -1)

    def hot(values):
        values = values[:, 0, 0][:, None]
        return (values == jnp.arange(seq_total, dtype=jnp.int32)[None, :]).astype(F32)

    sequences = jnp.concatenate(
        direct_gather(jnp.broadcast_to(slot_sequence, (1, 8, 128)), "y")
    )
    cuts = [0, half_span, 2 * half_span, 3 * half_span]
    turn_at = cuts[2] - HEAD_DIM
    columns = (
        qkv_weight.reshape(own_rows, 2, 3, 4, 2, half_span)
        .transpose(4, 3, 1, 0, 2, 5)
        .reshape(8, 2, own_rows, 3 * half_span)
    )
    columns = jnp.concatenate(
        [
            columns[..., : cuts[1]],
            columns[..., turn_at : cuts[2]],
            columns[..., cuts[1] : turn_at],
            columns[..., cuts[2] :],
            jnp.zeros(columns.shape[:-1] + (HEAD_DIM,), BF),
        ],
        axis=-1,
    )
    qkv_wide = columns.shape[3]

    to_slice = []
    for source in range(4 * shards):
        y_at, zh_at, i = source // 16, source // 8 % 2, source % 8
        to_slice.append((source, (i * 2 + zh_at) * 4 + y_at))
    from_slice = [(d, s) for s, d in to_slice]
    out_got = lax.ppermute(out_weight.transpose(1, 0, 2), OWNER, to_slice)

    unit = down_weight.shape[0]
    wide_unit = -(-unit // 128) * 128
    lane_in, lane_out = (jnp.arange(8 * u, dtype=jnp.int32) for u in (unit, wide_unit))
    spacing = (
        (lane_in // unit * wide_unit + lane_in % unit)[:, None] == lane_out[None, :]
    ).astype(BF)
    for name in ("zh", "core"):
        sequences = jnp.concatenate([sequences, turn(sequences, name, 1)])
    up_wide = mm(
        up_weight.transpose(1, 0, 2).reshape(16 * own_rows, 8 * unit), spacing
    ).astype(BF)
    up_send = mm_nt(
        up_wide.reshape(2 * own_rows, 8, 8, wide_unit)
        .transpose(2, 0, 1, 3)
        .reshape(16 * own_rows, 8 * wide_unit),
        spacing,
    ).astype(BF)
    got = from_columns(
        jnp.concatenate([columns, up_send.reshape(8, 2, own_rows, half_ff)], axis=-1)
    )
    sequences, got, out_got, down_weight, own_tokens, own_cots = sync(
        sequences,
        got,
        out_got,
        down_weight,
        jnp.concatenate(
            [
                image_tokens[0],
                text_tokens[0],
                jnp.broadcast_to(text_lengths[0, 0].astype(BF), (PAD, width)),
            ]
        ),
        jnp.concatenate([image_cotan[0], text_cotan[0], jnp.zeros((PAD, width), BF)]),
    )
    gathered = gather_ctx(jnp.concatenate([own_tokens, own_cots])).reshape(4, 2, rows, width)
    qkv_got, up_mine = got[:, :qkv_wide], got[:, qkv_wide:].reshape(1, 16 * own_rows, half_ff)
    down_mine = down_weight.transpose(1, 0, 2).reshape(1, 2 * unit, width)
    down_near = near_of(down_mine)

    near_hot = hot(sequences)
    live = jnp.sum(near_hot[0])
    cond_float = conditioning.astype(F32)
    cond_cols = lax.dynamic_slice_in_dim(
        jax.nn.silu(cond_float).astype(BF), owner_index * own_rows, own_rows, 1
    )
    mod_matrix = mod_weight.reshape(own_rows, -1)
    mod_hot = near_hot.reshape(2, 2, 4, seq_total).transpose(0, 2, 1, 3).reshape(16, seq_total)
    sums_mod = mod_parts(mm(mod_hot.astype(BF), cond_cols).astype(BF), mod_matrix)
    sums_mod = add_two(sums_mod[:8], turn(sums_mod[8:], "core", 1))
    sums_mod = [sums_mod[:2]] + [turn(sums_mod[2 * k : 2 * k + 2], "y", k) for k in range(1, 4)]
    sums_mod = sum(v.astype(F32) for v in sums_mod).astype(BF)

    third = width // 3
    first_layout = [(0, 8 * own_rows, 0, qkv_wide, 0), (1, 8 * own_rows, 0, qkv_wide, 8 * own_rows)]
    first_layout += [
        (2, 2 * own_rows, f * third, (f + 1) * third, (16 + 2 * f) * own_rows) for f in range(3)
    ]
    out_lines = out_got.reshape(2 * own_rows, width)
    first_mine = jnp.concatenate(
        [qkv_got]
        + [
            jnp.pad(out_lines[:, f * third : (f + 1) * third], ((0, 0), (0, qkv_wide - third)))
            for f in range(3)
        ]
    )[None]
    first_other = cross(first_mine)
    down_far = far_of(down_near)
    sums_mod, first_other, down_near, down_far, up_mine = sync(
        sums_mod, first_other, down_near, down_far, up_mine
    )

    slot_mod = add_two(sums_mod[0], turn(sums_mod[1], "zh", 1))
    modulation = (
        sum(m.astype(F32) for m in direct_gather(slot_mod, "ctx")).reshape(2, 6, width)
        + mod_bias.astype(F32).reshape(2, 6, width)
    ) * live
    first_block = jnp.concatenate([first_mine, first_other], 1)
    first_near = near_of(first_block)
    down_lines = tuple(lines_of(down_mine, down_near, down_far))
    image_line = cross(down_lines[0])
    modulation, first_near, image_line, text_line, up_mine = sync(
        modulation, first_near, image_line, down_lines[1], up_mine
    )

    first_far = far_of(first_near)
    up_other = cross(up_mine)
    first_far, up_other, gathered = sync(first_far, up_other, gathered)

    qkv_image, qkv_text, out_raw = unpack(
        first_layout,
        [(width, qkv_wide), (width, qkv_wide), (16 * own_rows, width)],
        first_block,
        first_near,
        first_far,
    )
    qkv_own = (qkv_image, qkv_text)
    qkv_other = tuple(turn(w, "core", 1) for w in qkv_own)
    out_own = out_raw.reshape(8, 2, own_rows, width).transpose(1, 0, 2, 3)
    out_own = out_own.reshape(2, 8 * own_rows, width)
    out_rows = (out_own, turn(out_own, "core", 1))
    up_block = jnp.concatenate([up_mine, up_other], 1)
    qkv_own, up_block, text_line = sync(qkv_own, up_block, text_line)

    cots_all = gathered[:, 1]
    lengths = gathered[:, 0, rows - 1, 0].astype(jnp.int32)
    row_at = jnp.arange(rows, dtype=jnp.int32)
    is_image = row_at < image_rows
    valid_all = (
        is_image[None, :] | (row_at[None, :] - image_rows < lengths[:, None])
    ).astype(F32)

    def by_row(vectors, plus=0.0):
        return jnp.where(is_image[:, None], vectors[0] + plus, vectors[1] + plus)

    def bias_part(values, start, size):
        return [
            lax.dynamic_slice_in_dim(values, start + k * size, size, 1).astype(F32)
            for k in (core, 1 - core)
        ]

    q_bias = bias_part(qv_bias, position * span, half_span)
    v_bias = bias_part(qv_bias, width + position * span, half_span)
    qkv_bias = jnp.stack(
        [
            jnp.concatenate([q, jnp.zeros_like(q), v, jnp.zeros((2, HEAD_DIM), F32)], 1)
            for q, v in zip(q_bias, v_bias)
        ]
    )[:, :, None, :]
    up_part = jnp.stack(
        [
            lax.dynamic_index_in_dim(
                up_bias.reshape(2, 8, 8, unit), k * 4 + position, 2, keepdims=False
            ).reshape(2, half_ff)
            for k in (core, 1 - core)
        ]
    ).astype(F32)[:, :, None, :]
    up_near = near_of(up_block)
    other_text_line = cross(text_line)
    modulated_first, proj_own, mixed_own = attend(
        image_rows, lengths, gathered, modulation, qkv_own, qkv_bias[0]
    )
    modulated_first, qkv_other = sync(modulated_first, qkv_other)
    proj_other, mixed_other = attend_other(
        image_rows, lengths, modulated_first, qkv_other, qkv_bias[1]
    )
    projs, mixed = (proj_own, proj_other), (mixed_own, mixed_other)
    qkv_cols = (qkv_own, qkv_other)
    attn_parts = attend_out(image_rows, mixed, out_rows)
    attn_parts, up_near, other_text_line = sync(attn_parts, up_near, other_text_line)

    attn_got = scatter_ctx(attn_parts)
    up_far = far_of(up_near)
    down_own = merge_lines((down_lines[0], text_line), (image_line, other_text_line))
    down_other = [turn(w, "core", 1) for w in down_own]
    attn_got, up_far, down_own, down_other = sync(attn_got, up_far, down_own, down_other)

    scalars = (text_lengths.reshape(1), live.reshape(1))
    flat, halved = ((rows, width), BF), ((rows, width), F32)
    out_line, down_line = out_bias.astype(F32), down_bias.astype(F32)
    base = (attn_got, own_tokens, modulation, out_line)
    (modulated_two,) = rows_call(rows_one_kernel, image_rows, "rows_one", [flat], (), base)
    modulated_two, up_far = sync(modulated_two, up_far)

    up_layout = [(t, 8 * own_rows, 0, half_ff, t * 8 * own_rows) for t in range(2)]
    down_layout = [(t, unit, 0, width, t * unit) for t in range(2)]
    up_own = unpack(up_layout, [(width, half_ff)] * 2, up_block, up_near, up_far)
    up_cols = [(w, turn(w, "core", 1)) for w in up_own]
    down_rows = list(zip(down_own, down_other))
    branch_grads = (
        cots_all.astype(F32) * (valid_all * live)[:, :, None] * by_row(modulation[:, 5])
    ).astype(BF)
    seconds = gather_ctx(modulated_two)
    seconds, up_cols, branch_grads = sync(seconds, up_cols, branch_grads)

    second_parts, down_parts, both_grads, up_sums = mlp(
        image_rows, seconds, branch_grads, up_cols, down_rows, up_part
    )
    second_parts, both_grads = sync(second_parts, both_grads)

    up_sum = sum_blocks(
        up_layout,
        16 * own_rows,
        half_ff,
        [both_grads[0], both_grads[4]],
        [turn(both_grads[k], "core", 1) for k in (1, 5)],
        "sum_up",
    )
    down_sum = sum_blocks(
        down_layout,
        2 * unit,
        width,
        [both_grads[2], both_grads[6]],
        [turn(both_grads[k], "core", 1) for k in (3, 7)],
        "sum_down",
    )
    second_got = scatter_ctx(second_parts)
    second_got, up_sum, down_sum = sync(second_got, up_sum, down_sum)

    grad_attn, grad_middle, sums_two = rows_call(
        rows_two_kernel,
        image_rows,
        "rows_two",
        [flat, halved, ((2, 4, width), F32)],
        scalars,
        (*base, own_cots, second_got),
    )
    grad_attn, up_sum, down_sum = sync(grad_attn, up_sum, down_sum)

    attn_grads = gather_ctx(grad_attn)
    up_got = scatter_near(up_sum[2], up_sum[3])
    down_got = scatter_near(down_sum[2], down_sum[3])
    up_sent = scatter_add(up_sum[1], up_sum[4], up_got)
    attn_grads, up_sent, down_got, down_parts = sync(attn_grads, up_sent, down_got, down_parts)

    branch_got = scatter_ctx(down_parts)
    up_got = scatter_far(up_sent)
    proj_grads = attend_back(image_rows, lengths, attn_grads, projs, out_rows)
    proj_grads, down_got = sync(proj_grads, down_got)

    down_sent = scatter_add(down_sum[1], down_sum[4], down_got)
    down_sent, proj_grads = sync(down_sent, proj_grads)
    down_got = scatter_far(down_sent)
    *d_qkv, d_out_own, d_out_other = attend_weights(
        image_rows, modulated_first, proj_grads, mixed, attn_grads
    )
    d_first = [d_qkv[0], d_qkv[1], d_out_own]
    d_first, d_first_other, proj_grads, up_got = sync(
        d_first, [d_qkv[2], d_qkv[3], d_out_other], proj_grads, up_got
    )
    first_gots = [turn(v, "core", 1) for v in d_first_other]
    first_parts, first_sums, proj_sums = attend_rows(
        image_rows, gathered, proj_grads, qkv_cols
    )
    up_keep, up_give = zones(add_three(up_sum[0], up_got))
    up_got = cross(up_give)
    first_parts, first_gots = sync(first_parts, first_gots)

    first_sum = sum_blocks(
        first_layout, first_mine.shape[1], qkv_wide, d_first, first_gots, "sum_first"
    )
    first_sum, first_parts, branch_got = sync(first_sum, first_parts, branch_got)
    first_got = scatter_ctx(first_parts)
    first_near = scatter_near(first_sum[2], first_sum[3])
    image_out, text_out, sums_three = rows_call(
        rows_three_kernel,
        image_rows,
        "rows_three",
        [(image_tokens.shape, BF), (text_tokens.shape, BF), ((2, 2, width), F32)],
        scalars,
        (*base, own_cots, branch_got, down_line),
    )

    vectors = jnp.concatenate(
        [
            jnp.concatenate([first_sums, sums_two[:, :3], sums_three[:, :1]], axis=1).reshape(-1),
            sums_two[:, 3].reshape(-1),
            sums_three[:, 1].reshape(-1),
        ]
    )

    def in_order(mine, other):
        return jnp.where(
            core == 0, jnp.concatenate([mine, other], -1), jnp.concatenate([other, mine], -1)
        )

    q_sums, v_sums = (
        in_order(*(proj_sums[h, :, 0, a * half_span : (a + 1) * half_span] for h in range(2)))
        for a in (0, 2)
    )
    heads = jnp.stack([q_sums, v_sums], 1).reshape(-1)
    message = jnp.concatenate([vectors, heads]).reshape(-1, 128)
    messages = direct_gather(message, "ctx")
    messages, first_near, down_got, up_got = sync(messages, first_near, down_got, up_got)

    first_sent = scatter_add(first_sum[1], first_sum[4], first_near)
    vectors = sum(m[: vectors.shape[0] // 128] for m in messages).reshape(-1)
    heads = jnp.stack([m[vectors.shape[0] // 128 :] for m in messages])
    heads = jnp.roll(heads.reshape(4, 2, 2, span), position, axis=0).transpose(1, 2, 0, 3)
    own_vector = jnp.concatenate([v.reshape(-1) for v in (vectors, heads, up_sums)])
    own_vector = (own_vector * live).astype(BF).reshape(1, -1, 128)
    everything = jnp.concatenate(direct_gather(own_vector, "y"))
    first_sent, everything, sequences, up_got, down_got = sync(
        first_sent, everything, sequences, up_got, down_got
    )
    first_back = scatter_far(first_sent)
    down_keep, down_give = zones(add_three(down_sum[0], down_got))
    down_got = cross(down_give)
    up_part_sum = add_two(up_keep, up_got)
    up_more = turn(up_part_sum, "rep", 1)
    for name in ("rep", "zh"):
        everything = jnp.concatenate([everything, turn(everything, name, 1)])
    far_hot = hot(turn(sequences, "rep", 1))
    image_grad, text_grad = rows_call(
        rows_four_kernel,
        image_rows,
        "rows_four",
        [(image_tokens.shape, F32), (text_tokens.shape, F32)],
        (),
        (own_tokens, modulation, first_got, grad_middle),
    )
    first_back, everything, up_more, down_got, far_hot, image_grad = sync(
        first_back, everything, up_more, down_got, far_hot, image_grad
    )

    first_keep, first_give = zones(add_three(first_sum[0], first_back))
    first_give, up_more, down_got, everything = sync(first_give, up_more, down_got, everything)
    first_back = cross(first_give)
    down_part_sum = add_two(down_keep, down_got)
    down_more = turn(down_part_sum, "rep", 1)
    first_back, everything, up_more = sync(first_back, everything, up_more)

    first_part_sum = add_two(first_keep, first_back)
    first_part_sum, up_more, everything = sync(first_part_sum, up_more, everything)
    qkv_lines = 16 * own_rows
    first_more = turn(first_part_sum[:qkv_lines], "rep", 1)
    everything = jnp.concatenate([everything, turn(everything, "core", 1)])
    out_total = jnp.concatenate(
        [
            first_part_sum[(16 + 2 * f) * own_rows : (18 + 2 * f) * own_rows, :third]
            for f in range(3)
        ],
        axis=1,
    ).reshape(2, own_rows, width)
    out_total = lax.ppermute(out_total, OWNER, from_slice)
    up_total = add_two(up_part_sum, up_more).reshape(2, 8, own_rows, half_ff)
    up_total = lax.all_to_all(
        up_total.transpose(1, 0, 2, 3), TP, split_axis=0, concat_axis=0, tiled=True
    )
    slot_hot = jnp.stack(
        [near_hot.reshape(4, 4, seq_total), far_hot.reshape(4, 4, seq_total)], axis=1
    ).reshape(2 * shards, seq_total)
    slot_cond = mm(slot_hot.astype(BF), cond_cols).astype(BF)
    first_more, everything, up_total, out_total = sync(first_more, everything, up_total, out_total)

    qkv_total = add_two(first_part_sum[:qkv_lines], first_more)
    qkv_total = qkv_total.reshape(2, 8, own_rows, qkv_wide)
    qkv_total = lax.all_to_all(
        qkv_total.transpose(1, 0, 2, 3), TP, split_axis=0, concat_axis=0, tiled=True
    )
    mod_weight_grad, slot_grads, totals = mod_last(everything, slot_cond, mod_matrix)
    out_grad = out_total.astype(F32) + turn(out_total, "rep", 1).astype(F32)
    out_grad = out_grad.transpose(1, 0, 2)
    up_wide = mm(up_total.reshape(16 * own_rows, 8 * unit), spacing).astype(BF)
    up_grad = (
        mm_nt(
            up_wide.reshape(8, 2 * own_rows, 8, wide_unit)
            .transpose(1, 2, 0, 3)
            .reshape(16 * own_rows, 8 * wide_unit),
            spacing,
        )
        .reshape(2, own_rows, ff)
        .transpose(1, 0, 2)
    )
    down_grad = (
        (down_part_sum.astype(F32) + down_more.astype(F32))
        .reshape(2, unit, width)
        .transpose(1, 0, 2)
    )
    qkv_total = qkv_total.astype(F32).reshape(2, 4, 2, own_rows, -1)
    qkv_grad = (
        jnp.stack(
            [
                qkv_total[..., : cuts[1]],
                jnp.concatenate(
                    [
                        qkv_total[..., cuts[1] + HEAD_DIM : cuts[2]],
                        qkv_total[..., cuts[1] : cuts[1] + HEAD_DIM],
                    ],
                    -1,
                ),
                qkv_total[..., cuts[2] : cuts[3]],
            ],
            axis=4,
        )
        .transpose(3, 2, 4, 1, 0, 5)
        .reshape(qkv_weight.shape)
    )
    mod_weight_grad = mod_weight_grad.reshape(mod_weight.shape)
    up_lines = 2 * half_ff // 128
    here_up = jnp.sum(everything[:shards, -2 * up_lines : -up_lines].astype(F32), 0) + jnp.sum(
        everything[shards:, -up_lines:].astype(F32), 0
    )
    totals = totals.reshape(-1)
    mod_size, wide = 12 * width, 2 * width

    def owner_slice(values):
        part = values.shape[1] // (4 * shards)
        return lax.dynamic_slice_in_dim(values, owner_index * part, part, 1)

    mod_bias_grad = owner_slice(totals[:mod_size].reshape(2, -1))
    out_bias_grad = owner_slice(totals[mod_size : mod_size + wide].reshape(2, -1))
    down_bias_grad = owner_slice(totals[mod_size + wide : mod_size + 2 * wide].reshape(2, -1))
    qv_bias_grad = owner_slice(totals[mod_size + 2 * wide : mod_size + 4 * wide].reshape(2, -1))
    up_bias_grad = lax.dynamic_index_in_dim(
        here_up.reshape(2, 8, unit), y * 2 + zh, 1, keepdims=False
    )
    grad_cond_cols = lax.dot_general(
        slot_hot, slot_grads, (((0,), (0,)), ((), ())), precision=lax.Precision.HIGHEST
    )
    cond_part = lax.dynamic_slice_in_dim(cond_float, owner_index * own_rows, own_rows, 1)
    cond_grad = jax.vjp(jax.nn.silu, cond_part)[1](grad_cond_cols)[0]
    return (
        image_out,
        text_out,
        image_grad,
        text_grad,
        cond_grad,
        mod_weight_grad,
        mod_bias_grad,
        qkv_grad,
        qv_bias_grad,
        out_grad,
        out_bias_grad,
        up_grad,
        up_bias_grad,
        down_grad,
        down_bias_grad,
    )


def solution(mesh):
    fine = Mesh(mesh.devices.reshape(2, 4, 2, 2, 4), EVERY)
    rows = P(SLOT, "ctx", None)
    owned = P(OWNER, None, None)
    columns = P(None, OWNER)
    return jax.shard_map(
        per_device,
        mesh=fine,
        in_specs=(
            rows,
            rows,
            P(SLOT, "ctx"),
            P(SLOT),
            P(),
            owned,
            P(),
            owned,
            P(),
            owned,
            P(),
            owned,
            P(),
            owned,
            P(),
            rows,
            rows,
        ),
        out_specs=(
            rows,
            rows,
            rows,
            rows,
            columns,
            owned,
            columns,
            owned,
            columns,
            owned,
            columns,
            owned,
            columns,
            owned,
            columns,
        ),
        check_vma=False,
    )
```

```python
import functools

import jax
import jax.numpy as jnp
from jax import lax
from jax.experimental import pallas as pl
from jax.experimental.pallas import tpu as pltpu
from jax.sharding import Mesh, PartitionSpec as P

HEAD_DIM = 64
SHARD = ("y", "zh", "core")
TP = ("core", "ctx")
OWNER = ("y", "zh", "core", "ctx")
SLOT = ("rep", "y", "zh", "core")
EVERY = ("rep", "y", "zh", "core", "ctx")
BF = jnp.bfloat16
F32 = jnp.float32


def norm_rows(values):
    center = values - jnp.mean(values, axis=-1, keepdims=True)
    inv_scale = lax.rsqrt(jnp.mean(center * center, axis=-1, keepdims=True) + 1e-06)
    return (center * inv_scale, inv_scale)


def norm_back(grad_out, normed, inv_scale):
    return inv_scale * (
        grad_out
        - jnp.mean(grad_out, axis=-1, keepdims=True)
        - normed * jnp.mean(grad_out * normed, axis=-1, keepdims=True)
    )


def mm(left, right):
    return jnp.dot(left, right, preferred_element_type=F32)


def mm_nt(left, right):
    return lax.dot_general(left, right, (((1,), (1,)), ((), ())), preferred_element_type=F32)


def mm_tn(left, right):
    return lax.dot_general(left, right, (((0,), (0,)), ((), ())), preferred_element_type=F32)


GELU_A = 0.7978845608028654
GELU_B = 0.044715
PAD = 8


def gelu_both(values):
    square = values * values
    bent = jnp.tanh(values * (GELU_A + GELU_A * GELU_B * square))
    half_up = 0.5 + 0.5 * bent
    slope = GELU_A + 3.0 * GELU_A * GELU_B * square
    return values * half_up, half_up + 0.5 * values * (1.0 - bent * bent) * slope


def mlp_kernel(image_rows, second_in, grad_in, *refs):
    weights, bias, outs = refs[:8], refs[8], refs[9:]
    second_out, down_out, weight_grads, bias_sums = outs[0], outs[1], outs[2:10], outs[10]
    turned, second_total, down_total = outs[11:]
    stream, chunk = pl.program_id(0), pl.program_id(1)
    last = pl.num_programs(1) - 1
    blocks, rows, width = second_in.shape

    def work(low, count, t):
        total = blocks * count
        left = second_in[:, low : low + count, :].reshape(total, width)
        grad = grad_in[:, low : low + count, :].reshape(total, width)

        @pl.when(chunk == 0)
        def _():
            turned[:, :total] = left.T
            second_total[:total, :] = jnp.zeros((total, width), F32)
            down_total[:total, :] = jnp.zeros((total, width), F32)

        seconds = forwards = None
        for h in range(2):
            up, down = weights[4 * t + h], weights[4 * t + 2 + h]
            hidden = mm(left, up[...]) + bias[h, 0]
            active, slope = gelu_both(hidden)
            active = active.astype(BF)
            grad_hidden = (slope * mm_nt(grad, down[...])).astype(BF)
            second = mm_nt(grad_hidden, up[...])
            forward = mm(active, down[...])
            if h == 0:
                seconds, forwards = second, forward
            else:
                second_total[:total, :] += seconds + second
                down_total[:total, :] += forwards + forward
            weight_grads[4 * t + h][...] = mm(turned[:, :total], grad_hidden).astype(BF)
            weight_grads[4 * t + 2 + h][...] = mm_tn(active, grad).astype(BF)
            bias_sums[h, 0] = jnp.sum(grad_hidden.astype(F32), axis=0, keepdims=True)

        @pl.when(chunk == last)
        def _():
            second_out[:, low : low + count, :] = (
                second_total[:total, :].astype(BF).reshape(blocks, count, width)
            )
            down_out[:, low : low + count, :] = (
                down_total[:total, :].astype(BF).reshape(blocks, count, width)
            )

    @pl.when(stream == 0)
    def _():
        work(0, image_rows, 0)

    @pl.when(stream == 1)
    def _():
        work(image_rows, rows - image_rows, 1)


def cost(microseconds):
    return pl.CostEstimate(
        flops=int(microseconds * 1e9), bytes_accessed=int(microseconds * 1e6), transcendentals=0
    )


def mlp(image_rows, seconds, grads, ups, downs, bias):
    blocks, rows, width = seconds.shape
    hidden = ups[0][0].shape[1]
    chunk = min(256, hidden)
    last = hidden // chunk - 1
    whole = pl.BlockSpec((blocks, rows, width), lambda t, c: (0, 0, 0))
    at = [lambda t, c: jnp.where(t == 0, c, last), lambda t, c: jnp.where(t == 1, c, 0)]
    columns = [pl.BlockSpec((width, chunk), lambda t, c, f=f: (0, f(t, c))) for f in at]
    lines = [pl.BlockSpec((chunk, width), lambda t, c, f=f: (f(t, c), 0)) for f in at]
    line = pl.BlockSpec((2, 1, 1, chunk), lambda t, c: (0, t, 0, c))
    image_all = blocks * image_rows
    like = jax.ShapeDtypeStruct
    weights = [w for t in range(2) for w in (*ups[t], *downs[t])]
    specs = [v for t in range(2) for v in (columns[t], columns[t], lines[t], lines[t])]
    outs = pl.pallas_call(
        functools.partial(mlp_kernel, image_rows),
        grid=(2, hidden // chunk),
        in_specs=[whole, whole, *specs, line],
        out_specs=[whole, whole, *specs, line],
        out_shape=[
            like(seconds.shape, BF),
            like(seconds.shape, BF),
            *(like(w.shape, BF) for w in weights),
            like(bias.shape, F32),
        ],
        scratch_shapes=[
            pltpu.VMEM((width, image_all), BF),
            pltpu.VMEM((image_all, width), F32),
            pltpu.VMEM((image_all, width), F32),
        ],
        compiler_params=pltpu.CompilerParams(
            dimension_semantics=("arbitrary", "arbitrary"), vmem_limit_bytes=48 << 20
        ),
        cost_estimate=cost(33),
        name="feed_forward",
    )(seconds, grads, *weights, bias)
    return outs[0], outs[1], outs[2:10], outs[10]


def turn(values, axis, step):
    count = lax.axis_size(axis)
    return lax.ppermute(values, axis, [(i, (i + step) % count) for i in range(count)])


def cross(values):
    return lax.ppermute(values, ("rep", "zh"), [(0, 3), (3, 0), (1, 2), (2, 1)])


def after(values, *others):
    return lax.optimization_barrier((values, *others))[0]


def sync(*values):
    return lax.optimization_barrier(values)


def all_after(values, *others):
    return lax.optimization_barrier((tuple(values), *others))[0]


def cut(values, axis, low, high):
    return lax.slice_in_dim(values, low, high, axis=axis)


def scatter_near(top, bottom):
    return turn(top, "y", 1), turn(bottom, "y", -1)


def scatter_add(ahead, behind, got):
    half = got[0].shape[1]
    size = ahead.shape[1]
    to_ahead = jnp.concatenate([cut(ahead, 1, 0, half) + got[0], cut(ahead, 1, half, size)], 1)
    to_behind = jnp.concatenate([cut(behind, 1, 0, half), cut(behind, 1, half, size) + got[1]], 1)
    return to_ahead, to_behind


def scatter_far(sent):
    return turn(sent[0], "y", 1), turn(sent[1], "y", -1)


def add_three(mine, got):
    return (mine.astype(F32) + got[0].astype(F32) + got[1].astype(F32)).astype(BF)


def add_two(left, right):
    return (left.astype(F32) + right.astype(F32)).astype(BF)


def direct_gather(block, axis):
    return [block] + [turn(block, axis, -k) for k in range(1, lax.axis_size(axis))]


def zones(both):
    both = both.reshape(2, both.shape[1] // 2, both.shape[2])
    zh = lax.axis_index("zh")
    return tuple(lax.dynamic_index_in_dim(both, k, 0, keepdims=False) for k in (zh, 1 - zh))


def gather_ctx(block):
    gathered = lax.all_gather(block, "ctx", axis=0, tiled=True)
    return gathered.reshape((4,) + block.shape)


def scatter_ctx(blocks):
    flat = blocks.reshape(-1, blocks.shape[-1])
    return lax.psum_scatter(flat, "ctx", scatter_dimension=0, tiled=True)


def spread_mask(width, high):
    lane = lax.broadcasted_iota(jnp.int32, (1, width), 1)
    return ((lane >= HEAD_DIM) if high else (lane < HEAD_DIM)).astype(F32)


def key_bias_row(lengths, blocks, rows, image_rows):
    lane = lax.broadcasted_iota(jnp.int32, (1, blocks * rows), 1)
    bias = jnp.zeros((1, blocks * rows), F32)
    for c in range(blocks):
        first = c * rows + image_rows + lengths[c]
        bias = jnp.where((lane >= first) & (lane < (c + 1) * rows), -1000000000.0, bias)
    return bias


def softmax_rows(query, keys, bias):
    scores = mm_nt(query, keys) + bias
    grown = jnp.exp(scores - jnp.max(scores, axis=-1, keepdims=True))
    return grown * (1.0 / jnp.sum(grown, axis=-1, keepdims=True))


def lane_tile(ref, at, width=128):
    return ref[:, :, at : at + width].reshape(ref.shape[0] * ref.shape[1], width)


def attend_heads(image_rows, lengths, modulated, weights, bias_row, proj, mixed):
    blocks, rows, width = modulated.shape
    for t, (low, high) in enumerate(((0, image_rows), (image_rows, rows))):
        left = modulated[:, low:high, :].reshape(-1, width)
        values = (mm(left, weights[t][...]) + bias_row[t]).astype(BF)
        proj[:, low:high, :] = values.reshape(blocks, high - low, -1)
    bias = key_bias_row(lengths, blocks, rows, image_rows)
    low_mask, high_mask = (spread_mask(128, high) for high in (False, True))
    lower = low_mask > 0.5
    masks = (low_mask * 0.125, high_mask * 0.125)

    @pl.loop(0, 1, unroll=True)
    def _(_):
        at = slice(0, blocks)
        pair_query = proj[at, :, 0:128].reshape(-1, 128).astype(F32)
        pair_keys, pair_values = (lane_tile(proj, 256), lane_tile(proj, 384))
        pair_out = [
            mm(softmax_rows((pair_query * m).astype(BF), pair_keys, bias).astype(BF), pair_values)
            for m in masks
        ]
        pair_out = jnp.where(lower, pair_out[0], pair_out[1]).astype(BF)
        mixed[at, :, 0:128] = pair_out.reshape(-1, rows, 128)
        last_query = pltpu.roll(proj[at, :, 128:256].reshape(-1, 128).astype(F32), HEAD_DIM, 1) * masks[1]
        weights = softmax_rows(last_query.astype(BF), lane_tile(proj, 128), bias).astype(BF)
        last_out = mm(weights, lane_tile(proj, 512))[:, :HEAD_DIM].astype(BF)
        mixed[at, :, 128:192] = last_out.reshape(-1, rows, HEAD_DIM)


def attend_kernel(image_rows, lengths, tokens, mods, image, text, bias, modulated, proj, mixed):
    blocks, rows = modulated.shape[:2]

    @pl.loop(0, blocks, unroll=4)
    def _(c):
        for t, (low, high) in enumerate(((0, image_rows), (image_rows, rows))):
            normed, _ = norm_rows(tokens[c, 0, low:high, :].astype(F32))
            modulated[c, low:high, :] = (
                normed * (1.0 + mods[t, 1:2, :]) + mods[t, 0:1, :]
            ).astype(BF)

    attend_heads(image_rows, lengths, modulated, (image, text), bias, proj, mixed)


def attend_other_kernel(image_rows, lengths, modulated, image, text, bias, proj, mixed):
    attend_heads(image_rows, lengths, modulated, (image, text), bias, proj, mixed)


def attend_out_kernel(
    image_rows, mixed_own, mixed_other, out_own, out_other, partial
):
    blocks, rows, width = partial.shape
    streams = ((0, image_rows), (image_rows, rows))
    for t, (low, high) in enumerate(streams):
        total = None
        for mixed, weight in ((mixed_own, out_own), (mixed_other, out_other)):
            left = mixed[:, low:high, :].reshape(blocks * (high - low), -1)
            term = mm(left, weight[t])
            total = term if total is None else total + term
        partial[:, low:high, :] = total.astype(BF).reshape(blocks, high - low, width)


def attend(image_rows, lengths, tokens, mods, weights, bias):
    blocks, _, rows, width = tokens.shape
    wide, deep = weights[0].shape[1], 3 * HEAD_DIM
    like = jax.ShapeDtypeStruct
    whole = pl.BlockSpec(memory_space=pltpu.VMEM)
    return pl.pallas_call(
        functools.partial(attend_kernel, image_rows),
        in_specs=[pl.BlockSpec(memory_space=pltpu.SMEM)] + [whole] * 5,
        out_specs=[whole] * 3,
        out_shape=[
            like((blocks, rows, width), BF),
            like((blocks, rows, wide), BF),
            like((blocks, rows, deep), BF),
        ],
        compiler_params=pltpu.CompilerParams(vmem_limit_bytes=24 << 20),
        cost_estimate=cost(7),
        name="attend",
    )(lengths, tokens, mods, *weights, bias)


def attend_other(image_rows, lengths, modulated, weights, bias):
    blocks, rows, _ = modulated.shape
    wide, deep = weights[0].shape[1], 3 * HEAD_DIM
    like = jax.ShapeDtypeStruct
    whole = pl.BlockSpec(memory_space=pltpu.VMEM)
    return pl.pallas_call(
        functools.partial(attend_other_kernel, image_rows),
        in_specs=[pl.BlockSpec(memory_space=pltpu.SMEM)] + [whole] * 4,
        out_specs=[whole] * 2,
        out_shape=[like((blocks, rows, wide), BF), like((blocks, rows, deep), BF)],
        compiler_params=pltpu.CompilerParams(vmem_limit_bytes=20 << 20),
        cost_estimate=cost(4),
        name="attend_other",
    )(lengths, modulated, *weights, bias)


def attend_out(image_rows, mixed, out_rows):
    blocks, rows, deep = mixed[0].shape
    width = out_rows[0].shape[2]
    whole = pl.BlockSpec(memory_space=pltpu.VMEM)
    return pl.pallas_call(
        functools.partial(attend_out_kernel, image_rows),
        in_specs=[whole] * 4,
        out_specs=whole,
        out_shape=jax.ShapeDtypeStruct((blocks, rows, width), BF),
        compiler_params=pltpu.CompilerParams(vmem_limit_bytes=12 << 20),
        cost_estimate=cost(1),
        name="attend_out",
    )(*mixed, *out_rows)


def mod_kernel(conds, weights, out):
    for tile in range(out.shape[1]):
        out[:, tile, :] = mm(conds[...], weights[:, tile * 128 : (tile + 1) * 128]).astype(BF)


def mod_parts(conds, weights):
    slots, width = conds.shape[0], weights.shape[1]
    whole = pl.BlockSpec(memory_space=pltpu.VMEM)
    return pl.pallas_call(
        mod_kernel,
        in_specs=[whole] * 2,
        out_specs=whole,
        out_shape=jax.ShapeDtypeStruct((slots, width // 128, 128), BF),
        compiler_params=pltpu.CompilerParams(vmem_limit_bytes=8 << 20),
        cost_estimate=cost(1.5),
        name="mod_parts",
    )(conds, weights)


def attend_back_kernel(
    image_rows,
    lengths,
    grads,
    proj_own,
    proj_other,
    out_own,
    out_other,
    grad_own,
    grad_other,
    grad_mixed,
    pair_key,
    pair_value,
    last_query,
    last_key,
    last_value,
):
    blocks, rows, width = grads.shape
    total_rows = blocks * rows
    streams = ((0, image_rows), (image_rows, rows))
    bias = key_bias_row(lengths, blocks, rows, image_rows)
    low_mask, high_mask = (spread_mask(128, high) for high in (False, True))
    lower = low_mask > 0.5
    masks = (low_mask * 0.125, high_mask * 0.125)
    halves = ((proj_own, out_own, grad_own), (proj_other, out_other, grad_other))
    grad_mixed[...] = jnp.zeros(grad_mixed.shape, BF)
    for proj, out, grad in halves:
        for t, (low, high) in enumerate(streams):
            right = grads[:, low:high, :].reshape(-1, width)
            grad_mixed[:, low:high, 0:192] = (
                mm_nt(right, out[t]).astype(BF).reshape(blocks, high - low, -1)
            )
        for total in (pair_key, pair_value, last_key, last_value):
            total[...] = jnp.zeros(total.shape, F32)

        @pl.loop(0, 1, unroll=True)
        def _(_):
            at = slice(0, blocks)
            pair_query = proj[at, :, 0:128].reshape(-1, 128).astype(F32)
            pair_grad = grad_mixed[at, :, 0:128].reshape(-1, 128).astype(F32)
            pair_keys, pair_values = (lane_tile(proj, 256), lane_tile(proj, 384))
            query_grads = []
            for mask, scaled in zip((low_mask, high_mask), masks):
                query, back = (pair_query * scaled).astype(BF), (pair_grad * mask).astype(BF)
                probs = softmax_rows(query, pair_keys, bias)
                grad_probs = mm_nt(back, pair_values)
                delta = jnp.sum(probs * grad_probs, axis=-1, keepdims=True)
                grad_scores = (probs * (grad_probs - delta)).astype(BF)
                query_grads.append(mm(grad_scores, pair_keys))
                pair_key[...] += mm_tn(grad_scores, query)
                pair_value[...] += mm_tn(probs.astype(BF), back)
            grad[at, :, 0:128] = (
                (jnp.where(lower, query_grads[0], query_grads[1]) * 0.125)
                .astype(BF)
                .reshape(-1, rows, 128)
            )
            keys = lane_tile(proj, 128)
            query = (pltpu.roll(proj[at, :, 128:256].reshape(-1, 128).astype(F32), HEAD_DIM, 1) * masks[1]).astype(BF)
            back = grad_mixed[at, :, 128:256].reshape(-1, 128)
            probs = softmax_rows(query, keys, bias)
            grad_probs = mm_nt(back, lane_tile(proj, 512))
            delta = jnp.sum(probs * grad_probs, axis=-1, keepdims=True)
            grad_scores = (probs * (grad_probs - delta)).astype(BF)
            last_query[at] = (pltpu.roll(mm(grad_scores, keys), HEAD_DIM, 1) * 0.125).reshape(
                -1, rows, 128
            )
            last_key[...] += mm_tn(grad_scores, query)
            last_value[...] += mm_tn(probs.astype(BF), back)

        shape = (blocks, rows, 128)
        grad[:, :, 128:256] = (
            jnp.where(lower, last_query[...].reshape(total_rows, 128), last_key[...])
            .astype(BF)
            .reshape(shape)
        )
        grad[:, :, 256:384] = pair_key[...].astype(BF).reshape(shape)
        grad[:, :, 384:512] = pair_value[...].astype(BF).reshape(shape)
        grad[:, :, 512:640] = last_value[...].astype(BF).reshape(shape)


def attend_rows_kernel(
    image_rows,
    tokens,
    grad_own,
    grad_other,
    own_image,
    own_text,
    other_image,
    other_text,
    partial,
    row_sums,
    proj_sums,
):
    blocks, rows, width = partial.shape
    streams = ((0, image_rows), (image_rows, rows))
    for t, (low, high) in enumerate(streams):
        count = high - low
        rights = [g[:, low:high, :].reshape(blocks * count, -1) for g in (grad_own, grad_other)]
        for h, right in enumerate(rights):
            proj_sums[h, t] = jnp.sum(right.astype(F32), axis=0, keepdims=True)
        own, other = ((own_image, other_image), (own_text, other_text))[t]
        total = mm_nt(rights[0], own[...]) + mm_nt(rights[1], other[...])
        partial[:, low:high, :] = total.astype(BF).reshape(blocks, count, width)
        row_sums[t, 0:1, :] = jnp.sum(total, axis=0, keepdims=True)
        row_sums[t, 1:2, :] = jnp.zeros((1, width), F32)

    @pl.loop(0, blocks, unroll=4)
    def _(c):
        for t, (low, high) in enumerate(streams):
            normed, _ = norm_rows(tokens[c, 0, low:high, :].astype(F32))
            row_sums[t, 1:2, :] += jnp.sum(
                normed * partial[c, low:high, :].astype(F32), axis=0, keepdims=True
            )


def attend_back(image_rows, lengths, grads, projs, out_rows):
    blocks, rows, width = grads.shape
    deep = out_rows[0].shape[1]
    total = blocks * rows
    like = jax.ShapeDtypeStruct
    whole = pl.BlockSpec(memory_space=pltpu.VMEM)
    return pl.pallas_call(
        functools.partial(attend_back_kernel, image_rows),
        in_specs=[pl.BlockSpec(memory_space=pltpu.SMEM)] + [whole] * 5,
        out_specs=[whole] * 2,
        out_shape=[like(projs[0].shape, BF), like(projs[0].shape, BF)],
        scratch_shapes=[
            pltpu.VMEM((blocks, rows, 256), BF),
            pltpu.VMEM((total, 128), F32),
            pltpu.VMEM((total, 128), F32),
            pltpu.VMEM((blocks, rows, 128), F32),
            pltpu.VMEM((total, 128), F32),
            pltpu.VMEM((total, 128), F32),
        ],
        compiler_params=pltpu.CompilerParams(vmem_limit_bytes=22 << 20),
        cost_estimate=cost(5),
        name="attend_back",
    )(lengths, grads, *projs, *out_rows)


def attend_rows(image_rows, tokens, proj_grads, qkv_cols):
    blocks, _, rows, width = tokens.shape
    wide = qkv_cols[0][0].shape[1]
    like = jax.ShapeDtypeStruct
    whole = pl.BlockSpec(memory_space=pltpu.VMEM)
    return pl.pallas_call(
        functools.partial(attend_rows_kernel, image_rows),
        in_specs=[whole] * 7,
        out_specs=[whole] * 3,
        out_shape=[
            like((blocks, rows, width), BF),
            like((2, 2, width), F32),
            like((2, 2, 1, wide), F32),
        ],
        compiler_params=pltpu.CompilerParams(vmem_limit_bytes=22 << 20),
        cost_estimate=cost(8),
        name="attend_rows",
    )(tokens, *proj_grads, *qkv_cols[0], *qkv_cols[1])


def attend_weights_kernel(
    image_rows,
    modulated,
    grad_own,
    grad_other,
    mixed_own,
    mixed_other,
    grads,
    own_image,
    own_text,
    other_image,
    other_text,
    d_out_own,
    d_out_other,
):
    blocks, rows, width = modulated.shape
    kept = []
    for t, (low, high) in enumerate(((0, image_rows), (image_rows, rows))):
        left = modulated[:, low:high, :].reshape(-1, width)
        right = grads[:, low:high, :].reshape(-1, width)
        turned = left.T
        sides = ((own_image, other_image), (own_text, other_text))[t]
        for grad, d_qkv in zip((grad_own, grad_other), sides):
            values = grad[:, low:high, :].reshape(blocks * (high - low), -1)
            d_qkv[...] = mm(turned, values).astype(BF)
        for mixed, d_out in ((mixed_own, d_out_own), (mixed_other, d_out_other)):
            values = mixed[:, low:high, :].reshape(blocks * (high - low), -1)
            value = mm_tn(values, right).reshape(8, -1, width)
            if t == 0:
                kept.append(value)
            else:
                both = jnp.concatenate([kept.pop(0), value], axis=1)
                d_out[...] = both.reshape(d_out.shape).astype(BF)


def attend_weights(image_rows, modulated, proj_grads, mixed, grads):
    blocks, rows, width = modulated.shape
    wide, deep = proj_grads[0].shape[2], mixed[0].shape[2]
    like = jax.ShapeDtypeStruct
    whole = pl.BlockSpec(memory_space=pltpu.VMEM)
    return pl.pallas_call(
        functools.partial(attend_weights_kernel, image_rows),
        in_specs=[whole] * 6,
        out_specs=[whole] * 6,
        out_shape=[
            *(like((width, wide), BF) for _ in range(4)),
            like((2 * deep, width), BF),
            like((2 * deep, width), BF),
        ],
        compiler_params=pltpu.CompilerParams(vmem_limit_bytes=28 << 20),
        cost_estimate=cost(1),
        name="attend_weights",
    )(modulated, *proj_grads, *mixed, grads)


def rows_one_kernel(image_rows, got, tokens, mods, out_bias, second):
    for t, (low, high) in enumerate(((0, image_rows), (image_rows, got.shape[0]))):
        attn = got[low:high, :].astype(F32) + out_bias[t : t + 1, :]
        normed, _ = norm_rows(tokens[low:high, :].astype(F32) + mods[t, 2:3, :] * attn)
        second[low:high, :] = (normed * (1.0 + mods[t, 4:5, :]) + mods[t, 3:4, :]).astype(BF)


def masked(cots, t, length, live):
    row = lax.broadcasted_iota(jnp.int32, cots.shape, 0)
    keep = live if t == 0 else jnp.where(row < length, live, 0.0)
    return cots.astype(F32) * keep


def rows_two_kernel(
    image_rows, length, live, got, tokens, mods, out_bias, cots, back, grad_attn, grad_middle, sums
):
    for t, (low, high) in enumerate(((0, image_rows), (image_rows, got.shape[0]))):
        attn = got[low:high, :].astype(F32) + out_bias[t : t + 1, :]
        normed, inv = norm_rows(tokens[low:high, :].astype(F32) + mods[t, 2:3, :] * attn)
        grad_two = back[low:high, :].astype(F32)
        middle = masked(cots[low:high, :], t, length[0], live[0]) + norm_back(
            grad_two * (1.0 + mods[t, 4:5, :]), normed, inv
        )
        grad_middle[low:high, :] = middle
        grad = (middle * mods[t, 2:3, :]).astype(BF)
        grad_attn[low:high, :] = grad
        terms = (middle * attn, grad_two, grad_two * normed, grad.astype(F32))
        for k, term in enumerate(terms):
            sums[t, k : k + 1, :] = jnp.sum(term, axis=0, keepdims=True)


def rows_three_kernel(
    image_rows,
    length,
    live,
    got,
    tokens,
    mods,
    out_bias,
    cots,
    branch_got,
    down_bias,
    image_out,
    text_out,
    sums,
):
    for t, (low, high) in enumerate(((0, image_rows), (image_rows, got.shape[0]))):
        attn = got[low:high, :].astype(F32) + out_bias[t : t + 1, :]
        middle = tokens[low:high, :].astype(F32) + mods[t, 2:3, :] * attn
        branch = branch_got[low:high, :].astype(F32) + down_bias[t : t + 1, :]
        grad = masked(cots[low:high, :], t, length[0], live[0])
        keep = masked(jnp.ones(grad.shape, F32), t, length[0], live[0])
        out = ((middle + mods[t, 5:6, :] * branch) * keep).astype(BF)
        target = (image_out, text_out)[t]
        target[0] = out[: target.shape[1], :]
        back = (grad * mods[t, 5:6, :]).astype(BF).astype(F32)
        for k, term in enumerate((grad * branch, back)):
            sums[t, k : k + 1, :] = jnp.sum(term, axis=0, keepdims=True)


def rows_four_kernel(image_rows, tokens, mods, back, grad_middle, image_grad, text_grad):
    for t, (low, high) in enumerate(((0, image_rows), (image_rows, tokens.shape[0]))):
        normed, inv = norm_rows(tokens[low:high, :].astype(F32))
        grad = grad_middle[low:high, :] + norm_back(
            back[low:high, :].astype(F32) * (1.0 + mods[t, 1:2, :]), normed, inv
        )
        target = (image_grad, text_grad)[t]
        target[0] = grad[: target.shape[1], :]


def rows_call(kernel, image_rows, name, outs, scalars, arrays):
    whole = pl.BlockSpec(memory_space=pltpu.VMEM)
    return pl.pallas_call(
        functools.partial(kernel, image_rows),
        in_specs=[pl.BlockSpec(memory_space=pltpu.SMEM)] * len(scalars) + [whole] * len(arrays),
        out_specs=[whole] * len(outs),
        out_shape=[jax.ShapeDtypeStruct(shape, dtype) for shape, dtype in outs],
        compiler_params=pltpu.CompilerParams(vmem_limit_bytes=16 << 20),
        cost_estimate=cost(2),
        name=name,
    )(*scalars, *arrays)


def unpack_kernel(layout, spots, y, zh, *refs):
    pieces, outs = refs[:5], refs[5:]
    for piece, (shift, halves) in zip(pieces, spots):
        for half, base in halves:
            spot = lax.rem(y[0] + shift, 4) * 2 + lax.rem(zh[0] + half, 2)
            for which, rows, low, high, first in layout:
                start = pl.multiple_of(spot * rows, 16)
                outs[which][pl.ds(start, rows), low:high] = piece[
                    0, base + first : base + first + rows, 0 : high - low
                ]


def unpack(layout, shapes, block, near, far):
    size = block.shape[1] // 2
    pair_at = [(0, 0), (1, size)]
    spots = [(0, pair_at), (3, pair_at), (1, pair_at), (2, [(0, 0)]), (2, [(1, 0)])]
    index = [lax.axis_index(n).astype(jnp.int32).reshape(1) for n in ("y", "zh")]
    whole = pl.BlockSpec(memory_space=pltpu.VMEM)
    return pl.pallas_call(
        functools.partial(unpack_kernel, layout, spots),
        in_specs=[pl.BlockSpec(memory_space=pltpu.SMEM)] * 2 + [whole] * 5,
        out_specs=[whole] * len(shapes),
        out_shape=[jax.ShapeDtypeStruct(v, BF) for v in shapes],
        compiler_params=pltpu.CompilerParams(vmem_limit_bytes=16 << 20),
        cost_estimate=cost(4),
        name="unpack",
    )(*index, block, *near, *far)


def sum_kernel(layout, size, count, y, *refs):
    owns, gots, outs = refs[:count], refs[count : 2 * count], refs[2 * count :]
    step = pl.program_id(0)

    def write(out, zone, base):
        for which, rows, low, high, first in layout:
            source = pl.ds(zone * rows, rows)
            value = owns[which][source, low:high].astype(F32) + gots[which][source, low:high].astype(F32)
            out[0, base + first : base + first + rows, 0 : high - low] = value.astype(BF)
            if high - low < out.shape[2]:
                out[0, base + first : base + first + rows, high - low :] = jnp.zeros(
                    (rows, out.shape[2] - high + low), BF
                )

    for j, targets in enumerate(((outs[0],), (outs[1],), (outs[2], outs[3]), (outs[4],))):

        @pl.when(step == j)
        def _(targets=targets):
            for zone in range(2):
                if len(targets) == 2:
                    write(targets[zone], zone, 0)
                else:
                    write(targets[0], zone, zone * size)


def sum_blocks(layout, size, wide, owns, gots, name):
    blocks = [
        pl.BlockSpec((v.shape[0] // 4, v.shape[1]), lambda j, y: (lax.rem(y[0] + j, 4), 0))
        for v in owns
    ]
    fixed = [pl.BlockSpec((1, n * size, wide), lambda j, y: (0, 0, 0)) for n in (2, 2, 1, 1, 2)]
    return pl.pallas_call(
        functools.partial(sum_kernel, layout, size, len(owns)),
        grid_spec=pltpu.PrefetchScalarGridSpec(
            num_scalar_prefetch=1, grid=(4,), in_specs=blocks + blocks, out_specs=fixed
        ),
        out_shape=[jax.ShapeDtypeStruct((1, n * size, wide), BF) for n in (2, 2, 1, 1, 2)],
        compiler_params=pltpu.CompilerParams(
            dimension_semantics=("arbitrary",), vmem_limit_bytes=20 << 20
        ),
        cost_estimate=cost(4),
        name=name,
    )(lax.axis_index("y").astype(jnp.int32).reshape(1), *owns, *gots)


def lines_kernel(y, own, behind, ahead, far_image, far_text, line_image, line_text):
    rows = line_image.shape[0] // 4
    for t, line in enumerate((line_image, line_text)):
        far = (far_image, far_text)[t]
        for piece, shift, low in ((own, 0, t * rows), (ahead, 1, t * rows), (behind, 3, t * rows), (far, 2, 0)):
            start = pl.multiple_of(lax.rem(y[0] + shift, 4) * rows, 16)
            line[pl.ds(start, rows), :] = piece[0, low : low + rows, :]


def lines_of(block, near, far):
    rows, width = 2 * block.shape[1], block.shape[2]
    whole = pl.BlockSpec(memory_space=pltpu.VMEM)
    return pl.pallas_call(
        lines_kernel,
        in_specs=[pl.BlockSpec(memory_space=pltpu.SMEM)] + [whole] * 5,
        out_specs=[whole] * 2,
        out_shape=[jax.ShapeDtypeStruct((rows, width), BF)] * 2,
        compiler_params=pltpu.CompilerParams(vmem_limit_bytes=12 << 20),
        cost_estimate=cost(2),
        name="lines",
    )(lax.axis_index("y").astype(jnp.int32).reshape(1), block, *near, *far)


def merge_kernel(zh, *refs):
    for line, other, out in zip(refs[:2], refs[2:4], refs[4:]):
        rows = out.shape[0] // 8
        for piece, shift in ((line, 0), (other, 1)):
            zone = lax.rem(zh[0] + shift, 2)
            for y in range(4):
                start = pl.multiple_of((2 * y + zone) * rows, 16)
                out[pl.ds(start, rows), :] = piece[y * rows : (y + 1) * rows, :]


def merge_lines(lines, others):
    rows, width = lines[0].shape
    whole = pl.BlockSpec(memory_space=pltpu.VMEM)
    return pl.pallas_call(
        merge_kernel,
        in_specs=[pl.BlockSpec(memory_space=pltpu.SMEM)] + [whole] * 4,
        out_specs=[whole] * 2,
        out_shape=[jax.ShapeDtypeStruct((2 * rows, width), BF)] * 2,
        compiler_params=pltpu.CompilerParams(vmem_limit_bytes=12 << 20),
        cost_estimate=cost(3),
        name="merge_lines",
    )(lax.axis_index("zh").astype(jnp.int32).reshape(1), *lines, *others)


def near_of(block):
    return turn(block, "y", 1), turn(block, "y", -1)


def far_of(near):
    half = near[0].shape[1] // 2
    return turn(cut(near[0], 1, 0, half), "y", 1), turn(cut(near[1], 1, half, 2 * half), "y", -1)


def mod_last_kernel(table, conds, weights, weight_grad, slot_grad, totals):
    total = jnp.zeros(slot_grad.shape, F32)
    for tile in range(weights.shape[1] // 128):
        lanes = slice(tile * 128, (tile + 1) * 128)
        values = table[:, tile, :]
        weight_grad[:, lanes] = mm_tn(conds[...], values)
        total += mm_nt(values, weights[:, lanes])
    slot_grad[...] = total
    for tile in range(0, table.shape[1], 8):
        totals[tile : tile + 8, :] = jnp.sum(table[:, tile : tile + 8, :].astype(F32), axis=0)


def mod_last(table, conds, weights):
    like = jax.ShapeDtypeStruct
    whole = pl.BlockSpec(memory_space=pltpu.VMEM)
    return pl.pallas_call(
        mod_last_kernel,
        in_specs=[whole] * 3,
        out_specs=[whole] * 3,
        out_shape=[
            like(weights.shape, F32),
            like(conds.shape, F32),
            like(table.shape[1:], F32),
        ],
        compiler_params=pltpu.CompilerParams(vmem_limit_bytes=16 << 20),
        cost_estimate=cost(4),
        name="mod_last",
    )(table, conds, weights)


def per_device(
    image_tokens,
    text_tokens,
    text_lengths,
    slot_sequence,
    conditioning,
    mod_weight,
    mod_bias,
    qkv_weight,
    qv_bias,
    out_weight,
    out_bias,
    up_weight,
    up_bias,
    down_weight,
    down_bias,
    image_cotan,
    text_cotan,
):
    seq_total, width = conditioning.shape
    image_rows, text_cap = image_tokens.shape[1], text_tokens.shape[1]
    rows = image_rows + text_cap + PAD
    own_rows = mod_weight.shape[0]
    span, ff = width // 4, up_weight.shape[2]
    ff_span = ff // 4
    half_span, half_ff = span // 2, ff_span // 2
    position = lax.axis_index("ctx")
    core = lax.axis_index("core")
    rep, y, zh = lax.axis_index("rep"), lax.axis_index("y"), lax.axis_index("zh")
    owner_index = lax.axis_index(OWNER)
    shards = 16

    def from_columns(columns):
        got = lax.all_to_all(columns, TP, split_axis=0, concat_axis=0, tiled=True)
        return got.transpose(1, 0, 2, 3).reshape(16 * own_rows, -1)

    def hot(values):
        values = values[:, 0, 0][:, None]
        return (values == jnp.arange(seq_total, dtype=jnp.int32)[None, :]).astype(F32)

    sequences = jnp.concatenate(
        direct_gather(jnp.broadcast_to(slot_sequence, (1, 8, 128)), "y")
    )
    cuts = [0, half_span, 2 * half_span, 3 * half_span]
    turn_at = cuts[2] - HEAD_DIM
    columns = (
        qkv_weight.reshape(own_rows, 2, 3, 4, 2, half_span)
        .transpose(4, 3, 1, 0, 2, 5)
        .reshape(8, 2, own_rows, 3 * half_span)
    )
    columns = jnp.concatenate(
        [
            columns[..., : cuts[1]],
            columns[..., turn_at : cuts[2]],
            columns[..., cuts[1] : turn_at],
            columns[..., cuts[2] :],
            jnp.zeros(columns.shape[:-1] + (HEAD_DIM,), BF),
        ],
        axis=-1,
    )
    qkv_wide = columns.shape[3]

    to_slice = []
    for source in range(4 * shards):
        y_at, zh_at, i = source // 16, source // 8 % 2, source % 8
        to_slice.append((source, (i * 2 + zh_at) * 4 + y_at))
    from_slice = [(d, s) for s, d in to_slice]
    out_got = lax.ppermute(out_weight.transpose(1, 0, 2), OWNER, to_slice)

    unit = down_weight.shape[0]
    wide_unit = -(-unit // 128) * 128
    lane_in, lane_out = (jnp.arange(8 * u, dtype=jnp.int32) for u in (unit, wide_unit))
    spacing = (
        (lane_in // unit * wide_unit + lane_in % unit)[:, None] == lane_out[None, :]
    ).astype(BF)
    for name in ("zh", "core"):
        sequences = jnp.concatenate([sequences, turn(sequences, name, 1)])
    up_wide = mm(
        up_weight.transpose(1, 0, 2).reshape(16 * own_rows, 8 * unit), spacing
    ).astype(BF)
    up_send = mm_nt(
        up_wide.reshape(2 * own_rows, 8, 8, wide_unit)
        .transpose(2, 0, 1, 3)
        .reshape(16 * own_rows, 8 * wide_unit),
        spacing,
    ).astype(BF)
    got = from_columns(
        jnp.concatenate([columns, up_send.reshape(8, 2, own_rows, half_ff)], axis=-1)
    )
    sequences, got, out_got, down_weight, own_tokens, own_cots = sync(
        sequences,
        got,
        out_got,
        down_weight,
        jnp.concatenate(
            [
                image_tokens[0],
                text_tokens[0],
                jnp.broadcast_to(text_lengths[0, 0].astype(BF), (PAD, width)),
            ]
        ),
        jnp.concatenate([image_cotan[0], text_cotan[0], jnp.zeros((PAD, width), BF)]),
    )
    gathered = gather_ctx(jnp.concatenate([own_tokens, own_cots])).reshape(4, 2, rows, width)
    qkv_got, up_mine = got[:, :qkv_wide], got[:, qkv_wide:].reshape(1, 16 * own_rows, half_ff)
    down_mine = down_weight.transpose(1, 0, 2).reshape(1, 2 * unit, width)
    down_near = near_of(down_mine)

    near_hot = hot(sequences)
    live = jnp.sum(near_hot[0])
    cond_float = conditioning.astype(F32)
    cond_cols = lax.dynamic_slice_in_dim(
        jax.nn.silu(cond_float).astype(BF), owner_index * own_rows, own_rows, 1
    )
    mod_matrix = mod_weight.reshape(own_rows, -1)
    mod_hot = near_hot.reshape(2, 2, 4, seq_total).transpose(0, 2, 1, 3).reshape(16, seq_total)
    sums_mod = mod_parts(mm(mod_hot.astype(BF), cond_cols).astype(BF), mod_matrix)
    sums_mod = add_two(sums_mod[:8], turn(sums_mod[8:], "core", 1))
    sums_mod = [sums_mod[:2]] + [turn(sums_mod[2 * k : 2 * k + 2], "y", k) for k in range(1, 4)]
    sums_mod = sum(v.astype(F32) for v in sums_mod).astype(BF)

    third = width // 3
    first_layout = [(0, 8 * own_rows, 0, qkv_wide, 0), (1, 8 * own_rows, 0, qkv_wide, 8 * own_rows)]
    first_layout += [
        (2, 2 * own_rows, f * third, (f + 1) * third, (16 + 2 * f) * own_rows) for f in range(3)
    ]
    out_lines = out_got.reshape(2 * own_rows, width)
    first_mine = jnp.concatenate(
        [qkv_got]
        + [
            jnp.pad(out_lines[:, f * third : (f + 1) * third], ((0, 0), (0, qkv_wide - third)))
            for f in range(3)
        ]
    )[None]
    first_other = cross(first_mine)
    down_far = far_of(down_near)
    sums_mod, first_other, down_near, down_far, up_mine = sync(
        sums_mod, first_other, down_near, down_far, up_mine
    )

    slot_mod = add_two(sums_mod[0], turn(sums_mod[1], "zh", 1))
    modulation = (
        sum(m.astype(F32) for m in direct_gather(slot_mod, "ctx")).reshape(2, 6, width)
        + mod_bias.astype(F32).reshape(2, 6, width)
    ) * live
    first_block = jnp.concatenate([first_mine, first_other], 1)
    first_near = near_of(first_block)
    down_lines = tuple(lines_of(down_mine, down_near, down_far))
    image_line = cross(down_lines[0])
    far_sequences = turn(sequences, "rep", 1)
    modulation, first_near, image_line, text_line, up_mine, far_sequences = sync(
        modulation, first_near, image_line, down_lines[1], up_mine, far_sequences
    )
    far_hot = hot(far_sequences)

    first_far = far_of(first_near)
    up_other = cross(up_mine)
    first_far, up_other, gathered = sync(first_far, up_other, gathered)

    qkv_image, qkv_text, out_raw = unpack(
        first_layout,
        [(width, qkv_wide), (width, qkv_wide), (16 * own_rows, width)],
        first_block,
        first_near,
        first_far,
    )
    qkv_own = (qkv_image, qkv_text)
    qkv_other = tuple(turn(w, "core", 1) for w in qkv_own)
    out_own = out_raw.reshape(8, 2, own_rows, width).transpose(1, 0, 2, 3)
    out_own = out_own.reshape(2, 8 * own_rows, width)
    out_rows = (out_own, turn(out_own, "core", 1))
    up_block = jnp.concatenate([up_mine, up_other], 1)
    qkv_own, up_block, text_line = sync(qkv_own, up_block, text_line)

    cots_all = gathered[:, 1]
    lengths = gathered[:, 0, rows - 1, 0].astype(jnp.int32)
    row_at = jnp.arange(rows, dtype=jnp.int32)
    is_image = row_at < image_rows
    valid_all = (
        is_image[None, :] | (row_at[None, :] - image_rows < lengths[:, None])
    ).astype(F32)

    def by_row(vectors, plus=0.0):
        return jnp.where(is_image[:, None], vectors[0] + plus, vectors[1] + plus)

    def bias_part(values, start, size):
        return [
            lax.dynamic_slice_in_dim(values, start + k * size, size, 1).astype(F32)
            for k in (core, 1 - core)
        ]

    q_bias = bias_part(qv_bias, position * span, half_span)
    v_bias = bias_part(qv_bias, width + position * span, half_span)
    qkv_bias = jnp.stack(
        [
            jnp.concatenate([q, jnp.zeros_like(q), v, jnp.zeros((2, HEAD_DIM), F32)], 1)
            for q, v in zip(q_bias, v_bias)
        ]
    )[:, :, None, :]
    up_part = jnp.stack(
        [
            lax.dynamic_index_in_dim(
                up_bias.reshape(2, 8, 8, unit), k * 4 + position, 2, keepdims=False
            ).reshape(2, half_ff)
            for k in (core, 1 - core)
        ]
    ).astype(F32)[:, :, None, :]
    up_near = near_of(up_block)
    other_text_line = cross(text_line)
    modulated_first, proj_own, mixed_own = attend(
        image_rows, lengths, gathered, modulation, qkv_own, qkv_bias[0]
    )
    modulated_first, qkv_other = sync(modulated_first, qkv_other)
    proj_other, mixed_other = attend_other(
        image_rows, lengths, modulated_first, qkv_other, qkv_bias[1]
    )
    projs, mixed = (proj_own, proj_other), (mixed_own, mixed_other)
    qkv_cols = (qkv_own, qkv_other)
    attn_parts = attend_out(image_rows, mixed, out_rows)
    attn_parts, up_near, other_text_line = sync(attn_parts, up_near, other_text_line)

    attn_got = scatter_ctx(attn_parts)
    up_far = far_of(up_near)
    down_own = merge_lines((down_lines[0], text_line), (image_line, other_text_line))
    down_other = [turn(w, "core", 1) for w in down_own]
    attn_got, up_far, down_own, down_other = sync(attn_got, up_far, down_own, down_other)

    scalars = (text_lengths.reshape(1), live.reshape(1))
    flat, halved = ((rows, width), BF), ((rows, width), F32)
    out_line, down_line = out_bias.astype(F32), down_bias.astype(F32)
    base = (attn_got, own_tokens, modulation, out_line)
    (modulated_two,) = rows_call(rows_one_kernel, image_rows, "rows_one", [flat], (), base)
    modulated_two, up_far = sync(modulated_two, up_far)

    up_layout = [(t, 8 * own_rows, 0, half_ff, t * 8 * own_rows) for t in range(2)]
    down_layout = [(t, unit, 0, width, t * unit) for t in range(2)]
    up_own = unpack(up_layout, [(width, half_ff)] * 2, up_block, up_near, up_far)
    up_cols = [(w, turn(w, "core", 1)) for w in up_own]
    down_rows = list(zip(down_own, down_other))
    branch_grads = (
        cots_all.astype(F32) * (valid_all * live)[:, :, None] * by_row(modulation[:, 5])
    ).astype(BF)
    seconds = gather_ctx(modulated_two)
    seconds, up_cols, branch_grads = sync(seconds, up_cols, branch_grads)

    second_parts, down_parts, both_grads, up_sums = mlp(
        image_rows, seconds, branch_grads, up_cols, down_rows, up_part
    )
    second_parts, both_grads = sync(second_parts, both_grads)

    up_sum = sum_blocks(
        up_layout,
        16 * own_rows,
        half_ff,
        [both_grads[0], both_grads[4]],
        [turn(both_grads[k], "core", 1) for k in (1, 5)],
        "sum_up",
    )
    down_sum = sum_blocks(
        down_layout,
        2 * unit,
        width,
        [both_grads[2], both_grads[6]],
        [turn(both_grads[k], "core", 1) for k in (3, 7)],
        "sum_down",
    )
    second_got = scatter_ctx(second_parts)
    second_got, up_sum, down_sum = sync(second_got, up_sum, down_sum)

    grad_attn, grad_middle, sums_two = rows_call(
        rows_two_kernel,
        image_rows,
        "rows_two",
        [flat, halved, ((2, 4, width), F32)],
        scalars,
        (*base, own_cots, second_got),
    )
    grad_attn, up_sum, down_sum = sync(grad_attn, up_sum, down_sum)

    attn_grads = gather_ctx(grad_attn)
    up_got = scatter_near(up_sum[2], up_sum[3])
    down_got = scatter_near(down_sum[2], down_sum[3])
    up_sent = scatter_add(up_sum[1], up_sum[4], up_got)
    attn_grads, up_sent, down_got, down_parts = sync(attn_grads, up_sent, down_got, down_parts)

    branch_got = scatter_ctx(down_parts)
    up_got = scatter_far(up_sent)
    proj_grads = attend_back(image_rows, lengths, attn_grads, projs, out_rows)
    proj_grads, down_got = sync(proj_grads, down_got)

    down_sent = scatter_add(down_sum[1], down_sum[4], down_got)
    down_sent, proj_grads = sync(down_sent, proj_grads)
    down_got = scatter_far(down_sent)
    *d_qkv, d_out_own, d_out_other = attend_weights(
        image_rows, modulated_first, proj_grads, mixed, attn_grads
    )
    d_first = [d_qkv[0], d_qkv[1], d_out_own]
    d_first, d_first_other, proj_grads, up_got = sync(
        d_first, [d_qkv[2], d_qkv[3], d_out_other], proj_grads, up_got
    )
    first_gots = [turn(v, "core", 1) for v in d_first_other]
    first_parts, first_sums, proj_sums = attend_rows(
        image_rows, gathered, proj_grads, qkv_cols
    )
    up_keep, up_give = zones(add_three(up_sum[0], up_got))
    up_got = cross(up_give)
    first_parts, first_gots = sync(first_parts, first_gots)

    first_sum = sum_blocks(
        first_layout, first_mine.shape[1], qkv_wide, d_first, first_gots, "sum_first"
    )
    first_sum, first_parts, branch_got = sync(first_sum, first_parts, branch_got)
    first_got = scatter_ctx(first_parts)
    first_near = scatter_near(first_sum[2], first_sum[3])
    image_out, text_out, sums_three = rows_call(
        rows_three_kernel,
        image_rows,
        "rows_three",
        [(image_tokens.shape, BF), (text_tokens.shape, BF), ((2, 2, width), F32)],
        scalars,
        (*base, own_cots, branch_got, down_line),
    )

    vectors = jnp.concatenate(
        [
            jnp.concatenate([first_sums, sums_two[:, :3], sums_three[:, :1]], axis=1).reshape(-1),
            sums_two[:, 3].reshape(-1),
            sums_three[:, 1].reshape(-1),
        ]
    )

    def in_order(mine, other):
        return jnp.where(
            core == 0, jnp.concatenate([mine, other], -1), jnp.concatenate([other, mine], -1)
        )

    q_sums, v_sums = (
        in_order(*(proj_sums[h, :, 0, a * half_span : (a + 1) * half_span] for h in range(2)))
        for a in (0, 2)
    )
    heads = jnp.stack([q_sums, v_sums], 1).reshape(-1)
    message = jnp.concatenate([vectors, heads]).reshape(-1, 128)
    messages = direct_gather(message, "ctx")
    messages, first_near, down_got, up_got = sync(messages, first_near, down_got, up_got)

    first_sent = scatter_add(first_sum[1], first_sum[4], first_near)
    vectors = sum(m[: vectors.shape[0] // 128] for m in messages).reshape(-1)
    heads = jnp.stack([m[vectors.shape[0] // 128 :] for m in messages])
    heads = jnp.roll(heads.reshape(4, 2, 2, span), position, axis=0).transpose(1, 2, 0, 3)
    own_vector = jnp.concatenate([v.reshape(-1) for v in (vectors, heads, up_sums)])
    own_vector = (own_vector * live).astype(BF).reshape(1, -1, 128)
    everything = jnp.concatenate(direct_gather(own_vector, "y"))
    first_sent, everything, sequences, up_got, down_got = sync(
        first_sent, everything, sequences, up_got, down_got
    )
    first_back = scatter_far(first_sent)
    down_keep, down_give = zones(add_three(down_sum[0], down_got))
    down_got = cross(down_give)
    up_part_sum = add_two(up_keep, up_got)
    up_more = turn(up_part_sum, "rep", 1)
    for name in ("rep", "zh"):
        everything = jnp.concatenate([everything, turn(everything, name, 1)])
    image_grad, text_grad = rows_call(
        rows_four_kernel,
        image_rows,
        "rows_four",
        [(image_tokens.shape, F32), (text_tokens.shape, F32)],
        (),
        (own_tokens, modulation, first_got, grad_middle),
    )
    first_back, everything, up_more, down_got, image_grad = sync(
        first_back, everything, up_more, down_got, image_grad
    )

    first_keep, first_give = zones(add_three(first_sum[0], first_back))
    first_give, up_more, down_got, everything = sync(first_give, up_more, down_got, everything)
    first_back = cross(first_give)
    down_part_sum = add_two(down_keep, down_got)
    down_more = turn(down_part_sum, "rep", 1)
    first_back, everything, up_more = sync(first_back, everything, up_more)

    first_part_sum = add_two(first_keep, first_back)
    first_part_sum, up_more, everything = sync(first_part_sum, up_more, everything)
    qkv_lines = 16 * own_rows
    first_more = turn(first_part_sum[:qkv_lines], "rep", 1)
    everything = jnp.concatenate([everything, turn(everything, "core", 1)])
    out_total = jnp.concatenate(
        [
            first_part_sum[(16 + 2 * f) * own_rows : (18 + 2 * f) * own_rows, :third]
            for f in range(3)
        ],
        axis=1,
    ).reshape(2, own_rows, width)
    out_total = lax.ppermute(out_total, OWNER, from_slice)
    up_total = add_two(up_part_sum, up_more).reshape(2, 8, own_rows, half_ff)
    up_total = lax.all_to_all(
        up_total.transpose(1, 0, 2, 3), TP, split_axis=0, concat_axis=0, tiled=True
    )
    slot_hot = jnp.stack(
        [near_hot.reshape(4, 4, seq_total), far_hot.reshape(4, 4, seq_total)], axis=1
    ).reshape(2 * shards, seq_total)
    slot_cond = mm(slot_hot.astype(BF), cond_cols).astype(BF)
    first_more, everything, up_total, out_total = sync(first_more, everything, up_total, out_total)

    qkv_total = add_two(first_part_sum[:qkv_lines], first_more)
    qkv_total = qkv_total.reshape(2, 8, own_rows, qkv_wide)
    qkv_total = lax.all_to_all(
        qkv_total.transpose(1, 0, 2, 3), TP, split_axis=0, concat_axis=0, tiled=True
    )
    mod_weight_grad, slot_grads, totals = mod_last(everything, slot_cond, mod_matrix)
    out_grad = out_total.astype(F32) + turn(out_total, "rep", 1).astype(F32)
    out_grad = out_grad.transpose(1, 0, 2)
    up_wide = mm(up_total.reshape(16 * own_rows, 8 * unit), spacing).astype(BF)
    up_grad = (
        mm_nt(
            up_wide.reshape(8, 2 * own_rows, 8, wide_unit)
            .transpose(1, 2, 0, 3)
            .reshape(16 * own_rows, 8 * wide_unit),
            spacing,
        )
        .reshape(2, own_rows, ff)
        .transpose(1, 0, 2)
    )
    down_grad = (
        (down_part_sum.astype(F32) + down_more.astype(F32))
        .reshape(2, unit, width)
        .transpose(1, 0, 2)
    )
    qkv_total = qkv_total.astype(F32).reshape(2, 4, 2, own_rows, -1)
    qkv_grad = (
        jnp.stack(
            [
                qkv_total[..., : cuts[1]],
                jnp.concatenate(
                    [
                        qkv_total[..., cuts[1] + HEAD_DIM : cuts[2]],
                        qkv_total[..., cuts[1] : cuts[1] + HEAD_DIM],
                    ],
                    -1,
                ),
                qkv_total[..., cuts[2] : cuts[3]],
            ],
            axis=4,
        )
        .transpose(3, 2, 4, 1, 0, 5)
        .reshape(qkv_weight.shape)
    )
    mod_weight_grad = mod_weight_grad.reshape(mod_weight.shape)
    up_lines = 2 * half_ff // 128
    here_up = jnp.sum(everything[:shards, -2 * up_lines : -up_lines].astype(F32), 0) + jnp.sum(
        everything[shards:, -up_lines:].astype(F32), 0
    )
    totals = totals.reshape(-1)
    mod_size, wide = 12 * width, 2 * width

    def owner_slice(values):
        part = values.shape[1] // (4 * shards)
        return lax.dynamic_slice_in_dim(values, owner_index * part, part, 1)

    mod_bias_grad = owner_slice(totals[:mod_size].reshape(2, -1))
    out_bias_grad = owner_slice(totals[mod_size : mod_size + wide].reshape(2, -1))
    down_bias_grad = owner_slice(totals[mod_size + wide : mod_size + 2 * wide].reshape(2, -1))
    qv_bias_grad = owner_slice(totals[mod_size + 2 * wide : mod_size + 4 * wide].reshape(2, -1))
    up_bias_grad = lax.dynamic_index_in_dim(
        here_up.reshape(2, 8, unit), y * 2 + zh, 1, keepdims=False
    )
    grad_cond_cols = lax.dot_general(
        slot_hot, slot_grads, (((0,), (0,)), ((), ())), precision=lax.Precision.HIGHEST
    )
    cond_part = lax.dynamic_slice_in_dim(cond_float, owner_index * own_rows, own_rows, 1)
    cond_grad = jax.vjp(jax.nn.silu, cond_part)[1](grad_cond_cols)[0]
    return (
        image_out,
        text_out,
        image_grad,
        text_grad,
        cond_grad,
        mod_weight_grad,
        mod_bias_grad,
        qkv_grad,
        qv_bias_grad,
        out_grad,
        out_bias_grad,
        up_grad,
        up_bias_grad,
        down_grad,
        down_bias_grad,
    )


def solution(mesh):
    fine = Mesh(mesh.devices.reshape(2, 4, 2, 2, 4), EVERY)
    rows = P(SLOT, "ctx", None)
    owned = P(OWNER, None, None)
    columns = P(None, OWNER)
    return jax.shard_map(
        per_device,
        mesh=fine,
        in_specs=(
            rows,
            rows,
            P(SLOT, "ctx"),
            P(SLOT),
            P(),
            owned,
            P(),
            owned,
            P(),
            owned,
            P(),
            owned,
            P(),
            owned,
            P(),
            rows,
            rows,
        ),
        out_specs=(
            rows,
            rows,
            rows,
            rows,
            columns,
            owned,
            columns,
            owned,
            columns,
            owned,
            columns,
            owned,
            columns,
            owned,
            columns,
        ),
        check_vma=False,
    )
```
